32 devices in a mesh: leaf: 8 (over z, x), rows: 2 (over y), rhs: 2 (over core).
Axes of the slice: x: 2, y: 2, z: 4, core: 2. Of those that a mesh axis runs over, the one named last changes fastest.
Arguments:
- right_side: float32 [16, 128, 2048], P('leaf', 'rhs', 'rows'), may hold values from -6 to 6
- inverse_diag: bfloat16 [16, 2048, 2048], P('leaf', None, ('rows', 'rhs')), may hold values from -0.1 to 1.5, as said below
- lower_blocks: bfloat16 [16, 16, 128, 2048], P('leaf', None, None, 'rows'), may hold values from -0.0625 to 0.0625
- block_rows: int32 [16, 16], P('leaf'), may hold values from 0 to 47, as said below
Outputs:
- solved: float32 [16, 128, 2048], P('leaf', 'rhs', 'rows')
The draws below stay inside these ranges and needn't reach their ends.
Inputs may be any that keep to these rules, and one draw needn't show every extreme that they name: `inverse_diag`: in every row of an inverse block, the diagonal entry is positive and larger than every other entry of that row. `block_rows`: row i lists 16 distinct block numbers below 2048 / 128 times the depth of slot i; the first is 0, the first block of the root's rows, and the second is the last block of its parent's rows; the rows of the root and of slot 15 are not read.
All inputs are finite; a program needn't handle non-finite values.
Results may differ from the reference program's by a relative error of at most 0.004.
Values may be sent and summed in bfloat16 or wider, within the bound.
No kernel may reach another device: no remote copies, remote signals or barrier semaphores. Data moves between devices by JAX's collectives and lax.ppermute only.
A program may use at most 64 MiB of HBM per device.

```python
import math
import jax
import jax.numpy as jnp
from jax import lax

S = 2048
BLK = 128
R = 16
LEVELS = 4
NODES = 16
NRHS = 128
N_LEAF = 8


def draw_inverse_diag(key, part):
    slot_keys = jax.random.split(key, 2 * N_LEAF)

    def single(slot_key):
        diag_key, noise_key = jax.random.split(slot_key)
        diagonal = jax.random.uniform(diag_key, (S,), jnp.float32, 0.6, 1.4)
        spread_part = jax.random.normal(noise_key, (S, S), jnp.float32) * 0.4 / math.sqrt(S)
        matrix = spread_part + jnp.diag(diagonal)
        return jnp.clip(matrix, -0.09375, 1.5).astype(jnp.bfloat16)
    return lax.map(single, slot_keys)


def draw_block_rows(key, part):
    blocks_each = S // BLK
    candidates = max(LEVELS - 1, 1) * blocks_each
    slot_ids = jnp.arange(2 * N_LEAF, dtype=jnp.int32)
    height = jnp.zeros((2 * N_LEAF,), jnp.int32)
    for power_index in range(1, LEVELS + 1):
        height = height + ((slot_ids + 1) % 2 ** power_index == 0).astype(jnp.int32)
    depth_all = LEVELS - 1 - height
    bound_now = jnp.maximum(depth_all, 1) * blocks_each
    columns = jnp.arange(candidates, dtype=jnp.int32)
    scores = jax.random.randint(key, (2 * N_LEAF, candidates), 0, 65536, dtype=jnp.int32) * candidates + columns[None, :]
    scores = jnp.where(columns[None, :] >= bound_now[:, None], scores + 2 ** 30, scores)
    active_rows = depth_all[:, None] >= 1
    forced_parent = active_rows & (columns[None, :] == depth_all[:, None] * blocks_each - 1)
    scores = jnp.where(forced_parent, -1, scores)
    forced_root = active_rows & (columns[None, :] == 0)
    scores = jnp.where(forced_root, -2, scores)
    ordering = jnp.argsort(scores, axis=1, stable=True)
    return ordering[:, :R].astype(jnp.int32)


def block_levels(own_key, shape, cuts, least, largest):
    def one(axis_at, parts):
        steps = jax.random.uniform(jax.random.fold_in(jax.random.fold_in(own_key, 6), axis_at), (parts,), jnp.float32, least / len(cuts), largest / len(cuts))
        return jnp.repeat(jnp.exp(steps), shape[axis_at] // parts).reshape((-1,) + (1,) * (len(shape) - axis_at - 1))

    level = one(*cuts[0])
    for cut in cuts[1:]:
        level = level * one(*cut)
    return level


def bell_draw(stream_key, shape, deviation, most, cuts=(), held_as=jnp.bfloat16):
    array = deviation * jax.random.normal(stream_key, shape, jnp.float32)
    if cuts:
        array = array * block_levels(stream_key, shape, cuts, -0.22, 0.18)
    return jnp.clip(array, -most, most).astype(held_as)


def setup_inputs(seed: int = 0) -> dict:
    streams_of = jax.random.split(jax.random.key(seed), 5)
    return {
        "right_side": bell_draw(streams_of[0], (NODES, NRHS, S), 1.0, 6.0, ((0, 8), (1, 2), (2, 2)), jnp.float32),
        "inverse_diag": draw_inverse_diag(jax.random.fold_in(streams_of[4], 71), 0),
        "lower_blocks": bell_draw(streams_of[2], (NODES, R, BLK, S), (4 * R * BLK) ** -0.5, 0.0625, ((0, 8), (3, 2))),
        "block_rows": draw_block_rows(jax.random.fold_in(streams_of[4], 71), 0),
    }


def reference(right_side, inverse_diag, lower_blocks, block_rows):
    top_depth = LEVELS - 1
    blocks_each = S // BLK
    solved = [None] * (2 * N_LEAF)
    rounded = [None] * (2 * N_LEAF)
    for depth_now in range(LEVELS):
        height = top_depth - depth_now
        for position in range(2 ** depth_now):
            node_id = (2 * position + 1) * 2 ** height - 1
            if depth_now > 0:
                pieces = []
                for upper_depth in range(depth_now):
                    above_pos = position >> (depth_now - upper_depth)
                    pieces.append(rounded[(2 * above_pos + 1) * 2 ** (top_depth - upper_depth) - 1])
                joined = jnp.concatenate(pieces, axis=1)
                tile_view = joined.reshape(NRHS, depth_now * blocks_each, BLK)
                picked = jnp.take(tile_view, block_rows[node_id], axis=1, mode="clip").reshape(NRHS, R * BLK)
                offset = jnp.dot(picked, lower_blocks[node_id].reshape(R * BLK, S), preferred_element_type=jnp.float32)
                reduced = (right_side[node_id] - offset).astype(jnp.bfloat16)
            else:
                reduced = right_side[node_id].astype(jnp.bfloat16)
            result = jnp.dot(reduced, inverse_diag[node_id], preferred_element_type=jnp.float32)
            solved[node_id] = result
            rounded[node_id] = result.astype(jnp.bfloat16)
    solved[2 * N_LEAF - 1] = jnp.zeros((NRHS, S), jnp.float32)
    return jnp.stack(solved)
```

```python
import functools
import jax
import jax.numpy as jnp
from jax import lax
from jax.experimental import pallas as pl
from jax.experimental.pallas import tpu as pltpu
from jax.sharding import PartitionSpec as P

F32 = jnp.float32
BF16 = jnp.bfloat16
VMEM = pltpu.VMEM


def cast_kernel(right_ref, out_ref):
    out_ref[...] = right_ref[1].astype(BF16)


def offset_kernel(level, slot, rows, fulls, position_ref, block_rows_ref, right_ref, lower_ref, *refs):
    full_refs = refs[:fulls]
    piece_refs = refs[fulls:fulls + rows]
    reduced_ref, newest_ref, picked = refs[fulls + rows:]
    width = piece_refs[0].shape[1]
    block_width = lower_ref.shape[2]
    blocks = lower_ref.shape[1]
    own = position_ref[0]
    for shift, piece_ref in enumerate(piece_refs):
        source = lax.rem(own - shift + rows, rows)
        newest_ref[:, pl.ds(pl.multiple_of(source * width, width), width)] = piece_ref[...]
    blocks_each = rows * width // block_width
    known = [*full_refs, newest_ref]
    for index in range(blocks):
        number = jnp.clip(block_rows_ref[slot, index], 0, level * blocks_each - 1)
        ancestor = number // blocks_each
        column = pl.multiple_of((number - ancestor * blocks_each) * block_width, block_width)
        target = pl.ds(index * block_width, block_width)
        for which, known_ref in enumerate(known):
            @pl.when(ancestor == which)
            def _():
                picked[:, target] = known_ref[:, pl.ds(column, block_width)]
    weights = lower_ref[slot].reshape(blocks * block_width, width)
    offset = jnp.dot(picked[...], weights, preferred_element_type=F32)
    reduced_ref[...] = (right_ref[slot] - offset).astype(BF16)


def apply_inverse(slot, rows, cores, position_ref, piece_refs, inverse_refs, store):
    width = piece_refs[0].shape[1]
    quarter = inverse_refs[0].shape[-1]
    own = position_ref[0]
    own_core = position_ref[1]
    for turn, inverse_ref in enumerate(inverse_refs):
        total = None
        for shift, piece_ref in enumerate(piece_refs):
            source = lax.rem(own - shift + rows, rows)
            depth = pl.ds(pl.multiple_of(source * width, width), width)
            part = inverse_ref[slot, depth, :]
            term = jnp.dot(piece_ref[...], part, preferred_element_type=F32)
            total = term if total is None else total + term
        core = lax.rem(own_core - turn + cores, cores)
        store(pl.ds(pl.multiple_of(core * quarter, quarter), quarter), total)


def solve_kernel(rows, cores, depth_now, position_ref, *refs):
    piece_refs = refs[:rows]
    inverse_refs = refs[rows:rows + cores]
    rest = refs[rows + cores:]
    if depth_now == 0:
        before_ref, (rounded_ref, solved_ref) = None, rest
    else:
        before_ref, rounded_ref, solved_ref = rest
    active = position_ref[2] == depth_now

    def store(columns, total):
        rounded_ref[:, columns] = total.astype(BF16)
        before = jnp.zeros_like(total) if before_ref is None else before_ref[:, columns]
        solved_ref[:, columns] = jnp.where(active, total, before)

    apply_inverse(1, rows, cores, position_ref, piece_refs, inverse_refs, store)


def last_kernel(rows, cores, position_ref, *refs):
    piece_refs = refs[:rows]
    inverse_refs = refs[rows:rows + cores]
    before_ref, out_ref = refs[rows + cores:]
    out_ref[1] = before_ref[...]

    def store(columns, total):
        out_ref[0, :, columns] = total

    apply_inverse(0, rows, cores, position_ref, piece_refs, inverse_refs, store)


SCALARS = pl.BlockSpec(memory_space=pltpu.SMEM)
WHOLE = pl.BlockSpec(memory_space=pltpu.VMEM)


def call(kernel, scalars, arrays, outs, scratch=(), flops=0):
    several = len(outs) > 1
    size = sum(a.size * a.dtype.itemsize for a in arrays)
    return pl.pallas_call(
        kernel,
        in_specs=[SCALARS] * len(scalars) + [WHOLE] * len(arrays),
        out_specs=[WHOLE] * len(outs) if several else WHOLE,
        out_shape=list(outs) if several else outs[0],
        scratch_shapes=list(scratch),
        cost_estimate=pl.CostEstimate(flops=flops, bytes_accessed=size, transcendentals=0),
        compiler_params=pltpu.CompilerParams(vmem_limit_bytes=24 * 2**20),
    )(*scalars, *arrays)


def local(right_side, inverse_diag, lower_blocks, block_rows):
    leafs, rows, cores = (lax.axis_size(name) for name in ("leaf", "rows", "rhs"))
    top = leafs.bit_length() - 1
    leaf = lax.axis_index("leaf")
    depth_upper = top - 1 - sum(((leaf + 1) % 2**power == 0).astype(jnp.int32) for power in range(1, top + 1))
    position = jnp.stack([lax.axis_index("rows"), lax.axis_index("rhs"), depth_upper]).astype(jnp.int32)
    count, width = right_side.shape[1:]
    quarter = inverse_diag.shape[2]
    full_width = rows * width
    places = ("leaf", "rows")

    def send(value, hops, shift):
        pairs = [(a * rows + r, b * rows + (r + shift) % rows) for a, b in hops for r in range(rows)]
        return lax.ppermute(value, places, pairs)

    def spread(value, hops):
        return [send(value, hops, shift) for shift in range(rows)]

    def rows_of(value, holders):
        return [value] + [send(value, [(h, h) for h in holders], shift) for shift in range(1, rows)]

    inverses = [inverse_diag]
    for turn in range(1, cores):
        inverses.append(lax.ppermute(inverse_diag, "rhs", [(c, (c + turn) % cores) for c in range(cores)]))

    half = jax.ShapeDtypeStruct((count, width), BF16)
    half_f32 = jax.ShapeDtypeStruct((count, width), F32)
    full = jax.ShapeDtypeStruct((count, full_width), BF16)
    work = 2 * count * full_width * width

    def holders(depth):
        return [(2 * p + 1) * 2 ** (top - depth - 1) - 1 for p in range(2**depth)]

    reduced = call(cast_kernel, [], [right_side], [half])
    known = []
    solved = None
    for depth in range(top + 1):
        last = depth == top
        slot = 0 if last else 1
        if depth > 0:
            kernel = functools.partial(offset_kernel, depth, slot, rows, len(known))
            reduced, newest = call(
                kernel, [position, block_rows], [right_side, lower_blocks, *known, *pieces], [half, full],
                [pltpu.VMEM((count, full_width), BF16)], work)
            known.append(newest)
        if last:
            everyone = range(leafs)
            gathered = rows_of(reduced, everyone)
            kernel = functools.partial(last_kernel, rows, cores)
            return call(kernel, [position], [*gathered, *inverses, solved],
                        [jax.ShapeDtypeStruct(right_side.shape, F32)], (), work)
        here = holders(depth)
        gathered = rows_of(reduced, here)
        kernel = functools.partial(solve_kernel, rows, cores, depth)
        arrays = [*gathered, *inverses] + ([] if depth == 0 else [solved])
        rounded, solved = call(kernel, [position], arrays, [half, half_f32], (), work)
        if depth + 1 < top:
            reach = 2 ** (top - depth - 2)
            left = [(h, h - reach) for h in here]
            right = [(h, h + reach) for h in here]
            moved = []
            lefts, rights = spread(rounded, left), spread(rounded, right)
            is_left = ((leaf + 1) // reach) % 4 == 1
            pieces = [jnp.where(is_left, a, b) for a, b in zip(lefts, rights)]
            known = [jnp.where(is_left, send(k, left, 0), send(k, right, 0)) for k in known]
        else:
            over = [(h, h + 1) for h in here]
            is_here = leaf % 2 == 0
            own = rows_of(rounded, here)
            others = spread(rounded, over)
            pieces = [jnp.where(is_here, a, b) for a, b in zip(own, others)]
            known = [jnp.where(is_here, k, send(k, over, 0)) for k in known]


def solution(mesh):
    return jax.shard_map(
        local,
        mesh=mesh,
        in_specs=(
            P("leaf", "rhs", "rows"),
            P("leaf", None, ("rows", "rhs")),
            P("leaf", None, None, "rows"),
            P("leaf", None),
        ),
        out_specs=P("leaf", "rhs", "rows"),
        check_vma=False,
    )
```

```python
import functools
import jax
import jax.numpy as jnp
from jax import lax
from jax.experimental import pallas as pl
from jax.experimental.pallas import tpu as pltpu
from jax.sharding import PartitionSpec as P

F32 = jnp.float32
BF16 = jnp.bfloat16
VMEM = pltpu.VMEM


def first_kernel(right_ref, inverse_ref, cast_ref, inverse_out, staged, semaphores):
    weights = pltpu.make_async_copy(inverse_ref.at[1], inverse_out, semaphores.at[0])
    values = pltpu.make_async_copy(right_ref.at[1], staged, semaphores.at[1])
    values.start()
    weights.start()
    values.wait()
    cast_ref[...] = staged[...].astype(BF16)
    weights.wait()


def load_kernel(after_ref, right_ref, inverse_ref, lower_ref, right_out, inverse_out, upper_out, lower_out, semaphores):
    copies = [
        pltpu.make_async_copy(lower_ref.at[1], upper_out, semaphores.at[0]),
        pltpu.make_async_copy(inverse_ref.at[0], inverse_out, semaphores.at[1]),
        pltpu.make_async_copy(right_ref, right_out, semaphores.at[2]),
        pltpu.make_async_copy(lower_ref.at[0], lower_out, semaphores.at[3]),
    ]
    for copy in copies:
        copy.start()
    for copy in copies:
        copy.wait()


def place_pieces(position_ref, piece_refs, target_ref, base):
    rows = len(piece_refs)
    width = piece_refs[0].shape[1]
    for shift, piece_ref in enumerate(piece_refs):
        source = lax.rem(position_ref[0] - shift + rows, rows)
        target_ref[:, pl.ds(pl.multiple_of(base + source * width, width), width)] = piece_ref[...]


def whole_kernel(rows, position_ref, after_ref, *refs):
    place_pieces(position_ref, refs[:rows], refs[rows], 0)


def offset_kernel(level, slot, rows, position_ref, block_rows_ref, right_ref, lower_ref, *refs):
    full_refs = refs[:level - 1]
    piece_refs = refs[level - 1:level - 1 + rows]
    reduced_ref, joined, picked = refs[level - 1 + rows:]
    width = piece_refs[0].shape[1]
    blocks, block_width = lower_ref.shape[:2]
    for index, full_ref in enumerate(full_refs):
        joined[:, index * rows * width:(index + 1) * rows * width] = full_ref[...]
    place_pieces(position_ref, piece_refs, joined, (level - 1) * rows * width)
    highest = joined.shape[1] // block_width - 1
    for index in range(blocks):
        number = jnp.clip(block_rows_ref[slot, index], 0, highest)
        column = pl.multiple_of(number * block_width, block_width)
        picked[:, index * block_width:(index + 1) * block_width] = joined[:, pl.ds(column, block_width)]
    weights = lower_ref[...].reshape(blocks * block_width, width)
    offset = jnp.dot(picked[...], weights, preferred_element_type=F32)
    reduced_ref[...] = (right_ref[slot] - offset).astype(BF16)


def apply_inverse(rows, cores, position_ref, piece_refs, inverse_refs, store):
    width = piece_refs[0].shape[1]
    quarter = inverse_refs[0].shape[-1]
    for turn, inverse_ref in enumerate(inverse_refs):
        total = None
        for shift, piece_ref in enumerate(piece_refs):
            source = lax.rem(position_ref[0] - shift + rows, rows)
            part = inverse_ref[pl.ds(pl.multiple_of(source * width, width), width), :]
            term = jnp.dot(piece_ref[...], part, preferred_element_type=F32)
            total = term if total is None else total + term
        core = lax.rem(position_ref[1] - turn + cores, cores)
        store(pl.ds(pl.multiple_of(core * quarter, quarter), quarter), total)


def solve_kernel(rows, cores, depth_now, position_ref, *refs):
    piece_refs = refs[:rows]
    inverse_refs = refs[rows:rows + cores]
    rest = refs[rows + cores:]
    if depth_now == 0:
        before_ref, (rounded_ref, solved_ref) = None, rest
    else:
        before_ref, rounded_ref, solved_ref = rest
    active = position_ref[2] == depth_now

    def store(columns, total):
        rounded_ref[:, columns] = total.astype(BF16)
        before = jnp.zeros_like(total) if before_ref is None else before_ref[:, columns]
        solved_ref[:, columns] = jnp.where(active, total, before)

    apply_inverse(rows, cores, position_ref, piece_refs, inverse_refs, store)


def last_kernel(rows, cores, position_ref, *refs):
    piece_refs = refs[:rows]
    inverse_refs = refs[rows:rows + cores]
    before_ref, out_ref = refs[rows + cores:]
    out_ref[1] = before_ref[...]

    def store(columns, total):
        out_ref[0, :, columns] = total

    apply_inverse(rows, cores, position_ref, piece_refs, inverse_refs, store)


SCALARS = pl.BlockSpec(memory_space=pltpu.SMEM)
WHOLE = pl.BlockSpec(memory_space=pltpu.VMEM)
FAR = pl.BlockSpec(memory_space=pltpu.HBM)


def call(kernel, scalars, arrays, outs, scratch=(), flops=0, far=0):
    several = len(outs) > 1
    size = sum(a.size * a.dtype.itemsize for a in arrays)
    here = len(arrays) - far
    arrays = [pltpu.with_memory_space_constraint(a, pltpu.VMEM) for a in arrays[:here]] + list(arrays[here:])
    return pl.pallas_call(
        kernel,
        in_specs=[SCALARS] * len(scalars) + [WHOLE] * here + [FAR] * far,
        out_specs=[WHOLE] * len(outs) if several else WHOLE,
        out_shape=list(outs) if several else outs[0],
        scratch_shapes=list(scratch),
        cost_estimate=pl.CostEstimate(flops=flops, bytes_accessed=size, transcendentals=0),
        compiler_params=pltpu.CompilerParams(vmem_limit_bytes=8 * 2**20),
    )(*scalars, *arrays)


def local(right_side, inverse_diag, lower_blocks, block_rows):
    leafs, rows, cores = (lax.axis_size(name) for name in ("leaf", "rows", "rhs"))
    top = leafs.bit_length() - 1
    leaf = lax.axis_index("leaf")
    depth_upper = top - 1 - sum(((leaf + 1) % 2**power == 0).astype(jnp.int32) for power in range(1, top + 1))
    position = jnp.stack([lax.axis_index("rows"), lax.axis_index("rhs"), depth_upper]).astype(jnp.int32)
    count, width = right_side.shape[1:]
    full_width = rows * width
    places = ("leaf", "rows")

    def send(value, hops, shift):
        pairs = [(a * rows + r, b * rows + (r + shift) % rows) for a, b in hops for r in range(rows)]
        return lax.ppermute(value, places, pairs)

    def spread(value, hops):
        return [send(value, hops, shift) for shift in range(rows)]

    def rows_of(value, holders):
        return [value] + [send(value, [(h, h) for h in holders], shift) for shift in range(1, rows)]

    def core_columns(own):
        turns = range(1, cores)
        return [own] + [lax.ppermute(own, "rhs", [(c, (c + t) % cores) for c in range(cores)]) for t in turns]

    def near(shape, dtype):
        return pltpu.VMEM(shape, dtype)

    half = near((count, width), BF16)
    half_f32 = near((count, width), F32)
    full = near((count, full_width), BF16)
    work = 2 * count * full_width * width
    square = near(inverse_diag.shape[1:], BF16)
    lower = near(lower_blocks.shape[1:], BF16)

    def depth_of(h):
        return top - 1 - sum((h + 1) % 2**power == 0 for power in range(1, top + 1))

    def holders(depth):
        return [(2 * p + 1) * 2 ** (top - depth - 1) - 1 for p in range(2**depth)]

    reduced, inverse_upper = call(
        first_kernel, [], [right_side, inverse_diag], [half, square],
        [pltpu.VMEM((count, width), F32), pltpu.SemaphoreType.DMA((2,))], far=2)
    gathered = rows_of(reduced, holders(0))
    inverse_upper = core_columns(inverse_upper)
    right, inverse_lower, lower_upper, lower_lower = call(
        load_kernel, [], [reduced, right_side, inverse_diag, lower_blocks],
        [near(right_side.shape, F32), square, lower, lower], [pltpu.SemaphoreType.DMA((4,))], far=3)
    inverse_lower = core_columns(inverse_lower)
    known = []
    solved = None
    for depth in range(top + 1):
        last = depth == top
        if depth > 0:
            slot = 0 if last else 1
            kernel = functools.partial(offset_kernel, depth, slot, rows)
            reduced = call(
                kernel, [position, block_rows],
                [right, lower_lower if last else lower_upper, *known, *pieces], [half],
                [pltpu.VMEM((count, depth * full_width), BF16), pltpu.VMEM((count, full_width), BF16)], work)
            gathered = rows_of(reduced, range(leafs) if last else holders(depth))
        if last:
            kernel = functools.partial(last_kernel, rows, cores)
            return call(kernel, [position], [*gathered, *inverse_lower, solved],
                        [jax.ShapeDtypeStruct(right_side.shape, F32)], (), work)
        here = holders(depth)
        if depth > 0:
            newest = call(functools.partial(whole_kernel, rows), [position], [reduced, *pieces], [full])
            known = [*known, newest]
        if depth + 1 < top:
            reach = 2 ** (top - depth - 2)
            left = [(h, h - reach) for h in here]
            right_hops = [(h, h + reach) for h in here]
            is_left = (depth_upper == depth + 1) & (((leaf + 1) // reach) % 4 == 1)
            is_right = (depth_upper == depth + 1) & (((leaf + 1) // reach) % 4 == 3)
            known = [jnp.where(is_left, send(k, left, 0), jnp.where(is_right, send(k, right_hops, 0), k)) for k in known]
        elif depth > 0:
            passed = []
            for index, k in enumerate(known):
                hops = [(h, h + 1) for h in here if depth_of(h + 1) <= index]
                goes = (leaf % 2 == 1) & (depth_upper <= index)
                passed.append(jnp.where(goes, send(k, hops, 0), k))
            known = passed
        kernel = functools.partial(solve_kernel, rows, cores, depth)
        arrays = [*gathered, *inverse_upper] + ([] if depth == 0 else [solved])
        rounded, solved = call(kernel, [position], arrays, [half, half_f32], (), work)
        if depth + 1 < top:
            lefts, rights = spread(rounded, left), spread(rounded, right_hops)
            pieces = [jnp.where(is_left, a, b) for a, b in zip(lefts, rights)]
        else:
            own = rows_of(rounded, here)
            others = spread(rounded, [(h, h + 1) for h in here])
            pieces = [jnp.where(leaf % 2 == 0, a, b) for a, b in zip(own, others)]


def solution(mesh):
    return jax.shard_map(
        local,
        mesh=mesh,
        in_specs=(
            P("leaf", "rhs", "rows"),
            P("leaf", None, ("rows", "rhs")),
            P("leaf", None, None, "rows"),
            P("leaf", None),
        ),
        out_specs=P("leaf", "rhs", "rows"),
        check_vma=False,
    )
```

```python
import functools
import jax
import jax.numpy as jnp
from jax import lax
from jax.experimental import pallas as pl
from jax.experimental.pallas import tpu as pltpu
from jax.sharding import PartitionSpec as P

F32 = jnp.float32
BF16 = jnp.bfloat16
VMEM = pltpu.VMEM


def first_kernel(right_ref, inverse_ref, cast_ref, inverse_out, staged, semaphores):
    weights = pltpu.make_async_copy(inverse_ref.at[1], inverse_out, semaphores.at[0])
    values = pltpu.make_async_copy(right_ref.at[1], staged, semaphores.at[1])
    values.start()
    weights.start()
    values.wait()
    cast_ref[...] = staged[...].astype(BF16)
    weights.wait()


def load_kernel(after_ref, right_ref, inverse_ref, lower_ref, right_out, inverse_out, upper_out, lower_out, semaphores):
    copies = [
        pltpu.make_async_copy(lower_ref.at[1], upper_out, semaphores.at[0]),
        pltpu.make_async_copy(inverse_ref.at[0], inverse_out, semaphores.at[1]),
        pltpu.make_async_copy(right_ref, right_out, semaphores.at[2]),
        pltpu.make_async_copy(lower_ref.at[0], lower_out, semaphores.at[3]),
    ]
    for copy in copies:
        copy.start()
    for copy in copies:
        copy.wait()


def place_pieces(position_ref, piece_refs, target_ref, base):
    rows = len(piece_refs)
    width = piece_refs[0].shape[1]
    for shift, piece_ref in enumerate(piece_refs):
        source = lax.rem(position_ref[0] - shift + rows, rows)
        target_ref[:, pl.ds(pl.multiple_of(base + source * width, width), width)] = piece_ref[...]


def whole_kernel(rows, position_ref, after_ref, *refs):
    place_pieces(position_ref, refs[:rows], refs[rows], 0)


def offset_kernel(level, slot, rows, position_ref, block_rows_ref, right_ref, lower_ref, *refs):
    full_refs = refs[:level - 1]
    piece_refs = refs[level - 1:level - 1 + rows]
    reduced_ref, joined, picked = refs[level - 1 + rows:]
    width = piece_refs[0].shape[1]
    blocks, block_width = lower_ref.shape[:2]
    for index, full_ref in enumerate(full_refs):
        joined[:, index * rows * width:(index + 1) * rows * width] = full_ref[...]
    place_pieces(position_ref, piece_refs, joined, (level - 1) * rows * width)
    highest = joined.shape[1] // block_width - 1
    for index in range(blocks):
        number = jnp.clip(block_rows_ref[slot, index], 0, highest)
        column = pl.multiple_of(number * block_width, block_width)
        picked[:, index * block_width:(index + 1) * block_width] = joined[:, pl.ds(column, block_width)]
    weights = lower_ref[...].reshape(blocks * block_width, width)
    offset = jnp.dot(picked[...], weights, preferred_element_type=F32)
    reduced_ref[...] = (right_ref[slot] - offset).astype(BF16)


def apply_inverse(cores, position_ref, piece_refs, inverse_refs, joined, store):
    quarter = inverse_refs[0].shape[-1]
    place_pieces(position_ref, piece_refs, joined, 0)
    for turn, inverse_ref in enumerate(inverse_refs):
        total = jnp.dot(joined[...], inverse_ref[...], preferred_element_type=F32)
        core = lax.rem(position_ref[1] - turn + cores, cores)
        store(pl.ds(pl.multiple_of(core * quarter, quarter), quarter), total)


def solve_kernel(rows, cores, depth_now, position_ref, *refs):
    piece_refs = refs[:rows]
    inverse_refs = refs[rows:rows + cores]
    rest = refs[rows + cores:]
    if depth_now == 0:
        before_ref, (rounded_ref, solved_ref, joined) = None, rest
    else:
        before_ref, rounded_ref, solved_ref, joined = rest
    active = position_ref[2] == depth_now

    def store(columns, total):
        rounded_ref[:, columns] = total.astype(BF16)
        before = jnp.zeros_like(total) if before_ref is None else before_ref[:, columns]
        solved_ref[:, columns] = jnp.where(active, total, before)

    apply_inverse(cores, position_ref, piece_refs, inverse_refs, joined, store)


def last_kernel(rows, cores, position_ref, *refs):
    piece_refs = refs[:rows]
    inverse_refs = refs[rows:rows + cores]
    before_ref, out_ref, joined = refs[rows + cores:]
    out_ref[1] = before_ref[...]

    def store(columns, total):
        out_ref[0, :, columns] = total

    apply_inverse(cores, position_ref, piece_refs, inverse_refs, joined, store)


SCALARS = pl.BlockSpec(memory_space=pltpu.SMEM)
WHOLE = pl.BlockSpec(memory_space=pltpu.VMEM)
FAR = pl.BlockSpec(memory_space=pltpu.HBM)


def call(kernel, scalars, arrays, outs, scratch=(), flops=0, far=0):
    several = len(outs) > 1
    size = sum(a.size * a.dtype.itemsize for a in arrays)
    here = len(arrays) - far
    spaces = [pltpu.VMEM] * here + [pltpu.HBM] * far
    arrays = [pltpu.with_memory_space_constraint(a, space) for a, space in zip(arrays, spaces)]
    return pl.pallas_call(
        kernel,
        in_specs=[SCALARS] * len(scalars) + [WHOLE] * here + [FAR] * far,
        out_specs=[WHOLE] * len(outs) if several else WHOLE,
        out_shape=list(outs) if several else outs[0],
        scratch_shapes=list(scratch),
        cost_estimate=pl.CostEstimate(flops=flops, bytes_accessed=size, transcendentals=0),
        compiler_params=pltpu.CompilerParams(vmem_limit_bytes=8 * 2**20),
    )(*scalars, *arrays)


def local(right_side, inverse_diag, lower_blocks, block_rows):
    leafs, rows, cores = (lax.axis_size(name) for name in ("leaf", "rows", "rhs"))
    top = leafs.bit_length() - 1
    leaf = lax.axis_index("leaf")
    depth_upper = top - 1 - sum(((leaf + 1) % 2**power == 0).astype(jnp.int32) for power in range(1, top + 1))
    position = jnp.stack([lax.axis_index("rows"), lax.axis_index("rhs"), depth_upper]).astype(jnp.int32)
    count, width = right_side.shape[1:]
    full_width = rows * width
    places = ("leaf", "rows")

    def send(value, hops, shift):
        pairs = [(a * rows + r, b * rows + (r + shift) % rows) for a, b in hops for r in range(rows)]
        return lax.ppermute(value, places, pairs)

    def spread(value, hops):
        return [send(value, hops, shift) for shift in range(rows)]

    def rows_of(value, holders):
        return [value] + [send(value, [(h, h) for h in holders], shift) for shift in range(1, rows)]

    def core_columns(own):
        turns = range(1, cores)
        return [own] + [lax.ppermute(own, "rhs", [(c, (c + t) % cores) for c in range(cores)]) for t in turns]

    def near(shape, dtype):
        return pltpu.VMEM(shape, dtype)

    half = near((count, width), BF16)
    half_f32 = near((count, width), F32)
    full = near((count, full_width), BF16)
    work = 2 * count * full_width * width
    joined = pltpu.VMEM((count, full_width), BF16)
    square = near(inverse_diag.shape[1:], BF16)
    lower = near(lower_blocks.shape[1:], BF16)

    def depth_of(h):
        return top - 1 - sum((h + 1) % 2**power == 0 for power in range(1, top + 1))

    def holders(depth):
        return [(2 * p + 1) * 2 ** (top - depth - 1) - 1 for p in range(2**depth)]

    reduced, inverse_upper = call(
        first_kernel, [], [right_side, inverse_diag], [half, square],
        [pltpu.VMEM((count, width), F32), pltpu.SemaphoreType.DMA((2,))], far=2)
    gathered = rows_of(reduced, holders(0))
    inverse_upper = core_columns(inverse_upper)
    right, inverse_lower, lower_upper, lower_lower = call(
        load_kernel, [], [reduced, right_side, inverse_diag, lower_blocks],
        [near(right_side.shape, F32), square, lower, lower], [pltpu.SemaphoreType.DMA((4,))], far=3)
    inverse_lower = core_columns(inverse_lower)
    known = []
    solved = None
    for depth in range(top + 1):
        last = depth == top
        if depth > 0:
            slot = 0 if last else 1
            kernel = functools.partial(offset_kernel, depth, slot, rows)
            reduced = call(
                kernel, [position, block_rows],
                [right, lower_lower if last else lower_upper, *known, *pieces], [half],
                [pltpu.VMEM((count, depth * full_width), BF16), joined], work)
            gathered = rows_of(reduced, range(leafs) if last else holders(depth))
        if last:
            kernel = functools.partial(last_kernel, rows, cores)
            return call(kernel, [position], [*gathered, *inverse_lower, solved],
                        [jax.ShapeDtypeStruct(right_side.shape, F32)], [joined], work)
        here = holders(depth)
        if depth > 0:
            newest = call(functools.partial(whole_kernel, rows), [position], [reduced, *pieces], [full], (), 8 * work)
            known = [*known, newest]
        if depth + 1 < top:
            reach = 2 ** (top - depth - 2)
            idle = [(h + (2 if reach == 1 else 1), h) for h in here]
            left = [(h, h - reach) for h in here] + idle
            right_hops = [(h, h + reach) for h in here] + idle
            is_left = (depth_upper == depth + 1) & (((leaf + 1) // reach) % 4 == 1)
            is_right = (depth_upper == depth + 1) & (((leaf + 1) // reach) % 4 == 3)
            known = [jnp.where(is_left, send(k, left, 0), jnp.where(is_right, send(k, right_hops, 0), k)) for k in known]
        elif depth > 0:
            passed = []
            for index, k in enumerate(known):
                hops = [(h, h + 1) for h in here if depth_of(h + 1) <= index]
                goes = (leaf % 2 == 1) & (depth_upper <= index)
                passed.append(jnp.where(goes, send(k, hops, 0), k))
            known = passed
        kernel = functools.partial(solve_kernel, rows, cores, depth)
        arrays = [*gathered, *inverse_upper] + ([] if depth == 0 else [solved])
        rounded, solved = call(kernel, [position], arrays, [half, half_f32], [joined], work)
        if depth + 1 < top:
            lefts, rights = spread(rounded, left), spread(rounded, right_hops)
            pieces = [jnp.where(is_left, a, b) for a, b in zip(lefts, rights)]
        else:
            own = rows_of(rounded, here)
            others = spread(rounded, [(h, h + 1) for h in here])
            pieces = [jnp.where(leaf % 2 == 0, a, b) for a, b in zip(own, others)]


def solution(mesh):
    return jax.shard_map(
        local,
        mesh=mesh,
        in_specs=(
            P("leaf", "rhs", "rows"),
            P("leaf", None, ("rows", "rhs")),
            P("leaf", None, None, "rows"),
            P("leaf", None),
        ),
        out_specs=P("leaf", "rhs", "rows"),
        check_vma=False,
    )
```

```python
import functools
import jax
import jax.numpy as jnp
from jax import lax
from jax.experimental import pallas as pl
from jax.experimental.pallas import tpu as pltpu
from jax.sharding import PartitionSpec as P

F32 = jnp.float32
BF16 = jnp.bfloat16


def upper_depth(leaf, top):
    return top - 1 - sum(((leaf + 1) % 2**power == 0).astype(jnp.int32) for power in range(1, top + 1))


def first_kernel(right_ref, inverse_ref, cast_ref, inverse_out, staged, semaphores):
    weights = pltpu.make_async_copy(inverse_ref.at[1], inverse_out, semaphores.at[0])
    values = pltpu.make_async_copy(right_ref.at[1], staged, semaphores.at[1])
    values.start()
    weights.start()
    values.wait()
    cast_ref[...] = staged[...].astype(BF16)
    weights.wait()


def upper_kernel(after_ref, right_ref, inverse_ref, lower_ref, right_out, lower_out, inverse_out, semaphores):
    copies = [
        pltpu.make_async_copy(lower_ref.at[1], lower_out, semaphores.at[0]),
        pltpu.make_async_copy(inverse_ref.at[0], inverse_out, semaphores.at[1]),
        pltpu.make_async_copy(right_ref, right_out, semaphores.at[2]),
    ]
    for copy in copies:
        copy.start()
    for copy in copies:
        copy.wait()


def lower_kernel(cores, after_ref, lower_ref, *refs):
    sources = [lower_ref.at[0], *refs[:cores]]
    targets = refs[cores:2 * cores + 1]
    semaphores = refs[2 * cores + 1]
    copies = [pltpu.make_async_copy(a, b, semaphores.at[i]) for i, (a, b) in enumerate(zip(sources, targets))]
    for copy in copies:
        copy.start()
    for copy in copies:
        copy.wait()


def place_pieces(piece_refs, target_ref, parts):
    rows = len(piece_refs)
    width = piece_refs[0].shape[1] // parts
    own = lax.axis_index("rows")
    first = target_ref.shape[1] // (rows * width) - parts
    for shift, piece_ref in enumerate(piece_refs):
        source = lax.rem(own - shift + rows, rows)
        for part in range(parts):
            column = (first + part) * rows * width + source * width
            from_column = (parts - 1 - part) * width
            target_ref[:, pl.ds(pl.multiple_of(column, width), width)] = piece_ref[:, from_column:from_column + width]


def place_either(choose, first_refs, second_refs, target_ref, parts):
    @pl.when(choose)
    def _():
        place_pieces(first_refs, target_ref, parts)

    @pl.when(jnp.logical_not(choose))
    def _():
        place_pieces(second_refs, target_ref, parts)


def offset_kernel(top, level, rows, block_rows_ref, right_ref, lower_ref, *refs):
    leaf = lax.axis_index("leaf")
    slot = 0 if level == top else 1
    first_refs, second_refs = refs[:rows], refs[rows:2 * rows]
    rest = refs[2 * rows:]
    width = right_ref.shape[2]
    numbers, semaphore, picked = rest[-3:]
    fetch = pltpu.make_async_copy(block_rows_ref, numbers, semaphore)
    fetch.start()
    if level == top:
        mine_ref, passed_ref, reduced_ref, joined = rest[:4]
        even = leaf % 2 == 0
        older = mine_ref.shape[1]

        @pl.when(even)
        def _():
            joined[:, :older] = mine_ref[...]

        @pl.when(jnp.logical_not(even))
        def _():
            joined[:, :older] = passed_ref[...]

        place_either(even, first_refs, second_refs, joined, 1)
    else:
        reduced_ref, joined = rest[:2]
        reach = 2 ** (top - level - 1)
        place_either(((leaf + 1) // reach) % 4 == 1, first_refs, second_refs, joined, level)
    blocks, block_width = lower_ref.shape[:2]
    highest = joined.shape[1] // block_width - 1
    fetch.wait()
    for index in range(blocks):
        number = jnp.clip(numbers[slot, index], 0, highest)
        column = pl.multiple_of(number * block_width, block_width)
        picked[:, index * block_width:(index + 1) * block_width] = joined[:, pl.ds(column, block_width)]
    weights = lower_ref[...].reshape(blocks * block_width, width)
    offset = jnp.dot(picked[...], weights, preferred_element_type=F32)
    reduced_ref[...] = (right_ref[slot] - offset).astype(BF16)


def apply_inverse(cores, piece_refs, inverse_refs, joined, store):
    quarter = inverse_refs[0].shape[-1]
    place_pieces(piece_refs, joined, 1)
    own = lax.axis_index("rhs")
    for turn, inverse_ref in enumerate(inverse_refs):
        total = jnp.dot(joined[...], inverse_ref[...], preferred_element_type=F32)
        core = lax.rem(own - turn + cores, cores)
        store(pl.ds(pl.multiple_of(core * quarter, quarter), quarter), total)


def solve_kernel(top, depth, rows, cores, carried, *refs):
    piece_refs = refs[:rows]
    inverse_refs = refs[rows:rows + cores]
    rest = list(refs[rows + cores:])
    joined = rest.pop()
    before_ref = rest.pop(0) if depth > 0 else None
    first_refs = [rest.pop(0) for _ in range(2 if carried else 0)]
    rounded_ref, solved_ref = rest
    width = piece_refs[0].shape[1]
    leaf = lax.axis_index("leaf")
    active = upper_depth(leaf, top) == depth
    if carried:
        reach = 2 ** (top - depth - 1)
        is_left = ((leaf + 1) // reach) % 4 == 1
        for wanted, ref in zip((is_left, jnp.logical_not(is_left)), first_refs):
            @pl.when(wanted)
            def _():
                rounded_ref[:, width:] = ref[...]

    def store(columns, total):
        rounded_ref[:, columns] = total.astype(BF16)
        before = jnp.zeros_like(total) if before_ref is None else before_ref[:, columns]
        solved_ref[:, columns] = jnp.where(active, total, before)

    apply_inverse(cores, piece_refs, inverse_refs, joined, store)


def last_kernel(rows, cores, *refs):
    piece_refs = refs[:rows]
    inverse_refs = refs[rows:rows + cores]
    before_ref, out_ref, joined = refs[rows + cores:]
    out_ref[1] = before_ref[...]

    def store(columns, total):
        out_ref[0, :, columns] = total

    apply_inverse(cores, piece_refs, inverse_refs, joined, store)


WHOLE = pl.BlockSpec(memory_space=pltpu.VMEM)
FAR = pl.BlockSpec(memory_space=pltpu.HBM)


def call(kernel, near, far, outs, scratch=(), flops=0):
    several = len(outs) > 1
    size = sum(a.size * a.dtype.itemsize for a in [*near, *far])
    near = [pltpu.with_memory_space_constraint(a, pltpu.VMEM) for a in near]
    far = [pltpu.with_memory_space_constraint(a, pltpu.HBM) for a in far]
    specs = [FAR if getattr(o, "memory_space", None) == pltpu.HBM else WHOLE for o in outs]
    return pl.pallas_call(
        kernel,
        in_specs=[WHOLE] * len(near) + [FAR] * len(far),
        out_specs=specs if several else specs[0],
        out_shape=list(outs) if several else outs[0],
        scratch_shapes=list(scratch),
        cost_estimate=pl.CostEstimate(flops=flops, bytes_accessed=size, transcendentals=0),
        compiler_params=pltpu.CompilerParams(vmem_limit_bytes=8 * 2**20),
    )(*near, *far)


def local(right_side, inverse_diag, lower_blocks, block_rows):
    leafs, rows, cores = (lax.axis_size(name) for name in ("leaf", "rows", "rhs"))
    top = leafs.bit_length() - 1
    count, width = right_side.shape[1:]
    full_width = rows * width
    places = ("leaf", "rows")

    def send(value, hops, shift):
        pairs = [(a * rows + r, b * rows + (r + shift) % rows) for a, b in hops for r in range(rows)]
        return lax.ppermute(value, places, pairs)

    def spread(value, hops):
        return [send(value, hops, shift) for shift in range(rows)]

    def rows_of(value, holders):
        return [value] + [send(value, [(h, h) for h in holders], shift) for shift in range(1, rows)]

    def core_columns(own):
        turns = range(1, cores)
        return [own] + [lax.ppermute(own, "rhs", [(c, (c + t) % cores) for c in range(cores)]) for t in turns]

    def holders(depth):
        return [(2 * p + 1) * 2 ** (top - depth - 1) - 1 for p in range(2**depth)]

    near = pltpu.VMEM
    half = near((count, width), BF16)
    half_f32 = near((count, width), F32)
    square = near(inverse_diag.shape[1:], BF16)
    lower = near(lower_blocks.shape[1:], BF16)
    joined = near((count, full_width), BF16)
    work = 2 * count * full_width * width
    semaphores = lambda n: pltpu.SemaphoreType.DMA((n,))

    reduced, inverse_upper = call(
        first_kernel, [], [right_side, inverse_diag], [half, square], [near((count, width), F32), semaphores(2)])
    gathered = rows_of(reduced, holders(0))
    inverse_upper = core_columns(inverse_upper)
    right, lower_upper, inverse_own = call(
        upper_kernel, [reduced], [right_side, inverse_diag, lower_blocks],
        [near(right_side.shape, F32), lower, pltpu.HBM(square.shape, BF16)], [semaphores(3)])
    inverse_lower = core_columns(inverse_own)
    solved = None
    lower_now = lower_upper
    for depth in range(top + 1):
        if depth > 0:
            all_joined = near((count, depth * full_width), BF16)
            fetched = [pltpu.SMEM(block_rows.shape, jnp.int32), pltpu.SemaphoreType.DMA(()), joined]
            kernel = functools.partial(offset_kernel, top, depth, rows)
            if depth == top:
                reduced = call(kernel, [block_rows, right, lower_now, *lefts, *rights, mine, passed], [],
                               [half], [all_joined, *fetched], work)
            elif depth == top - 1:
                reduced, mine = call(kernel, [block_rows, right, lower_now, *lefts, *rights], [],
                                     [half, all_joined], fetched, work)
                passed = send(mine, [(h, h + 1) for h in holders(depth)], 0)
            else:
                reduced = call(kernel, [block_rows, right, lower_now, *lefts, *rights], [],
                               [half], [all_joined, *fetched], work)
            gathered = rows_of(reduced, range(leafs) if depth == top else holders(depth))
        if depth == top:
            return call(functools.partial(last_kernel, rows, cores), [*gathered, *inverse_lower, solved], [],
                        [jax.ShapeDtypeStruct(right_side.shape, F32)], [joined], work)
        here = holders(depth)
        carried = depth > 0 and depth + 1 < top
        parts = depth + 1 if carried else 1
        kernel = functools.partial(solve_kernel, top, depth, rows, cores, carried)
        arrays = [*gathered, *inverse_upper] + ([solved] if depth else []) + ([lefts[0], rights[0]] if carried else [])
        rounded, solved = call(kernel, arrays, [], [near((count, parts * width), BF16), half_f32], [joined], work)
        if depth + 1 < top:
            reach = 2 ** (top - depth - 2)
            lefts = spread(rounded, [(h, h - reach) for h in here])
            rights = spread(rounded, [(h, h + reach) for h in here])
        else:
            lefts = rows_of(rounded, here)
            rights = spread(rounded, [(h, h + 1) for h in here])
            lower_now, *inverse_lower = call(
                functools.partial(lower_kernel, cores), [rounded], [lower_blocks, *inverse_lower],
                [lower] + [square] * cores, [semaphores(cores + 1)])


def solution(mesh):
    return jax.shard_map(
        local,
        mesh=mesh,
        in_specs=(
            P("leaf", "rhs", "rows"),
            P("leaf", None, ("rows", "rhs")),
            P("leaf", None, None, "rows"),
            P("leaf", None),
        ),
        out_specs=P("leaf", "rhs", "rows"),
        check_vma=False,
    )
```

```python
import functools
import jax
import jax.numpy as jnp
from jax import lax
from jax.experimental import pallas as pl
from jax.experimental.pallas import tpu as pltpu
from jax.sharding import PartitionSpec as P

F32 = jnp.float32
BF16 = jnp.bfloat16


def upper_depth(leaf, top):
    return top - 1 - sum(((leaf + 1) % 2**power == 0).astype(jnp.int32) for power in range(1, top + 1))


def first_kernel(right_ref, inverse_ref, cast_ref, inverse_out, staged, semaphores):
    weights = pltpu.make_async_copy(inverse_ref.at[1], inverse_out, semaphores.at[0])
    values = pltpu.make_async_copy(right_ref.at[1], staged, semaphores.at[1])
    values.start()
    weights.start()
    values.wait()
    cast_ref[...] = staged[...].astype(BF16)
    weights.wait()


def load_kernel(after_ref, right_ref, inverse_ref, lower_ref, *refs):
    semaphores = refs[-1]
    sources = [lower_ref.at[1], right_ref, inverse_ref.at[0], lower_ref.at[0]]
    copies = [pltpu.make_async_copy(a, b, semaphores.at[i]) for i, (a, b) in enumerate(zip(sources, refs[:-1]))]
    for copy in copies:
        copy.start()
    for copy in copies:
        copy.wait()


def place_pieces(piece_refs, target_ref, start):
    rows = len(piece_refs)
    width = piece_refs[0].shape[1]
    own = lax.axis_index("rows")
    for shift, piece_ref in enumerate(piece_refs):
        source = lax.rem(own - shift + rows, rows)
        target_ref[:, pl.ds(pl.multiple_of(start + source * width, width), width)] = piece_ref[...]


def offset_kernel(top, level, rows, block_rows_ref, right_ref, lower_ref, *refs):
    leaf = lax.axis_index("leaf")
    slot = 0 if level == top else 1
    pieces = [refs[:rows], refs[rows:2 * rows]]
    older = 2 if level > 1 else 0
    older_refs = refs[2 * rows:2 * rows + older]
    reduced_ref, joined, numbers, semaphore, picked = refs[-5:]
    width = right_ref.shape[2]
    fetch = pltpu.make_async_copy(block_rows_ref, numbers, semaphore)
    fetch.start()
    reach = 2 ** (top - level - 1) if level < top else 1
    first = leaf % 2 == 0 if level == top else ((leaf + 1) // reach) % 4 == 1
    before = (level - 1) * rows * width
    for which, wanted in enumerate((first, jnp.logical_not(first))):
        @pl.when(wanted)
        def _():
            if older:
                joined[:, :before] = older_refs[which][...]
            place_pieces(pieces[which], joined, before)
    blocks, block_width = lower_ref.shape[:2]
    highest = joined.shape[1] // block_width - 1
    fetch.wait()
    for index in range(blocks):
        number = jnp.clip(numbers[slot, index], 0, highest)
        column = pl.multiple_of(number * block_width, block_width)
        picked[:, index * block_width:(index + 1) * block_width] = joined[:, pl.ds(column, block_width)]
    weights = lower_ref[...].reshape(blocks * block_width, width)
    offset = jnp.dot(picked[...], weights, preferred_element_type=F32)
    reduced_ref[...] = (right_ref[slot] - offset).astype(BF16)


def apply_inverse(cores, piece_refs, inverse_refs, joined, store):
    quarter = inverse_refs[0].shape[-1]
    place_pieces(piece_refs, joined, 0)
    own = lax.axis_index("rhs")
    for turn, inverse_ref in enumerate(inverse_refs):
        total = jnp.dot(joined[...], inverse_ref[...], preferred_element_type=F32)
        core = lax.rem(own - turn + cores, cores)
        store(pl.ds(pl.multiple_of(core * quarter, quarter), quarter), total)


def solve_kernel(top, depth, rows, cores, *refs):
    piece_refs = refs[:rows]
    inverse_refs = refs[rows:rows + cores]
    before_ref = refs[rows + cores] if depth > 0 else None
    rounded_ref, solved_ref, joined = refs[-3:]
    active = upper_depth(lax.axis_index("leaf"), top) == depth

    def store(columns, total):
        rounded_ref[:, columns] = total.astype(BF16)
        before = jnp.zeros_like(total) if before_ref is None else before_ref[:, columns]
        solved_ref[:, columns] = jnp.where(active, total, before)

    apply_inverse(cores, piece_refs, inverse_refs, joined, store)


def last_kernel(rows, cores, *refs):
    piece_refs = refs[:rows]
    inverse_refs = refs[rows:rows + cores]
    before_ref, out_ref, joined = refs[rows + cores:]
    out_ref[1] = before_ref[...]

    def store(columns, total):
        out_ref[0, :, columns] = total

    apply_inverse(cores, piece_refs, inverse_refs, joined, store)


WHOLE = pl.BlockSpec(memory_space=pltpu.VMEM)
FAR = pl.BlockSpec(memory_space=pltpu.HBM)


def call(kernel, near, far, outs, scratch=(), flops=0):
    several = len(outs) > 1
    size = sum(a.size * a.dtype.itemsize for a in [*near, *far])
    near = [pltpu.with_memory_space_constraint(a, pltpu.VMEM) for a in near]
    far = [pltpu.with_memory_space_constraint(a, pltpu.HBM) for a in far]
    specs = [FAR if getattr(o, "memory_space", None) == pltpu.HBM else WHOLE for o in outs]
    return pl.pallas_call(
        kernel,
        in_specs=[WHOLE] * len(near) + [FAR] * len(far),
        out_specs=specs if several else specs[0],
        out_shape=list(outs) if several else outs[0],
        scratch_shapes=list(scratch),
        cost_estimate=pl.CostEstimate(flops=flops, bytes_accessed=size, transcendentals=0),
        compiler_params=pltpu.CompilerParams(vmem_limit_bytes=8 * 2**20),
    )(*near, *far)


def local(right_side, inverse_diag, lower_blocks, block_rows):
    leafs, rows, cores = (lax.axis_size(name) for name in ("leaf", "rows", "rhs"))
    top = leafs.bit_length() - 1
    count, width = right_side.shape[1:]
    full_width = rows * width
    places = ("leaf", "rows")

    def send(value, hops, shift):
        pairs = [(a * rows + r, b * rows + (r + shift) % rows) for a, b in hops for r in range(rows)]
        return lax.ppermute(value, places, pairs)

    def spread(value, hops):
        return [send(value, hops, shift) for shift in range(rows)]

    def rows_of(value, holders):
        return [value] + [send(value, [(h, h) for h in holders], shift) for shift in range(1, rows)]

    def core_columns(own):
        turns = range(1, cores)
        return [own] + [lax.ppermute(own, "rhs", [(c, (c + t) % cores) for c in range(cores)]) for t in turns]

    def holders(depth):
        return [(2 * p + 1) * 2 ** (top - depth - 1) - 1 for p in range(2**depth)]

    near = pltpu.VMEM
    half = near((count, width), BF16)
    half_f32 = near((count, width), F32)
    square = near(inverse_diag.shape[1:], BF16)
    lower = near(lower_blocks.shape[1:], BF16)
    joined = near((count, full_width), BF16)
    work = 2 * count * full_width * width
    semaphores = lambda n: pltpu.SemaphoreType.DMA((n,))

    reduced, inverse_upper = call(
        first_kernel, [], [right_side, inverse_diag], [half, square], [near((count, width), F32), semaphores(2)])
    gathered = rows_of(reduced, holders(0))
    inverse_upper = core_columns(inverse_upper)
    solved = None
    kept = []
    for depth in range(top + 1):
        if depth > 0:
            all_joined = near((count, depth * full_width), BF16)
            fetched = [pltpu.SMEM(block_rows.shape, jnp.int32), pltpu.SemaphoreType.DMA(()), joined]
            kernel = functools.partial(offset_kernel, top, depth, rows)
            weights = kept[0] if depth == top else lower_upper
            arrays = [block_rows, right, weights, *lefts, *rights, *older]
            if depth == top:
                reduced = call(kernel, arrays, [], [half], [all_joined, *fetched], work)
            else:
                reduced, mine = call(kernel, [*arrays, *kept], [], [half, all_joined], fetched, work)
            gathered = rows_of(reduced, range(leafs) if depth == top else holders(depth))
        if depth == top:
            return call(functools.partial(last_kernel, rows, cores), [*gathered, *kept[1:], solved], [],
                        [jax.ShapeDtypeStruct(right_side.shape, F32)], [joined], work)
        here = holders(depth)
        if depth + 1 < top:
            reach = 2 ** (top - depth - 2)
            ways = [[(h, h - reach) for h in here], [(h, h + reach) for h in here]]
            older = [send(mine, way, 0) for way in ways] if depth else []
        else:
            over = [(h, h + 1) for h in here]
            older = [mine, send(mine, over, 0)]
        kernel = functools.partial(solve_kernel, top, depth, rows, cores)
        arrays = [*gathered, *inverse_upper] + ([solved] if depth else []) + kept
        rounded, solved = call(kernel, arrays, [], [half, half_f32], [joined], work)
        if depth + 1 < top:
            lefts, rights = [spread(rounded, way) for way in ways]
        else:
            lefts, rights = rows_of(rounded, here), spread(rounded, over)
        if depth == 0:
            lower_upper, right, inverse_own, lower_own = call(
                load_kernel, [rounded], [right_side, inverse_diag, lower_blocks],
                [lower, near(right_side.shape, F32), square, lower], [semaphores(4)])
            kept = [lower_own, *core_columns(inverse_own)]


def solution(mesh):
    return jax.shard_map(
        local,
        mesh=mesh,
        in_specs=(
            P("leaf", "rhs", "rows"),
            P("leaf", None, ("rows", "rhs")),
            P("leaf", None, None, "rows"),
            P("leaf", None),
        ),
        out_specs=P("leaf", "rhs", "rows"),
        check_vma=False,
    )
```

```python
import functools
import jax
import jax.numpy as jnp
from jax import lax
from jax.experimental import pallas as pl
from jax.experimental.pallas import tpu as pltpu
from jax.sharding import PartitionSpec as P

F32 = jnp.float32
BF16 = jnp.bfloat16


def upper_depth(leaf, top):
    return top - 1 - sum(((leaf + 1) % 2**power == 0).astype(jnp.int32) for power in range(1, top + 1))


def cast_kernel(right_ref, cast_ref, staged, semaphore):
    values = pltpu.make_async_copy(right_ref.at[1], staged, semaphore)
    values.start()
    values.wait()
    cast_ref[...] = staged[...].astype(BF16)


def load_kernel(after_ref, right_ref, inverse_ref, lower_ref, right_out, inverse_out, lower_out, semaphores):
    pairs = [(inverse_ref, inverse_out), (right_ref, right_out), (lower_ref, lower_out)]
    copies = [pltpu.make_async_copy(a, b, semaphores.at[i]) for i, (a, b) in enumerate(pairs)]
    for copy in copies:
        copy.start()
    for copy in copies:
        copy.wait()


def place_pieces(piece_refs, target_ref, start):
    rows = len(piece_refs)
    width = piece_refs[0].shape[1]
    own = lax.axis_index("rows")
    for shift, piece_ref in enumerate(piece_refs):
        source = lax.rem(own - shift + rows, rows)
        target_ref[:, pl.ds(pl.multiple_of(start + source * width, width), width)] = piece_ref[...]


def offset_kernel(top, level, rows, plan, block_rows_ref, right_ref, lower_ref, *refs):
    leaf = lax.axis_index("leaf")
    slot = 0 if level == top else 1
    pieces = [refs[:rows], refs[rows:2 * rows]]
    extra = refs[2 * rows:-5]
    reduced_ref, joined, numbers, semaphore, picked = refs[-5:]
    width = right_ref.shape[2]
    fetch = pltpu.make_async_copy(block_rows_ref, numbers, semaphore)
    fetch.start()
    reach = 2 ** (top - level - 1) if level < top else 1
    first = leaf % 2 == 0 if level == top else ((leaf + 1) // reach) % 4 == 1
    before = (level - 1) * rows * width
    for which, wanted in enumerate((first, jnp.logical_not(first))):
        @pl.when(wanted)
        def _():
            if plan == "crossed":
                place_pieces(pieces[1 - which], joined, 0)
            elif before:
                joined[:, :before] = extra[which][...]
            place_pieces(pieces[which], joined, before)
    blocks, block_width = lower_ref.shape[1:3]
    highest = joined.shape[1] // block_width - 1
    fetch.wait()
    for index in range(blocks):
        number = jnp.clip(numbers[slot, index], 0, highest)
        column = pl.multiple_of(number * block_width, block_width)
        picked[:, index * block_width:(index + 1) * block_width] = joined[:, pl.ds(column, block_width)]
    weights = lower_ref[slot].reshape(blocks * block_width, width)
    offset = jnp.dot(picked[...], weights, preferred_element_type=F32)
    reduced_ref[...] = (right_ref[slot] - offset).astype(BF16)
    if plan == "held":
        @pl.when(upper_depth(leaf, top) == 0)
        def _():
            reduced_ref[...] = extra[0][...]


def apply_inverse(slot, cores, piece_refs, inverse_refs, joined, store):
    quarter = inverse_refs[0].shape[-1]
    place_pieces(piece_refs, joined, 0)
    own = lax.axis_index("rhs")
    for turn, inverse_ref in enumerate(inverse_refs):
        total = jnp.dot(joined[...], inverse_ref[slot], preferred_element_type=F32)
        core = lax.rem(own - turn + cores, cores)
        store(pl.ds(pl.multiple_of(core * quarter, quarter), quarter), total)


def solve_kernel(top, depth, rows, cores, plan, *refs):
    piece_refs = refs[:rows]
    inverse_refs = refs[rows:rows + cores]
    before_ref = refs[rows + cores] if depth > 0 else None
    held_ref = refs[rows + cores + 1] if plan == "held" else None
    rounded_ref, solved_ref, joined = refs[-3:]
    leaf = lax.axis_index("leaf")
    active = upper_depth(leaf, top) == depth

    def store(columns, total):
        rounded_ref[:, columns] = total.astype(BF16)
        before = jnp.zeros_like(total) if before_ref is None else before_ref[:, columns]
        solved_ref[:, columns] = jnp.where(active, total, before)

    apply_inverse(1, cores, piece_refs, inverse_refs, joined, store)
    if plan == "held":
        @pl.when(upper_depth(leaf, top) == 0)
        def _():
            rounded_ref[...] = held_ref[...]

        @pl.when(leaf == lax.axis_size("leaf") - 1)
        def _():
            rounded_ref[...] = piece_refs[1][...]


def last_kernel(rows, cores, *refs):
    piece_refs = refs[:rows]
    inverse_refs = refs[rows:rows + cores]
    before_ref, out_ref, joined = refs[rows + cores:]
    out_ref[1] = before_ref[...]

    def store(columns, total):
        out_ref[0, :, columns] = total

    apply_inverse(0, cores, piece_refs, inverse_refs, joined, store)


WHOLE = pl.BlockSpec(memory_space=pltpu.VMEM)
FAR = pl.BlockSpec(memory_space=pltpu.HBM)


def call(kernel, near, far, outs, scratch=(), flops=0):
    several = len(outs) > 1
    size = sum(a.size * a.dtype.itemsize for a in [*near, *far])
    near = [pltpu.with_memory_space_constraint(a, pltpu.VMEM) for a in near]
    far = [pltpu.with_memory_space_constraint(a, pltpu.HBM) for a in far]
    specs = [FAR if getattr(o, "memory_space", None) == pltpu.HBM else WHOLE for o in outs]
    return pl.pallas_call(
        kernel,
        in_specs=[WHOLE] * len(near) + [FAR] * len(far),
        out_specs=specs if several else specs[0],
        out_shape=list(outs) if several else outs[0],
        scratch_shapes=list(scratch),
        cost_estimate=pl.CostEstimate(flops=flops, bytes_accessed=size, transcendentals=0),
        compiler_params=pltpu.CompilerParams(vmem_limit_bytes=8 * 2**20),
    )(*near, *far)


def local(right_side, inverse_diag, lower_blocks, block_rows):
    leafs, rows, cores = (lax.axis_size(name) for name in ("leaf", "rows", "rhs"))
    top = leafs.bit_length() - 1
    count, width = right_side.shape[1:]
    full_width = rows * width
    places = ("leaf", "rows")

    def send(value, hops, shift):
        pairs = [(a * rows + r, b * rows + (r + shift) % rows) for a, b in hops for r in range(rows)]
        return lax.ppermute(value, places, pairs)

    def spread(value, hops):
        return [send(value, hops, shift) for shift in range(rows)]

    def rows_of(value, holders, others=()):
        arrived = [value]
        for shift in range(1, rows):
            pairs = [(h * rows + r, h * rows + (r + shift) % rows) for h in holders for r in range(rows)]
            if shift == 1:
                pairs += [(a * rows + r, b * rows + r) for a, b in others for r in range(rows)]
            arrived.append(lax.ppermute(value, places, pairs))
        return arrived

    def core_columns(own):
        turns = range(1, cores)
        return [own] + [lax.ppermute(own, "rhs", [(c, (c + t) % cores) for c in range(cores)]) for t in turns]

    def holders(depth):
        return [(2 * p + 1) * 2 ** (top - depth - 1) - 1 for p in range(2**depth)]

    near = pltpu.VMEM
    half = near((count, width), BF16)
    half_f32 = near((count, width), F32)
    joined = near((count, full_width), BF16)
    work = 2 * count * full_width * width
    semaphores = lambda n: pltpu.SemaphoreType.DMA((n,))

    crossing = top == 3 and rows > 1
    spare = leafs - 1
    swapped = core_columns(inverse_diag)[1:]
    reduced = call(cast_kernel, [], [right_side], [half], [near((count, width), F32), pltpu.SemaphoreType.DMA(())])
    gathered = rows_of(reduced, holders(0))
    right, inverse_own, lower = call(
        load_kernel, [reduced], [right_side, inverse_diag, lower_blocks],
        [near(a.shape, a.dtype) for a in (right_side, inverse_diag, lower_blocks)], [semaphores(3)])
    inverses = [inverse_own, *swapped]
    solved = None
    for depth in range(top + 1):
        held = crossing and depth == 1
        crossed = crossing and depth == 2
        if depth > 0:
            all_joined = near((count, depth * full_width), BF16)
            fetched = [pltpu.SMEM(block_rows.shape, jnp.int32), pltpu.SemaphoreType.DMA(()), joined]
            plan = "held" if held else "crossed" if crossed else "plain"
            kernel = functools.partial(offset_kernel, top, depth, rows, plan)
            arrays = [block_rows, right, lower, *lefts, *rights, *older] + ([rounded] if held else [])
            if depth == top:
                reduced = call(kernel, arrays, [], [half], [all_joined, *fetched], work)
            else:
                reduced, mine = call(kernel, arrays, [], [half, all_joined], fetched, work)
            others = [(h, spare) for h in holders(0)] if held else []
            gathered = rows_of(reduced, range(leafs) if depth == top else holders(depth), others)
        if depth == top:
            return call(functools.partial(last_kernel, rows, cores), [*gathered, *inverses, solved], [],
                        [jax.ShapeDtypeStruct(right_side.shape, F32)], [joined], work)
        here = holders(depth)
        older = []
        if depth + 1 < top:
            reach = 2 ** (top - depth - 2)
            ways = [[(h, h - reach) for h in here], [(h, h + reach) for h in here]]
            if held:
                tops = [*holders(0), spare]
                ways = [ways[0] + [(h, h - reach) for h in tops], ways[1] + [(h, h - 3 * reach) for h in tops]]
            elif depth > 0:
                older = [send(mine, way, 0) for way in ways]
        else:
            over = [(h, h + 1) for h in here]
            older = [mine, send(mine, over, 0)]
        kernel = functools.partial(solve_kernel, top, depth, rows, cores, "held" if held else "plain")
        arrays = [*gathered, *inverses] + ([solved] if depth else []) + ([rounded] if held else [])
        rounded, solved = call(kernel, arrays, [], [half, half_f32], [joined], work)
        if depth + 1 < top:
            lefts, rights = [spread(rounded, way) for way in ways]
        else:
            lefts, rights = rows_of(rounded, here), spread(rounded, over)


def solution(mesh):
    return jax.shard_map(
        local,
        mesh=mesh,
        in_specs=(
            P("leaf", "rhs", "rows"),
            P("leaf", None, ("rows", "rhs")),
            P("leaf", None, None, "rows"),
            P("leaf", None),
        ),
        out_specs=P("leaf", "rhs", "rows"),
        check_vma=False,
    )
```

```python
import functools
import jax
import jax.numpy as jnp
from jax import lax
from jax.experimental import pallas as pl
from jax.experimental.pallas import tpu as pltpu
from jax.sharding import PartitionSpec as P

F32 = jnp.float32
BF16 = jnp.bfloat16


def upper_depth(leaf, top):
    return top - 1 - sum(((leaf + 1) % 2**power == 0).astype(jnp.int32) for power in range(1, top + 1))


def first_kernel(right_ref, inverse_ref, cast_ref, inverse_out, staged, semaphores):
    weights = pltpu.make_async_copy(inverse_ref.at[1], inverse_out, semaphores.at[0])
    values = pltpu.make_async_copy(right_ref.at[1], staged, semaphores.at[1])
    values.start()
    weights.start()
    values.wait()
    cast_ref[...] = staged[...].astype(BF16)
    weights.wait()


def load_kernel(after_ref, right_ref, lower_ref, right_out, lower_out, semaphores):
    pairs = [(lower_ref.at[1], lower_out), (right_ref, right_out)]
    copies = [pltpu.make_async_copy(a, b, semaphores.at[i]) for i, (a, b) in enumerate(pairs)]
    for copy in copies:
        copy.start()
    for copy in copies:
        copy.wait()


def place_pieces(piece_refs, target_ref, start):
    rows = len(piece_refs)
    width = piece_refs[0].shape[1]
    own = lax.axis_index("rows")
    for shift, piece_ref in enumerate(piece_refs):
        source = lax.rem(own - shift + rows, rows)
        target_ref[:, pl.ds(pl.multiple_of(start + source * width, width), width)] = piece_ref[...]


def offset_kernel(top, level, rows, plan, fetch, block_rows_ref, right_ref, lower_ref, *refs):
    leaf = lax.axis_index("leaf")
    slot = 0 if level == top else 1
    pieces = [refs[:rows], refs[rows:2 * rows]]
    if fetch:
        *refs, far_ref, reduced_ref, near_ref, joined, numbers, semaphores, picked = refs
        load = pltpu.make_async_copy(far_ref.at[0], near_ref, semaphores.at[1])
        load.start()
    else:
        *refs, reduced_ref, joined, numbers, semaphores, picked = refs
    extra = refs[2 * rows:]
    width = right_ref.shape[2]
    listed = pltpu.make_async_copy(block_rows_ref, numbers, semaphores.at[0])
    listed.start()
    reach = 2 ** (top - level - 1) if level < top else 1
    first = leaf % 2 == 0 if level == top else ((leaf + 1) // reach) % 4 == 1
    before = (level - 1) * rows * width
    for which, wanted in enumerate((first, jnp.logical_not(first))):
        @pl.when(wanted)
        def _():
            if plan == "crossed":
                place_pieces(pieces[1 - which], joined, 0)
            elif before:
                joined[:, :before] = extra[which][...]
            place_pieces(pieces[which], joined, before)
    blocks, block_width = lower_ref.shape[:2]
    highest = joined.shape[1] // block_width - 1
    listed.wait()
    for index in range(blocks):
        number = jnp.clip(numbers[slot, index], 0, highest)
        column = pl.multiple_of(number * block_width, block_width)
        picked[:, index * block_width:(index + 1) * block_width] = joined[:, pl.ds(column, block_width)]
    weights = lower_ref[...].reshape(blocks * block_width, width)
    offset = jnp.dot(picked[...], weights, preferred_element_type=F32)
    reduced_ref[...] = (right_ref[slot] - offset).astype(BF16)
    if plan == "held":
        @pl.when(upper_depth(leaf, top) == 0)
        def _():
            reduced_ref[...] = extra[0][...]

    if fetch:
        load.wait()


def apply_inverse(cores, piece_refs, inverse_refs, joined, store):
    quarter = inverse_refs[0].shape[-1]
    place_pieces(piece_refs, joined, 0)
    own = lax.axis_index("rhs")
    for turn, inverse_ref in enumerate(inverse_refs):
        total = jnp.dot(joined[...], inverse_ref[...], preferred_element_type=F32)
        core = lax.rem(own - turn + cores, cores)
        store(pl.ds(pl.multiple_of(core * quarter, quarter), quarter), total)


def solve_kernel(top, depth, rows, cores, plan, fetch, *refs):
    piece_refs = refs[:rows]
    inverse_refs = refs[rows:rows + cores]
    before_ref = refs[rows + cores] if depth > 0 else None
    held_ref = refs[rows + cores + 1] if plan == "held" else None
    if fetch:
        far_ref, rounded_ref, solved_ref, near_ref, joined, semaphore = refs[-6:]
        load = pltpu.make_async_copy(far_ref.at[0], near_ref, semaphore)
        load.start()
    else:
        rounded_ref, solved_ref, joined = refs[-3:]
    leaf = lax.axis_index("leaf")
    active = upper_depth(leaf, top) == depth

    def store(columns, total):
        rounded_ref[:, columns] = total.astype(BF16)
        before = jnp.zeros_like(total) if before_ref is None else before_ref[:, columns]
        solved_ref[:, columns] = jnp.where(active, total, before)

    apply_inverse(cores, piece_refs, inverse_refs, joined, store)
    if plan == "held":
        @pl.when(upper_depth(leaf, top) == 0)
        def _():
            rounded_ref[...] = held_ref[...]

        @pl.when(leaf == lax.axis_size("leaf") - 1)
        def _():
            rounded_ref[...] = piece_refs[1][...]

    if fetch:
        load.wait()


def last_kernel(rows, cores, *refs):
    piece_refs = refs[:rows]
    inverse_refs = refs[rows:rows + cores]
    before_ref, out_ref, joined, staged, semaphores = refs[rows + cores:]
    copies = [pltpu.make_async_copy(before_ref, out_ref.at[1], semaphores.at[0])]
    copies[0].start()

    def store(columns, total):
        staged[:, columns] = total
        copy = pltpu.make_async_copy(staged.at[:, columns], out_ref.at[0, :, columns], semaphores.at[len(copies)])
        copy.start()
        copies.append(copy)

    apply_inverse(cores, piece_refs, inverse_refs, joined, store)
    for copy in copies:
        copy.wait()


WHOLE = pl.BlockSpec(memory_space=pltpu.VMEM)
FAR = pl.BlockSpec(memory_space=pltpu.HBM)


def call(kernel, near, far, outs, scratch=(), flops=0):
    several = len(outs) > 1
    size = sum(a.size * a.dtype.itemsize for a in [*near, *far])
    near = [pltpu.with_memory_space_constraint(a, pltpu.VMEM) for a in near]
    far = [pltpu.with_memory_space_constraint(a, pltpu.HBM) for a in far]
    specs = [FAR if getattr(o, "memory_space", None) == pltpu.HBM else WHOLE for o in outs]
    return pl.pallas_call(
        kernel,
        in_specs=[WHOLE] * len(near) + [FAR] * len(far),
        out_specs=specs if several else specs[0],
        out_shape=list(outs) if several else outs[0],
        scratch_shapes=list(scratch),
        cost_estimate=pl.CostEstimate(flops=flops, bytes_accessed=size, transcendentals=0),
        compiler_params=pltpu.CompilerParams(vmem_limit_bytes=8 * 2**20),
    )(*near, *far)


def local(right_side, inverse_diag, lower_blocks, block_rows):
    leafs, rows, cores = (lax.axis_size(name) for name in ("leaf", "rows", "rhs"))
    top = leafs.bit_length() - 1
    count, width = right_side.shape[1:]
    full_width = rows * width
    places = ("leaf", "rows")

    def send(value, hops, shift):
        pairs = [(a * rows + r, b * rows + (r + shift) % rows) for a, b in hops for r in range(rows)]
        return lax.ppermute(value, places, pairs)

    def spread(value, hops):
        return [send(value, hops, shift) for shift in range(rows)]

    def rows_of(value, swaps=()):
        trading = dict([*swaps, *((b, a) for a, b in swaps)])
        arrived = [value]
        for shift in range(1, rows):
            pairs = [(h * rows + r, trading[h] * rows + r) if h in trading and shift == 1 else
                     (h * rows + r, h * rows + (r + shift) % rows) for h in range(leafs) for r in range(rows)]
            arrived.append(lax.ppermute(value, places, pairs))
        return arrived

    def ring(value, stops):
        after = dict(zip(stops, [*stops[1:], stops[0]]))
        pairs = [(h * rows + r, after[h] * rows + r if h in after else h * rows + (r + 1) % rows)
                 for h in range(leafs) for r in range(rows)]
        return lax.ppermute(value, places, pairs)

    def core_columns(own):
        turns = range(1, cores)
        return [own] + [lax.ppermute(own, "rhs", [(c, (c + t) % cores) for c in range(cores)]) for t in turns]

    def holders(depth):
        return [(2 * p + 1) * 2 ** (top - depth - 1) - 1 for p in range(2**depth)]

    near = pltpu.VMEM
    half = near((count, width), BF16)
    half_f32 = near((count, width), F32)
    joined = near((count, full_width), BF16)
    work = 2 * count * full_width * width
    semaphores = lambda n: pltpu.SemaphoreType.DMA((n,))

    crossing = top == 3 and rows == 2
    spare = leafs - 1
    square = near(inverse_diag.shape[1:], BF16)
    blocks = near(lower_blocks.shape[1:], BF16)
    reduced, own_columns = call(
        first_kernel, [], [right_side, inverse_diag], [half, square], [near((count, width), F32), semaphores(2)])
    inverses = core_columns(own_columns)
    gathered = rows_of(reduced)
    right, lower = call(
        load_kernel, [reduced], [right_side, lower_blocks], [near(right_side.shape, F32), blocks], [semaphores(2)])
    solved = None
    kept = []
    for depth in range(top + 1):
        held = crossing and depth == 1
        crossed = crossing and depth == 2
        if depth > 0:
            all_joined = near((count, depth * full_width), BF16)
            fetched = [pltpu.SMEM(block_rows.shape, jnp.int32), semaphores(2), joined]
            plan = "held" if held else "crossed" if crossed else "plain"
            kernel = functools.partial(offset_kernel, top, depth, rows, plan, depth == 1)
            arrays = [block_rows, right, kept[0] if depth == top else lower, *lefts, *rights, *older]
            arrays += ([rounded] if held else []) + ([] if depth == top else kept)
            passes = depth == top - 1 or (depth < top and not crossing)
            outs = [half] + ([blocks] if depth == 1 else []) + ([all_joined] if passes else [])
            scratch = ([] if passes else [all_joined]) + fetched
            reduced = call(kernel, arrays, [lower_blocks] if depth == 1 else [], outs, scratch, work)
            if passes:
                *reduced, mine = reduced
                reduced = reduced if depth == 1 else reduced[0]
            if depth == 1:
                reduced, lower_last = reduced
                kept = [lower_last]
            gathered = rows_of(reduced, [(h, spare) for h in holders(0)] if held else ())
        if depth == top:
            pieces = [near((count, width), F32), semaphores(cores + 1)]
            return call(functools.partial(last_kernel, rows, cores), [*gathered, *kept[1:], solved], [],
                        [pltpu.HBM(right_side.shape, F32)], [joined, *pieces], work)
        here = holders(depth)
        older = []
        if depth + 1 < top:
            reach = 2 ** (top - depth - 2)
            ways = [[(h, h - reach) for h in here], [(h, h + reach) for h in here]]
            if held:
                tops = [*holders(0), spare]
                ways = [ways[0] + [(h, h - reach) for h in tops], ways[1] + [(h, h - 3 * reach) for h in tops]]
            elif depth > 0:
                older = [send(mine, way, 0) for way in ways]
        else:
            over = [(h, h + 1) for h in here]
            older = [mine, send(mine, over, 0)]
        kernel = functools.partial(solve_kernel, top, depth, rows, cores, "held" if held else "plain", depth == 1)
        arrays = [*gathered, *inverses] + ([solved] if depth else []) + ([rounded] if held else []) + kept
        if depth == 1:
            rounded, solved, own_last = call(
                kernel, arrays, [inverse_diag], [half, half_f32, square], [joined, pltpu.SemaphoreType.DMA(())], work)
            kept += core_columns(own_last)
        else:
            rounded, solved = call(kernel, arrays, [], [half, half_f32], [joined], work)
        if crossing and depth == 0:
            (root,) = here
            cross = [[send(rounded, way, shift) for way in ways[::-1]] for shift in range(1, rows)]
            rights = [ring(rounded, [root, root + reach, root + 1])]
            lefts = [ring(rounded, [root, root - reach, root - 1])]
            rights += [pair[0] for pair in cross]
            lefts += [pair[1] for pair in cross]
        elif depth + 1 < top:
            rights, lefts = [spread(rounded, way) for way in ways[::-1]]
        else:
            rights = spread(rounded, over)
            lefts = rows_of(rounded)


def solution(mesh):
    return jax.shard_map(
        local,
        mesh=mesh,
        in_specs=(
            P("leaf", "rhs", "rows"),
            P("leaf", None, ("rows", "rhs")),
            P("leaf", None, None, "rows"),
            P("leaf", None),
        ),
        out_specs=P("leaf", "rhs", "rows"),
        check_vma=False,
    )
```

```python
import functools
import jax
import jax.numpy as jnp
from jax import lax
from jax.experimental import pallas as pl
from jax.experimental.pallas import tpu as pltpu
from jax.sharding import PartitionSpec as P

F32 = jnp.float32
BF16 = jnp.bfloat16


def upper_depth(leaf, top):
    return top - 1 - sum(((leaf + 1) % 2**power == 0).astype(jnp.int32) for power in range(1, top + 1))


def cast_kernel(right_ref, cast_ref, staged, semaphore):
    values = pltpu.make_async_copy(right_ref.at[1], staged, semaphore)
    values.start()
    values.wait()
    cast_ref[...] = staged[...].astype(BF16)


def load_kernel(count, after_ref, *refs):
    semaphores = refs[-1]
    copies = [pltpu.make_async_copy(refs[i], refs[count + i], semaphores.at[i]) for i in range(count)]
    for copy in copies:
        copy.start()
    for copy in copies:
        copy.wait()


def place_pieces(piece_refs, target_ref, start):
    rows = len(piece_refs)
    width = piece_refs[0].shape[1]
    own = lax.axis_index("rows")
    for shift, piece_ref in enumerate(piece_refs):
        source = lax.rem(own - shift + rows, rows)
        target_ref[:, pl.ds(pl.multiple_of(start + source * width, width), width)] = piece_ref[...]


def offset_kernel(top, level, rows, plan, block_rows_ref, right_ref, lower_ref, *refs):
    leaf = lax.axis_index("leaf")
    slot = 0 if level == top else 1
    *refs, reduced_ref, joined, numbers, semaphore, picked = refs
    if level == top:
        pieces = [refs[1:2 * rows:2], refs[:2 * rows:2]]
    else:
        pieces = [refs[:2 * rows:2][::-1], refs[1:2 * rows:2][::-1]]
    extra = refs[2 * rows:]
    width = right_ref.shape[2]
    full = rows * width
    listed = pltpu.make_async_copy(block_rows_ref, numbers, semaphore)
    listed.start()
    reach = 2 ** (top - level - 1) if level < top else 1
    first = leaf % 2 == 0 if level == top else ((leaf + 1) // reach) % 4 == 1
    before = (level - 1) * full
    for which, wanted in enumerate((first, jnp.logical_not(first))):
        @pl.when(wanted)
        def _():
            if plan == "crossed":
                place_pieces(pieces[1 - which], joined, 0)
            elif plan != "traded" and before:
                joined[:, :before] = extra[which][...]
            place_pieces(pieces[which], joined, before)
    if plan == "traded":
        mine_ref, both_ref, passed_ref, *roots = extra

        @pl.when(leaf % 2 == 0)
        def _():
            joined[:, :before] = mine_ref[...]

        for which, place in enumerate((1, 3)):
            @pl.when((leaf % 4 == 1) & ((leaf + 1) // 2 % 4 == place))
            def _():
                place_pieces(roots[which::2][::-1], joined, 0)
                joined[:, full:before] = both_ref[...]

        @pl.when(leaf % 4 == 3)
        def _():
            joined[:, :full] = both_ref[...]
            joined[:, full:before] = passed_ref[...]
    blocks, block_width = lower_ref.shape[1:3]
    highest = joined.shape[1] // block_width - 1
    listed.wait()
    for index in range(blocks):
        number = jnp.clip(numbers[slot, index], 0, highest)
        column = pl.multiple_of(number * block_width, block_width)
        picked[:, index * block_width:(index + 1) * block_width] = joined[:, pl.ds(column, block_width)]
    weights = lower_ref[slot].reshape(blocks * block_width, width)
    offset = jnp.dot(picked[...], weights, preferred_element_type=F32)
    reduced_ref[...] = (right_ref[slot] - offset).astype(BF16)
    if plan in ("held", "crossed"):
        @pl.when(upper_depth(leaf, top) == 0 if plan == "held" else leaf % 2 == 1)
        def _():
            reduced_ref[...] = extra[0][...]


def apply_inverse(slot, cores, piece_refs, inverse_refs, joined, store):
    quarter = inverse_refs[0].shape[-1]
    place_pieces(piece_refs, joined, 0)
    own = lax.axis_index("rhs")
    for turn, inverse_ref in enumerate(inverse_refs):
        total = jnp.dot(joined[...], inverse_ref[slot], preferred_element_type=F32)
        core = lax.rem(own - turn + cores, cores)
        store(pl.ds(pl.multiple_of(core * quarter, quarter), quarter), total)


def solve_kernel(top, depth, rows, cores, plan, *refs):
    piece_refs = refs[:rows]
    inverse_refs = refs[rows:rows + cores]
    before_ref = refs[rows + cores] if depth > 0 else None
    held_ref = refs[rows + cores + 1] if plan == "held" else None
    rounded_ref, solved_ref, joined = refs[-3:]
    leaf = lax.axis_index("leaf")
    active = upper_depth(leaf, top) == depth

    def store(columns, total):
        rounded_ref[:, columns] = total.astype(BF16)
        before = jnp.zeros_like(total) if before_ref is None else before_ref[:, columns]
        solved_ref[:, columns] = jnp.where(active, total, before)

    apply_inverse(1, cores, piece_refs, inverse_refs, joined, store)
    if plan == "held":
        @pl.when(upper_depth(leaf, top) == 0)
        def _():
            rounded_ref[...] = held_ref[...]

        @pl.when(leaf == lax.axis_size("leaf") - 1)
        def _():
            rounded_ref[...] = piece_refs[1][...]


def last_kernel(rows, cores, *refs):
    piece_refs = refs[:rows]
    inverse_refs = refs[rows:rows + cores]
    before_ref, out_ref, joined, staged, semaphores = refs[rows + cores:]
    copies = [pltpu.make_async_copy(before_ref, out_ref.at[1], semaphores.at[0])]
    copies[0].start()

    def store(columns, total):
        staged[:, columns] = total
        copy = pltpu.make_async_copy(staged.at[:, columns], out_ref.at[0, :, columns], semaphores.at[len(copies)])
        copy.start()
        copies.append(copy)

    apply_inverse(0, cores, piece_refs, inverse_refs, joined, store)
    for copy in copies:
        copy.wait()


WHOLE = pl.BlockSpec(memory_space=pltpu.VMEM)
FAR = pl.BlockSpec(memory_space=pltpu.HBM)


def call(kernel, near, far, outs, scratch=(), flops=0):
    several = len(outs) > 1
    size = sum(a.size * a.dtype.itemsize for a in [*near, *far])
    near = [pltpu.with_memory_space_constraint(a, pltpu.VMEM) for a in near]
    far = [pltpu.with_memory_space_constraint(a, pltpu.HBM) for a in far]
    specs = [FAR if getattr(o, "memory_space", None) == pltpu.HBM else WHOLE for o in outs]
    return pl.pallas_call(
        kernel,
        in_specs=[WHOLE] * len(near) + [FAR] * len(far),
        out_specs=specs if several else specs[0],
        out_shape=list(outs) if several else outs[0],
        scratch_shapes=list(scratch),
        cost_estimate=pl.CostEstimate(flops=flops, bytes_accessed=size, transcendentals=0),
        compiler_params=pltpu.CompilerParams(vmem_limit_bytes=8 * 2**20),
    )(*near, *far)


def local(right_side, inverse_diag, lower_blocks, block_rows):
    leafs, rows, cores = (lax.axis_size(name) for name in ("leaf", "rows", "rhs"))
    top = leafs.bit_length() - 1
    count, width = right_side.shape[1:]
    full_width = rows * width
    places = ("leaf", "rows")

    def send(value, hops, shift):
        pairs = [(a * rows + r, b * rows + (r + shift) % rows) for a, b in hops for r in range(rows)]
        return lax.ppermute(value, places, pairs)

    def spread(value, hops):
        return [send(value, hops, shift) for shift in range(rows)]

    def rows_of(value, swaps=()):
        trading = dict([*swaps, *((b, a) for a, b in swaps)])
        arrived = [value]
        for shift in range(1, rows):
            pairs = [(h * rows + r, trading[h] * rows + r) if h in trading and shift == 1 else
                     (h * rows + r, h * rows + (r + shift) % rows) for h in range(leafs) for r in range(rows)]
            arrived.append(lax.ppermute(value, places, pairs))
        return arrived

    def ring(value, stops):
        after = dict(zip(stops, [*stops[1:], stops[0]]))
        pairs = [(h * rows + r, after[h] * rows + r if h in after else h * rows + (r + 1) % rows)
                 for h in range(leafs) for r in range(rows)]
        return lax.ppermute(value, places, pairs)

    def core_columns(own):
        turns = range(1, cores)
        return [own] + [lax.ppermute(own, "rhs", [(c, (c + t) % cores) for c in range(cores)]) for t in turns]

    def holders(depth):
        return [(2 * p + 1) * 2 ** (top - depth - 1) - 1 for p in range(2**depth)]

    near = pltpu.VMEM
    half = near((count, width), BF16)
    half_f32 = near((count, width), F32)
    joined = near((count, full_width), BF16)
    work = 2 * count * full_width * width
    semaphores = lambda n: pltpu.SemaphoreType.DMA((n,))

    crossing = top == 3 and rows == 2
    spare = leafs - 1
    swapped = core_columns(inverse_diag)[1:]

    def load(after, arrays):
        outs = [near(a.shape, a.dtype) for a in arrays]
        return call(functools.partial(load_kernel, len(arrays)), [after], arrays, outs, [semaphores(len(arrays))])

    def paired(lefts, rights):
        return [piece for pair in zip(lefts[::-1], rights[::-1]) for piece in pair]

    reduced = call(cast_kernel, [], [right_side], [half], [near((count, width), F32), pltpu.SemaphoreType.DMA(())])
    gathered = rows_of(reduced)
    inverses = [load(reduced, [inverse_diag]), *swapped]
    solved = None
    for depth in range(top + 1):
        held = crossing and depth == 1
        crossed = crossing and depth == 2
        if depth > 0:
            all_joined = near((count, depth * full_width), BF16)
            fetched = [pltpu.SMEM(block_rows.shape, jnp.int32), pltpu.SemaphoreType.DMA(()), joined]
            plan = "held" if held else "crossed" if crossed else "traded" if crossing else "plain"
            kernel = functools.partial(offset_kernel, top, depth, rows, plan)
            extra = older + ([rounded] if held or crossed else [])
            pieces = paired(rights[::-1], lefts[::-1]) if depth == top else paired(lefts, rights)
            arrays = [block_rows, right, lower, *pieces, *extra]
            if depth < top and not held:
                reduced, mine = call(kernel, arrays, [], [half, all_joined], fetched, work)
            else:
                reduced = call(kernel, arrays, [], [half], [all_joined, *fetched], work)
            gathered = rows_of(reduced, [(h, spare) for h in holders(0)] if held else ())
        if depth == top:
            staged = [near((count, width), F32), semaphores(cores + 1)]
            return call(functools.partial(last_kernel, rows, cores), [*gathered, *inverses, solved], [],
                        [pltpu.HBM(right_side.shape, F32)], [joined, *staged], work)
        here = holders(depth)
        older = []
        if depth + 1 < top:
            reach = 2 ** (top - depth - 2)
            ways = [[(h, h - reach) for h in here], [(h, h + reach) for h in here]]
            if held:
                tops = [*holders(0), spare]
                ways = [ways[0] + [(h, h - reach) for h in tops], ways[1] + [(h, h - 3 * reach) for h in tops]]
            elif depth > 0:
                older = [send(mine, way, 0) for way in ways]
        else:
            over = [(h, h + 1) for h in here]
            older = [] if crossing else [mine, send(mine, over, 0)]
        kernel = functools.partial(solve_kernel, top, depth, rows, cores, "held" if held else "plain")
        arrays = [*gathered, *inverses] + ([solved] if depth else []) + ([rounded] if held else [])
        if crossed:
            both_full = near((count, full_width), BF16)
            rounded, solved, both = call(kernel, arrays, [], [half, half_f32, both_full], (), work)
            passed = send(both, [(h, h + 2) for h in holders(1)], 0)
            older = [mine, both, passed, *roots]
        else:
            rounded, solved = call(kernel, arrays, [], [half, half_f32], [joined], work)
        if crossing and depth == 0:
            (root,) = here
            lefts = [ring(rounded, [root, root - reach, root - 1]), send(rounded, ways[0], 1)]
            rights = [ring(rounded, [root, root + reach, root + 1]), send(rounded, ways[1], 1)]
            roots = paired(lefts, rights)
        elif depth + 1 < top:
            lefts, rights = [spread(rounded, way) for way in ways]
        else:
            lefts, rights = rows_of(rounded), spread(rounded, over)
        if depth == 0:
            right, lower = load(rounded, [right_side, lower_blocks])


def solution(mesh):
    return jax.shard_map(
        local,
        mesh=mesh,
        in_specs=(
            P("leaf", "rhs", "rows"),
            P("leaf", None, ("rows", "rhs")),
            P("leaf", None, None, "rows"),
            P("leaf", None),
        ),
        out_specs=P("leaf", "rhs", "rows"),
        check_vma=False,
    )
```

```python
import functools
import jax
import jax.numpy as jnp
from jax import lax
from jax.experimental import pallas as pl
from jax.experimental.pallas import tpu as pltpu
from jax.sharding import PartitionSpec as P

F32 = jnp.float32
BF16 = jnp.bfloat16


def upper_depth(leaf, top):
    return top - 1 - sum(((leaf + 1) % 2**power == 0).astype(jnp.int32) for power in range(1, top + 1))


def cast_kernel(right_ref, cast_ref, staged, semaphore):
    values = pltpu.make_async_copy(right_ref.at[1], staged, semaphore)
    values.start()
    values.wait()
    cast_ref[...] = staged[...].astype(BF16)


def load_kernel(count, after_ref, *refs):
    semaphores = refs[-1]
    copies = [pltpu.make_async_copy(refs[i], refs[count + i], semaphores.at[i]) for i in range(count)]
    for copy in copies:
        copy.start()
    for copy in copies:
        copy.wait()


def place_pieces(piece_refs, target_ref, start):
    rows = len(piece_refs)
    width = piece_refs[0].shape[1]
    own = lax.axis_index("rows")
    for shift, piece_ref in enumerate(piece_refs):
        source = lax.rem(own - shift + rows, rows)
        target_ref[:, pl.ds(pl.multiple_of(start + source * width, width), width)] = piece_ref[...]


def offset_kernel(top, level, rows, plan, block_rows_ref, right_ref, lower_ref, *refs):
    leaf = lax.axis_index("leaf")
    slot = 0 if level == top else 1
    if plan == "rooted":
        *refs, reduced_ref, piece_ref, joined, numbers, semaphore, picked = refs
    else:
        *refs, reduced_ref, joined, numbers, semaphore, picked = refs
    if plan in ("crossed", "traded"):
        late_ref, *refs = refs
    if level == top:
        pieces = [refs[1:2 * rows:2], refs[:2 * rows:2]]
    else:
        pieces = [refs[:2 * rows:2][::-1], refs[1:2 * rows:2][::-1]]
    extra = refs[2 * rows:]
    width = right_ref.shape[2]
    full = rows * width
    listed = pltpu.make_async_copy(block_rows_ref, numbers, semaphore)
    listed.start()
    reach = 2 ** (top - level - 1) if level < top else 1
    first = leaf % 2 == 0 if level == top else ((leaf + 1) // reach) % 4 == 1
    before = (level - 1) * full
    for which, wanted in enumerate((first, jnp.logical_not(first))):
        @pl.when(wanted)
        def _():
            if plan == "rooted":
                piece_ref[...] = pieces[which][0][...]
            elif plan == "plain" and before:
                joined[:, :before] = extra[which][...]
            place_pieces(pieces[which], joined, before)
    if plan == "crossed":
        place_pieces([extra[0], late_ref], joined, 0)
    elif plan == "traded":
        for wanted, ref in ((leaf % 2 == 0, extra[0]), (leaf % 4 == 1, extra[1]), (leaf % 4 == 3, late_ref)):
            @pl.when(wanted)
            def _():
                joined[:, :before] = ref[...]
    blocks, block_width = lower_ref.shape[1:3]
    highest = joined.shape[1] // block_width - 1
    listed.wait()
    for index in range(blocks):
        number = jnp.clip(numbers[slot, index], 0, highest)
        column = pl.multiple_of(number * block_width, block_width)
        picked[:, index * block_width:(index + 1) * block_width] = joined[:, pl.ds(column, block_width)]
    weights = lower_ref[slot].reshape(blocks * block_width, width)
    offset = jnp.dot(picked[...], weights, preferred_element_type=F32)
    reduced_ref[...] = (right_ref[slot] - offset).astype(BF16)
    if plan == "crossed":
        @pl.when(leaf % 2 == 1)
        def _():
            reduced_ref[...] = extra[1][...]


def apply_inverse(slot, cores, piece_refs, inverse_refs, joined, store):
    quarter = inverse_refs[0].shape[-1]
    place_pieces(piece_refs, joined, 0)
    own = lax.axis_index("rhs")
    for turn, inverse_ref in enumerate(inverse_refs):
        total = jnp.dot(joined[...], inverse_ref[slot], preferred_element_type=F32)
        core = lax.rem(own - turn + cores, cores)
        store(pl.ds(pl.multiple_of(core * quarter, quarter), quarter), total)


def solve_kernel(top, depth, rows, cores, plan, *refs):
    piece_refs = refs[:rows]
    inverse_refs = refs[rows:rows + cores]
    before_ref = refs[rows + cores] if depth > 0 else None
    if plan == "crossed":
        own_ref, *root_refs = refs[rows + cores + 1:-4]
        rounded_ref, solved_ref, both_ref, joined = refs[-4:]
    else:
        rounded_ref, solved_ref, joined = refs[-3:]
    leaf = lax.axis_index("leaf")
    active = upper_depth(leaf, top) == depth

    def store(columns, total):
        rounded_ref[:, columns] = total.astype(BF16)
        before = jnp.zeros_like(total) if before_ref is None else before_ref[:, columns]
        solved_ref[:, columns] = jnp.where(active, total, before)

    apply_inverse(1, cores, piece_refs, inverse_refs, joined, store)
    if plan == "crossed":
        for which, place in enumerate((1, 3)):
            @pl.when((leaf % 4 == 1) & ((leaf + 1) // 2 % 4 == place))
            def _():
                place_pieces([own_ref, root_refs[which]], both_ref, 0)
                both_ref[:, joined.shape[1]:] = joined[...]


def last_kernel(rows, cores, *refs):
    piece_refs = refs[:rows]
    inverse_refs = refs[rows:rows + cores]
    before_ref, out_ref, joined, staged, semaphores = refs[rows + cores:]
    copies = [pltpu.make_async_copy(before_ref, out_ref.at[1], semaphores.at[0])]
    copies[0].start()

    def store(columns, total):
        staged[:, columns] = total
        copy = pltpu.make_async_copy(staged.at[:, columns], out_ref.at[0, :, columns], semaphores.at[len(copies)])
        copy.start()
        copies.append(copy)

    apply_inverse(0, cores, piece_refs, inverse_refs, joined, store)
    for copy in copies:
        copy.wait()


WHOLE = pl.BlockSpec(memory_space=pltpu.VMEM)
FAR = pl.BlockSpec(memory_space=pltpu.HBM)


def call(kernel, near, far, outs, scratch=(), flops=0):
    several = len(outs) > 1
    size = sum(a.size * a.dtype.itemsize for a in [*near, *far])
    near = [pltpu.with_memory_space_constraint(a, pltpu.VMEM) for a in near]
    far = [pltpu.with_memory_space_constraint(a, pltpu.HBM) for a in far]
    specs = [FAR if getattr(o, "memory_space", None) == pltpu.HBM else WHOLE for o in outs]
    return pl.pallas_call(
        kernel,
        in_specs=[WHOLE] * len(near) + [FAR] * len(far),
        out_specs=specs if several else specs[0],
        out_shape=list(outs) if several else outs[0],
        scratch_shapes=list(scratch),
        cost_estimate=pl.CostEstimate(flops=flops, bytes_accessed=size, transcendentals=0),
        compiler_params=pltpu.CompilerParams(vmem_limit_bytes=8 * 2**20),
    )(*near, *far)


def local(right_side, inverse_diag, lower_blocks, block_rows):
    leafs, rows, cores = (lax.axis_size(name) for name in ("leaf", "rows", "rhs"))
    top = leafs.bit_length() - 1
    count, width = right_side.shape[1:]
    full_width = rows * width
    places = ("leaf", "rows")

    def send(value, hops, shift):
        pairs = [(a * rows + r, b * rows + (r + shift) % rows) for a, b in hops for r in range(rows)]
        return lax.ppermute(value, places, pairs)

    def spread(value, hops):
        return [send(value, hops, shift) for shift in range(rows)]

    def rows_of(value):
        arrived = [value]
        for shift in range(1, rows):
            pairs = [(h * rows + r, h * rows + (r + shift) % rows) for h in range(leafs) for r in range(rows)]
            arrived.append(lax.ppermute(value, places, pairs))
        return arrived

    def ring(value, *rings):
        after = {a: b for stops in rings for a, b in zip(stops, [*stops[1:], stops[0]])}
        pairs = [(h * rows + r, after[h] * rows + r if h in after else h * rows + (r + 1) % rows)
                 for h in range(leafs) for r in range(rows)]
        return lax.ppermute(value, places, pairs)

    def core_columns(own):
        turns = range(1, cores)
        return [own] + [lax.ppermute(own, "rhs", [(c, (c + t) % cores) for c in range(cores)]) for t in turns]

    def holders(depth):
        return [(2 * p + 1) * 2 ** (top - depth - 1) - 1 for p in range(2**depth)]

    near = pltpu.VMEM
    half = near((count, width), BF16)
    half_f32 = near((count, width), F32)
    joined = near((count, full_width), BF16)
    work = 2 * count * full_width * width
    semaphores = lambda n: pltpu.SemaphoreType.DMA((n,))

    crossing = top == 3 and rows == 2
    swapped = core_columns(inverse_diag)[1:]

    def load(after, arrays):
        outs = [near(a.shape, a.dtype) for a in arrays]
        return call(functools.partial(load_kernel, len(arrays)), [after], arrays, outs, [semaphores(len(arrays))])

    def paired(lefts, rights):
        return [piece for pair in zip(lefts[::-1], rights[::-1]) for piece in pair]

    reduced = call(cast_kernel, [], [right_side], [half], [near((count, width), F32), pltpu.SemaphoreType.DMA(())])
    gathered = rows_of(reduced)
    inverses = [load(reduced, [inverse_diag]), *swapped]
    plans = ["rooted", "crossed", "traded"] if crossing else ["plain"] * top
    plans = ["plain", *plans]
    older = []
    solved = None
    for depth, plan in enumerate(plans):
        if depth > 0:
            all_joined = near((count, depth * full_width), BF16)
            fetched = [pltpu.SMEM(block_rows.shape, jnp.int32), pltpu.SemaphoreType.DMA(()), joined]
            kernel = functools.partial(offset_kernel, top, depth, rows, plan)
            pieces = paired(rights[::-1], lefts[::-1]) if depth == top else paired(lefts, rights)
            if plan == "crossed":
                older = [late, *pieces, relayed, rounded]
            elif plan == "traded":
                older = [passed, *pieces, mine, both]
            else:
                older = [*pieces, *older]
            arrays = [block_rows, right, lower, *older]
            if plan == "rooted":
                reduced, own_root = call(kernel, arrays, [], [half, half], [all_joined, *fetched], work)
            elif depth < top:
                reduced, mine = call(kernel, arrays, [], [half, all_joined], fetched, work)
            else:
                reduced = call(kernel, arrays, [], [half], [all_joined, *fetched], work)
        if depth > 0:
            gathered = rows_of(reduced)
        if depth == top:
            staged = [near((count, width), F32), semaphores(cores + 1)]
            return call(functools.partial(last_kernel, rows, cores), [*gathered, *inverses, solved], [],
                        [pltpu.HBM(right_side.shape, F32)], [joined, *staged], work)
        here = holders(depth)
        older = []
        if depth + 1 < top:
            reach = 2 ** (top - depth - 2)
            ways = [[(h, h - reach) for h in here], [(h, h + reach) for h in here]]
            if plan == "rooted":
                sides = [ring(own_root, *way) for way in ways]
                relayed = jnp.where(lax.axis_index("leaf") % 4 == 0, *sides)
            elif depth > 0:
                older = [send(mine, way, 0) for way in ways]
        else:
            over = [(h, h + 1) for h in here]
            older = [] if crossing else [mine, send(mine, over, 0)]
        kernel = functools.partial(solve_kernel, top, depth, rows, cores, plan)
        arrays = [*gathered, *inverses] + ([solved] if depth else [])
        if plan == "crossed":
            rounded, solved, both = call(kernel, [*arrays, own_root, *roots], [],
                                         [half, half_f32, all_joined], [joined], work)
            passed = send(both, [(h, h + 2) for h in holders(1)], 0)
        else:
            rounded, solved = call(kernel, arrays, [], [half, half_f32], [joined], work)
        if crossing and depth == 0:
            (root,) = here
            lefts = [ring(rounded, [root, root - reach, root - 1]), send(rounded, ways[0], 1)]
            rights = [ring(rounded, [root, root + reach, root + 1]), send(rounded, ways[1], 1)]
            roots = [lefts[1], rights[1]]
        elif depth + 1 < top:
            lefts, rights = [spread(rounded, way) for way in ways]
            if plan == "rooted":
                late = rows_of(relayed)[1]
        else:
            lefts, rights = rows_of(rounded), spread(rounded, over)
        if depth == 0:
            right, lower = load(rounded, [right_side, lower_blocks])


def solution(mesh):
    return jax.shard_map(
        local,
        mesh=mesh,
        in_specs=(
            P("leaf", "rhs", "rows"),
            P("leaf", None, ("rows", "rhs")),
            P("leaf", None, None, "rows"),
            P("leaf", None),
        ),
        out_specs=P("leaf", "rhs", "rows"),
        check_vma=False,
    )
```

```python
import functools
import jax
import jax.numpy as jnp
from jax import lax
from jax.experimental import pallas as pl
from jax.experimental.pallas import tpu as pltpu
from jax.sharding import PartitionSpec as P

F32 = jnp.float32
BF16 = jnp.bfloat16


def upper_depth(leaf, top):
    return top - 1 - sum(((leaf + 1) % 2**power == 0).astype(jnp.int32) for power in range(1, top + 1))


def cast_kernel(right_ref, cast_ref, staged, semaphore):
    values = pltpu.make_async_copy(right_ref.at[1], staged, semaphore)
    values.start()
    values.wait()
    cast_ref[...] = staged[...].astype(BF16)


def load_kernel(count, after_ref, *refs):
    semaphores = refs[-1]
    copies = [pltpu.make_async_copy(refs[i], refs[count + i], semaphores.at[i]) for i in range(count)]
    for copy in copies:
        copy.start()
    for copy in copies:
        copy.wait()


def choose_kernel(first_ref, second_ref, own_ref, out_ref):
    leaf = lax.axis_index("leaf")
    first = (leaf % 4 == 0) | (leaf == lax.axis_size("leaf") - 1)
    second = leaf % 4 == 2
    for wanted, ref in ((first, first_ref), (second, second_ref), (jnp.logical_not(first | second), own_ref)):
        @pl.when(wanted)
        def _():
            out_ref[...] = ref[...]


def place_pieces(piece_refs, target_ref, start):
    rows = len(piece_refs)
    width = piece_refs[0].shape[1]
    own = lax.axis_index("rows")
    for shift, piece_ref in enumerate(piece_refs):
        source = lax.rem(own - shift + rows, rows)
        target_ref[:, pl.ds(pl.multiple_of(start + source * width, width), width)] = piece_ref[...]


def offset_kernel(top, level, rows, plan, block_rows_ref, right_ref, lower_ref, *refs):
    leaf = lax.axis_index("leaf")
    slot = 0 if level == top else 1
    if plan == "rooted":
        *refs, reduced_ref, piece_ref, joined, numbers, semaphore, picked = refs
    else:
        *refs, reduced_ref, joined, numbers, semaphore, picked = refs
    if plan == "crossed":
        late_ref, *refs = refs
    if level == top:
        pieces = [refs[1:2 * rows:2], refs[:2 * rows:2]]
        if plan == "traded":
            pieces[1] = pieces[1][::-1]
    else:
        pieces = [refs[:2 * rows:2][::-1], refs[1:2 * rows:2][::-1]]
    extra = refs[2 * rows:]
    width = right_ref.shape[2]
    full = rows * width
    listed = pltpu.make_async_copy(block_rows_ref, numbers, semaphore)
    listed.start()
    reach = 2 ** (top - level - 1) if level < top else 1
    first = leaf % 2 == 0 if level == top else ((leaf + 1) // reach) % 4 == 1
    before = (level - 1) * full
    for which, wanted in enumerate((first, jnp.logical_not(first))):
        @pl.when(wanted)
        def _():
            if plan == "rooted":
                piece_ref[...] = pieces[which][0][...]
            elif plan == "traded" and which == 0:
                joined[:, :before] = extra[0][...]
            elif plan == "traded":
                place_pieces(extra[1:1 + rows], joined, 0)
                place_pieces(pieces[0], joined, full)
            elif plan == "plain" and before:
                joined[:, :before] = extra[which][...]
            place_pieces(pieces[which], joined, before)
    if plan == "rooted":
        @pl.when(upper_depth(leaf, top) == 0)
        def _():
            piece_ref[...] = extra[0][...]
    elif plan == "crossed":
        place_pieces([extra[0], late_ref], joined, 0)
    blocks, block_width = lower_ref.shape[1:3]
    highest = joined.shape[1] // block_width - 1
    listed.wait()
    for index in range(blocks):
        number = jnp.clip(numbers[slot, index], 0, highest)
        column = pl.multiple_of(number * block_width, block_width)
        picked[:, index * block_width:(index + 1) * block_width] = joined[:, pl.ds(column, block_width)]
    weights = lower_ref[slot].reshape(blocks * block_width, width)
    offset = jnp.dot(picked[...], weights, preferred_element_type=F32)
    reduced_ref[...] = (right_ref[slot] - offset).astype(BF16)
    if plan == "crossed":
        @pl.when(leaf % 2 == 1)
        def _():
            reduced_ref[...] = extra[1][...]


def apply_inverse(slot, cores, piece_refs, inverse_refs, joined, store):
    quarter = inverse_refs[0].shape[-1]
    place_pieces(piece_refs, joined, 0)
    own = lax.axis_index("rhs")
    for turn, inverse_ref in enumerate(inverse_refs):
        total = jnp.dot(joined[...], inverse_ref[slot], preferred_element_type=F32)
        core = lax.rem(own - turn + cores, cores)
        store(pl.ds(pl.multiple_of(core * quarter, quarter), quarter), total)


def solve_kernel(top, depth, rows, cores, plan, *refs):
    piece_refs = refs[:rows]
    inverse_refs = refs[rows:rows + cores]
    before_ref, held_ref = refs[rows + cores:rows + cores + 2]
    rounded_ref, solved_ref, joined = refs[-3:]
    leaf = lax.axis_index("leaf")
    active = upper_depth(leaf, top) == depth

    def store(columns, total):
        rounded_ref[:, columns] = total.astype(BF16)
        before = before_ref[:, columns] if depth > 0 else jnp.zeros_like(total)
        solved_ref[:, columns] = jnp.where(active, total, before)

    apply_inverse(1, cores, piece_refs, inverse_refs, joined, store)
    if plan == "crossed":
        for wanted, ref in ((leaf % 4 == 1, held_ref), (leaf % 4 == 3, piece_refs[1])):
            @pl.when(wanted)
            def _():
                rounded_ref[...] = ref[...]


def last_kernel(rows, cores, *refs):
    piece_refs = refs[:rows]
    inverse_refs = refs[rows:rows + cores]
    before_ref, out_ref, joined, staged, semaphores = refs[rows + cores:]
    copies = [pltpu.make_async_copy(before_ref, out_ref.at[1], semaphores.at[0])]
    copies[0].start()

    def store(columns, total):
        staged[:, columns] = total
        copy = pltpu.make_async_copy(staged.at[:, columns], out_ref.at[0, :, columns], semaphores.at[len(copies)])
        copy.start()
        copies.append(copy)

    apply_inverse(0, cores, piece_refs, inverse_refs, joined, store)
    for copy in copies:
        copy.wait()


WHOLE = pl.BlockSpec(memory_space=pltpu.VMEM)
FAR = pl.BlockSpec(memory_space=pltpu.HBM)


def call(kernel, near, far, outs, scratch=(), flops=0):
    several = len(outs) > 1
    size = sum(a.size * a.dtype.itemsize for a in [*near, *far])
    near = [pltpu.with_memory_space_constraint(a, pltpu.VMEM) for a in near]
    far = [pltpu.with_memory_space_constraint(a, pltpu.HBM) for a in far]
    specs = [FAR if getattr(o, "memory_space", None) == pltpu.HBM else WHOLE for o in outs]
    return pl.pallas_call(
        kernel,
        in_specs=[WHOLE] * len(near) + [FAR] * len(far),
        out_specs=specs if several else specs[0],
        out_shape=list(outs) if several else outs[0],
        scratch_shapes=list(scratch),
        cost_estimate=pl.CostEstimate(flops=flops, bytes_accessed=size, transcendentals=0),
        compiler_params=pltpu.CompilerParams(vmem_limit_bytes=8 * 2**20),
    )(*near, *far)


def local(right_side, inverse_diag, lower_blocks, block_rows):
    leafs, rows, cores = (lax.axis_size(name) for name in ("leaf", "rows", "rhs"))
    top = leafs.bit_length() - 1
    count, width = right_side.shape[1:]
    full_width = rows * width
    places = ("leaf", "rows")

    def send(value, hops, shift):
        pairs = [(a * rows + r, b * rows + (r + shift) % rows) for a, b in hops for r in range(rows)]
        return lax.ppermute(value, places, pairs)

    def spread(value, hops):
        return [send(value, hops, shift) for shift in range(rows)]

    def rows_of(value):
        arrived = [value]
        for shift in range(1, rows):
            pairs = [(h * rows + r, h * rows + (r + shift) % rows) for h in range(leafs) for r in range(rows)]
            arrived.append(lax.ppermute(value, places, pairs))
        return arrived

    def ring(value, rings, shift=0):
        after = {a: b for stops in rings for a, b in zip(stops, [*stops[1:], stops[0]])}
        pairs = [(h * rows + r, after[h] * rows + (r + shift) % rows if h in after else h * rows + (r + 1) % rows)
                 for h in range(leafs) for r in range(rows)]
        return lax.ppermute(value, places, pairs)

    def core_columns(own):
        turns = range(1, cores)
        return [own] + [lax.ppermute(own, "rhs", [(c, (c + t) % cores) for c in range(cores)]) for t in turns]

    def holders(depth):
        return [(2 * p + 1) * 2 ** (top - depth - 1) - 1 for p in range(2**depth)]

    near = pltpu.VMEM
    half = near((count, width), BF16)
    half_f32 = near((count, width), F32)
    joined = near((count, full_width), BF16)
    work = 2 * count * full_width * width
    semaphores = lambda n: pltpu.SemaphoreType.DMA((n,))

    crossing = top == 3 and rows == 2
    swapped = core_columns(inverse_diag)[1:]

    def load(after, arrays):
        outs = [near(a.shape, a.dtype) for a in arrays]
        return call(functools.partial(load_kernel, len(arrays)), [after], arrays, outs, [semaphores(len(arrays))])

    def paired(lefts, rights):
        return [piece for pair in zip(lefts[::-1], rights[::-1]) for piece in pair]

    reduced = call(cast_kernel, [], [right_side], [half], [near((count, width), F32), pltpu.SemaphoreType.DMA(())])
    gathered = rows_of(reduced)
    inverses = [load(reduced, [inverse_diag]), *swapped]
    plans = ["rooted", "crossed", "traded"] if crossing else ["plain"] * top
    plans = ["plain", *plans]
    older = []
    solved = None
    for depth, plan in enumerate(plans):
        here = holders(min(depth, top - 1))
        if depth > 0:
            all_joined = near((count, depth * full_width), BF16)
            fetched = [pltpu.SMEM(block_rows.shape, jnp.int32), pltpu.SemaphoreType.DMA(()), joined]
            kernel = functools.partial(offset_kernel, top, depth, rows, plan)
            pieces = paired(rights[::-1], lefts[::-1]) if depth == top else paired(lefts, rights)
            if plan == "rooted":
                pieces = [*pieces, rounded]
            elif plan == "crossed":
                pieces = [late, *pieces, relayed, rounded]
            elif plan == "traded":
                rights = rights[::-1]
                pieces = [rights[0], lefts[0], rights[1], lefts[1], mine, relayed, late]
            else:
                pieces = [*pieces, *older]
            arrays = [block_rows, right, lower, *pieces]
            if plan == "rooted":
                reduced, own_root = call(kernel, arrays, [], [half, half], [all_joined, *fetched], work)
            elif depth < top:
                reduced, mine = call(kernel, arrays, [], [half, all_joined], fetched, work)
            else:
                reduced = call(kernel, arrays, [], [half], [all_joined, *fetched], work)
            if plan == "crossed":
                gathered = [reduced, ring(reduced, [(h, h + 2) for h in holders(1)])]
            else:
                gathered = rows_of(reduced)
        if depth == top:
            staged = [near((count, width), F32), semaphores(cores + 1)]
            return call(functools.partial(last_kernel, rows, cores), [*gathered, *inverses, solved], [],
                        [pltpu.HBM(right_side.shape, F32)], [joined, *staged], work)
        older = []
        if depth + 1 < top:
            reach = 2 ** (top - depth - 2)
            ways = [[(h, h - reach) for h in here], [(h, h + reach) for h in here]]
            if plan == "rooted":
                others = [(h, leafs - 1) for h in holders(0)]
                first_side, second_side = ring(own_root, ways[0] + others), ring(own_root, ways[1])
                relayed = call(choose_kernel, [first_side, second_side, own_root], [], [half])
            elif depth > 0:
                older = [send(mine, way, 0) for way in ways]
        else:
            over = [(h, h + 1) for h in here]
            older = [] if crossing else [mine, send(mine, over, 0)]
        kernel = functools.partial(solve_kernel, top, depth, rows, cores, plan)
        arrays = [*gathered, *inverses] + ([solved, rounded] if depth else [])
        rounded, solved = call(kernel, arrays, [], [half, half_f32], [joined], work)
        if crossing and depth == 0:
            (root,) = here
            lefts = [ring(rounded, [(root, root - reach, root - 1)]), send(rounded, ways[0], 1)]
            rights = [ring(rounded, [(root, root + reach, root + 1)]), send(rounded, ways[1], 1)]
        elif depth + 1 < top:
            lefts, rights = [spread(rounded, way) for way in ways]
            if plan == "rooted":
                late = rows_of(relayed)[1]
        elif crossing:
            lefts, rights = rows_of(rounded), [ring(rounded, over, shift) for shift in range(rows)]
        else:
            lefts, rights = rows_of(rounded), spread(rounded, over)
        if depth == 0:
            right, lower = load(rounded, [right_side, lower_blocks])


def solution(mesh):
    return jax.shard_map(
        local,
        mesh=mesh,
        in_specs=(
            P("leaf", "rhs", "rows"),
            P("leaf", None, ("rows", "rhs")),
            P("leaf", None, None, "rows"),
            P("leaf", None),
        ),
        out_specs=P("leaf", "rhs", "rows"),
        check_vma=False,
    )
```

```python
import functools
import jax
import jax.numpy as jnp
from jax import lax
from jax.experimental import pallas as pl
from jax.experimental.pallas import tpu as pltpu
from jax.sharding import PartitionSpec as P

F32 = jnp.float32
BF16 = jnp.bfloat16


def upper_depth(leaf, top):
    return top - 1 - sum(((leaf + 1) % 2**power == 0).astype(jnp.int32) for power in range(1, top + 1))


def cast_kernel(right_ref, cast_ref, staged, semaphore):
    values = pltpu.make_async_copy(right_ref.at[1], staged, semaphore)
    values.start()
    values.wait()
    cast_ref[...] = staged[...].astype(BF16)


def load_kernel(count, after_ref, *refs):
    semaphores = refs[-1]
    copies = [pltpu.make_async_copy(refs[i], refs[count + i], semaphores.at[i]) for i in range(count)]
    for copy in copies:
        copy.start()
    for copy in copies:
        copy.wait()


def choose_kernel(first_ref, second_ref, own_ref, out_ref):
    leaf = lax.axis_index("leaf")
    first = (leaf % 4 == 0) | (leaf == lax.axis_size("leaf") - 1)
    second = leaf % 4 == 2
    for wanted, ref in ((first, first_ref), (second, second_ref), (jnp.logical_not(first | second), own_ref)):
        @pl.when(wanted)
        def _():
            out_ref[...] = ref[...]


def place_pieces(piece_refs, target_ref, start):
    rows = len(piece_refs)
    width = piece_refs[0].shape[1]
    own = lax.axis_index("rows")
    for shift, piece_ref in enumerate(piece_refs):
        source = lax.rem(own - shift + rows, rows)
        target_ref[:, pl.ds(pl.multiple_of(start + source * width, width), width)] = piece_ref[...]


def offset_kernel(top, level, rows, plan, block_rows_ref, right_ref, lower_ref, *refs):
    leaf = lax.axis_index("leaf")
    slot = 0 if level == top else 1
    if plan == "rooted":
        *refs, reduced_ref, piece_ref, joined, numbers, semaphore, picked = refs
    else:
        *refs, reduced_ref, joined, numbers, semaphore, picked = refs
    if plan == "crossed":
        late_ref, *refs = refs
    if level == top:
        pieces = [refs[1:2 * rows:2], refs[:2 * rows:2]]
        if plan == "traded":
            pieces[1] = pieces[1][::-1]
    else:
        pieces = [refs[:2 * rows:2][::-1], refs[1:2 * rows:2][::-1]]
    extra = refs[2 * rows:]
    width = right_ref.shape[2]
    full = rows * width
    listed = pltpu.make_async_copy(block_rows_ref, numbers, semaphore)
    listed.start()
    reach = 2 ** (top - level - 1) if level < top else 1
    first = leaf % 2 == 0 if level == top else ((leaf + 1) // reach) % 4 == 1
    before = (level - 1) * full
    for which, wanted in enumerate((first, jnp.logical_not(first))):
        @pl.when(wanted)
        def _():
            if plan == "rooted":
                piece_ref[...] = pieces[which][0][...]
            elif plan == "traded" and which == 0:
                joined[:, :before] = extra[0][...]
            elif plan == "traded":
                place_pieces(extra[1:1 + rows], joined, 0)
                place_pieces(pieces[0], joined, full)
            elif plan == "plain" and before:
                joined[:, :before] = extra[which][...]
            place_pieces(pieces[which], joined, before)
    if plan == "rooted":
        @pl.when(upper_depth(leaf, top) == 0)
        def _():
            piece_ref[...] = extra[0][...]
    elif plan == "crossed":
        place_pieces([extra[0], late_ref], joined, 0)
    blocks, block_width = lower_ref.shape[1:3]
    highest = joined.shape[1] // block_width - 1
    listed.wait()
    for index in range(blocks):
        number = jnp.clip(numbers[slot, index], 0, highest)
        column = pl.multiple_of(number * block_width, block_width)
        picked[:, index * block_width:(index + 1) * block_width] = joined[:, pl.ds(column, block_width)]
    weights = lower_ref[slot].reshape(blocks * block_width, width)
    offset = jnp.dot(picked[...], weights, preferred_element_type=F32)
    reduced_ref[...] = (right_ref[slot] - offset).astype(BF16)
    if plan == "crossed":
        @pl.when(leaf % 2 == 1)
        def _():
            reduced_ref[...] = extra[1][...]


def apply_inverse(slot, cores, piece_refs, inverse_refs, joined, store):
    quarter = inverse_refs[0].shape[-1]
    place_pieces(piece_refs, joined, 0)
    own = lax.axis_index("rhs")
    for turn, inverse_ref in enumerate(inverse_refs):
        total = jnp.dot(joined[...], inverse_ref[slot], preferred_element_type=F32)
        core = lax.rem(own - turn + cores, cores)
        store(pl.ds(pl.multiple_of(core * quarter, quarter), quarter), total)


def solve_kernel(top, depth, rows, cores, plan, *refs):
    piece_refs = refs[:rows]
    inverse_refs = refs[rows:rows + cores]
    before_ref, held_ref = refs[rows + cores:rows + cores + 2]
    rounded_ref, solved_ref, joined = refs[-3:]
    leaf = lax.axis_index("leaf")
    active = upper_depth(leaf, top) == depth

    def store(columns, total):
        rounded_ref[:, columns] = total.astype(BF16)
        before = before_ref[:, columns] if depth > 0 else jnp.zeros_like(total)
        solved_ref[:, columns] = jnp.where(active, total, before)

    apply_inverse(1, cores, piece_refs, inverse_refs, joined, store)
    if plan == "crossed":
        for wanted, ref in ((leaf % 4 == 1, held_ref), (leaf % 4 == 3, piece_refs[1])):
            @pl.when(wanted)
            def _():
                rounded_ref[...] = ref[...]


def last_kernel(rows, cores, *refs):
    piece_refs = refs[:rows]
    inverse_refs = refs[rows:rows + cores]
    before_ref, out_ref, joined, staged, semaphores = refs[rows + cores:]
    copies = [pltpu.make_async_copy(before_ref, out_ref.at[1], semaphores.at[0])]
    copies[0].start()

    def store(columns, total):
        staged[:, columns] = total
        copy = pltpu.make_async_copy(staged.at[:, columns], out_ref.at[0, :, columns], semaphores.at[len(copies)])
        copy.start()
        copies.append(copy)

    apply_inverse(0, cores, piece_refs, inverse_refs, joined, store)
    for copy in copies:
        copy.wait()


WHOLE = pl.BlockSpec(memory_space=pltpu.VMEM)
FAR = pl.BlockSpec(memory_space=pltpu.HBM)


def call(kernel, near, far, outs, scratch=(), flops=0):
    several = len(outs) > 1
    size = sum(a.size * a.dtype.itemsize for a in [*near, *far])
    near = [pltpu.with_memory_space_constraint(a, pltpu.VMEM) for a in near]
    far = [pltpu.with_memory_space_constraint(a, pltpu.HBM) for a in far]
    specs = [FAR if getattr(o, "memory_space", None) == pltpu.HBM else WHOLE for o in outs]
    return pl.pallas_call(
        kernel,
        in_specs=[WHOLE] * len(near) + [FAR] * len(far),
        out_specs=specs if several else specs[0],
        out_shape=list(outs) if several else outs[0],
        scratch_shapes=list(scratch),
        cost_estimate=pl.CostEstimate(flops=flops, bytes_accessed=size, transcendentals=0),
        compiler_params=pltpu.CompilerParams(vmem_limit_bytes=8 * 2**20),
    )(*near, *far)


def local(right_side, inverse_diag, lower_blocks, block_rows):
    leafs, rows, cores = (lax.axis_size(name) for name in ("leaf", "rows", "rhs"))
    top = leafs.bit_length() - 1
    count, width = right_side.shape[1:]
    full_width = rows * width
    places = ("leaf", "rows")

    def send(value, hops, shift):
        pairs = [(a * rows + r, b * rows + (r + shift) % rows) for a, b in hops for r in range(rows)]
        return lax.ppermute(value, places, pairs)

    def spread(value, hops):
        return [send(value, hops, shift) for shift in range(rows)]

    def permute(value, target):
        pairs = []
        for place in range(leafs * rows):
            goal = target(*divmod(place, rows))
            for core in range(cores):
                if goal is None:
                    pairs.append((place * cores + core, place * cores + (core + 1) % cores))
                else:
                    pairs.append((place * cores + core, (goal[0] * rows + goal[1]) * cores + core))
        return lax.ppermute(value, ("leaf", "rows", "rhs"), pairs)

    def rows_of(value, traders=None):
        traders = range(leafs) if traders is None else traders
        return [value] + [permute(value, lambda h, r: (h, (r + shift) % rows) if h in traders else None)
                          for shift in range(1, rows)]

    def ring(value, rings, shift=0, traders=()):
        after = {a: b for stops in rings for a, b in zip(stops, [*stops[1:], stops[0]])}

        def target(h, r):
            if h in after:
                return after[h], (r + shift) % rows
            return (h, (r + 1) % rows) if h in traders else None

        return permute(value, target)

    def core_columns(own):
        turns = range(1, cores)
        return [own] + [lax.ppermute(own, "rhs", [(c, (c + t) % cores) for c in range(cores)]) for t in turns]

    def holders(depth):
        return [(2 * p + 1) * 2 ** (top - depth - 1) - 1 for p in range(2**depth)]

    near = pltpu.VMEM
    half = near((count, width), BF16)
    half_f32 = near((count, width), F32)
    joined = near((count, full_width), BF16)
    work = 2 * count * full_width * width
    semaphores = lambda n: pltpu.SemaphoreType.DMA((n,))

    crossing = top == 3 and rows == 2
    swapped = core_columns(inverse_diag)[1:]

    def load(after, arrays):
        outs = [near(a.shape, a.dtype) for a in arrays]
        return call(functools.partial(load_kernel, len(arrays)), [after], arrays, outs, [semaphores(len(arrays))])

    def paired(lefts, rights):
        return [piece for pair in zip(lefts[::-1], rights[::-1]) for piece in pair]

    reduced = call(cast_kernel, [], [right_side], [half], [near((count, width), F32), pltpu.SemaphoreType.DMA(())])
    gathered = rows_of(reduced, holders(0))
    inverses = [load(reduced, [inverse_diag]), *swapped]
    plans = ["rooted", "crossed", "traded"] if crossing else ["plain"] * top
    plans = ["plain", *plans]
    older = []
    solved = None
    for depth, plan in enumerate(plans):
        here = holders(min(depth, top - 1))
        if depth > 0:
            all_joined = near((count, depth * full_width), BF16)
            fetched = [pltpu.SMEM(block_rows.shape, jnp.int32), pltpu.SemaphoreType.DMA(()), joined]
            kernel = functools.partial(offset_kernel, top, depth, rows, plan)
            pieces = paired(rights[::-1], lefts[::-1]) if depth == top else paired(lefts, rights)
            if plan == "rooted":
                pieces = [*pieces, rounded]
            elif plan == "crossed":
                pieces = [late, *pieces, relayed, rounded]
            elif plan == "traded":
                rights = rights[::-1]
                pieces = [rights[0], lefts[0], rights[1], lefts[1], mine, relayed, late]
            else:
                pieces = [*pieces, *older]
            arrays = [block_rows, right, lower, *pieces]
            if plan == "rooted":
                reduced, own_root = call(kernel, arrays, [], [half, half], [all_joined, *fetched], work)
            elif depth < top:
                reduced, mine = call(kernel, arrays, [], [half, all_joined], fetched, work)
            else:
                reduced = call(kernel, arrays, [], [half], [all_joined, *fetched], work)
            if plan == "crossed":
                gathered = [reduced, ring(reduced, [(h, h + 2) for h in holders(1)], 0, here)]
            else:
                gathered = rows_of(reduced, here if depth < top else None)
        if depth == top:
            staged = [near((count, width), F32), semaphores(cores + 1)]
            return call(functools.partial(last_kernel, rows, cores), [*gathered, *inverses, solved], [],
                        [pltpu.HBM(right_side.shape, F32)], [joined, *staged], work)
        older = []
        if depth + 1 < top:
            reach = 2 ** (top - depth - 2)
            ways = [[(h, h - reach) for h in here], [(h, h + reach) for h in here]]
            if plan == "rooted":
                others = [(h, leafs - 1) for h in holders(0)]
                first_side, second_side = ring(own_root, ways[0] + others), ring(own_root, ways[1])
                relayed = call(choose_kernel, [first_side, second_side, own_root], [], [half])
            elif depth > 0:
                older = [send(mine, way, 0) for way in ways]
        else:
            over = [(h, h + 1) for h in here]
            older = [] if crossing else [mine, send(mine, over, 0)]
        kernel = functools.partial(solve_kernel, top, depth, rows, cores, plan)
        arrays = [*gathered, *inverses] + ([solved, rounded] if depth else [])
        rounded, solved = call(kernel, arrays, [], [half, half_f32], [joined], work)
        if crossing and depth == 0:
            (root,) = here
            lefts = [ring(rounded, [(root, root - reach, root - 1)]), ring(rounded, ways[0], 1)]
            rights = [ring(rounded, [(root, root + reach, root + 1)]), ring(rounded, ways[1], 1)]
        elif depth + 1 < top:
            lefts, rights = [spread(rounded, way) for way in ways]
            if plan == "rooted":
                late = rows_of(relayed)[1]
        elif crossing:
            lefts, rights = rows_of(rounded), [ring(rounded, over, shift) for shift in range(rows)]
        else:
            lefts, rights = rows_of(rounded), spread(rounded, over)
        if depth == 0:
            right, lower = load(rounded, [right_side, lower_blocks])


def solution(mesh):
    return jax.shard_map(
        local,
        mesh=mesh,
        in_specs=(
            P("leaf", "rhs", "rows"),
            P("leaf", None, ("rows", "rhs")),
            P("leaf", None, None, "rows"),
            P("leaf", None),
        ),
        out_specs=P("leaf", "rhs", "rows"),
        check_vma=False,
    )
```

```python
import functools
import jax
import jax.numpy as jnp
from jax import lax
from jax.experimental import pallas as pl
from jax.experimental.pallas import tpu as pltpu
from jax.sharding import PartitionSpec as P

F32 = jnp.float32
BF16 = jnp.bfloat16


def upper_depth(leaf, top):
    return top - 1 - sum(((leaf + 1) % 2**power == 0).astype(jnp.int32) for power in range(1, top + 1))


def cast_kernel(right_ref, cast_ref, staged, semaphore):
    values = pltpu.make_async_copy(right_ref.at[1], staged, semaphore)
    values.start()
    values.wait()
    cast_ref[...] = staged[...].astype(BF16)


def load_kernel(count, after_ref, *refs):
    semaphores = refs[-1]
    copies = [pltpu.make_async_copy(refs[i], refs[count + i], semaphores.at[i]) for i in range(count)]
    for copy in copies:
        copy.start()
    for copy in copies:
        copy.wait()


def choose_kernel(first_ref, second_ref, own_ref, out_ref):
    leaf = lax.axis_index("leaf")
    first = (leaf % 4 == 0) | (leaf == lax.axis_size("leaf") - 1)
    second = leaf % 4 == 2
    for wanted, ref in ((first, first_ref), (second, second_ref), (jnp.logical_not(first | second), own_ref)):
        @pl.when(wanted)
        def _():
            out_ref[...] = ref[...]


def place_pieces(piece_refs, target_ref, start):
    rows = len(piece_refs)
    width = piece_refs[0].shape[1]
    own = lax.axis_index("rows")
    for shift, piece_ref in enumerate(piece_refs):
        source = lax.rem(own - shift + rows, rows)
        target_ref[:, pl.ds(pl.multiple_of(start + source * width, width), width)] = piece_ref[...]


def offset_kernel(top, level, rows, plan, block_rows_ref, right_ref, lower_ref, *refs):
    leaf = lax.axis_index("leaf")
    slot = 0 if level == top else 1
    if plan == "rooted":
        *refs, reduced_ref, piece_ref, joined, picked = refs
    else:
        *refs, reduced_ref, joined, picked = refs
    if plan == "crossed":
        late_ref, *refs = refs
    if level == top:
        pieces = [refs[1:2 * rows:2], refs[:2 * rows:2]]
        if plan == "traded":
            pieces[1] = pieces[1][::-1]
    else:
        pieces = [refs[:2 * rows:2][::-1], refs[1:2 * rows:2][::-1]]
    extra = refs[2 * rows:]
    width = right_ref.shape[2]
    full = rows * width
    reach = 2 ** (top - level - 1) if level < top else 1
    first = leaf % 2 == 0 if level == top else ((leaf + 1) // reach) % 4 == 1
    before = (level - 1) * full
    for which, wanted in enumerate((first, jnp.logical_not(first))):
        @pl.when(wanted)
        def _():
            if plan == "rooted":
                piece_ref[...] = pieces[which][0][...]
            elif plan == "traded" and which == 0:
                joined[:, :before] = extra[0][...]
            elif plan == "traded":
                place_pieces(extra[1:1 + rows], joined, 0)
                place_pieces(pieces[0], joined, full)
            elif plan == "plain" and before:
                joined[:, :before] = extra[which][...]
            place_pieces(pieces[which], joined, before)
    if plan == "rooted":
        @pl.when(upper_depth(leaf, top) == 0)
        def _():
            piece_ref[...] = extra[0][...]
    elif plan == "crossed":
        place_pieces([extra[0], late_ref], joined, 0)
    blocks, block_width = lower_ref.shape[1:3]
    highest = joined.shape[1] // block_width - 1
    numbers = block_rows_ref[...]
    for index in range(blocks):
        number = jnp.clip(numbers[slot, index], 0, highest)
        column = pl.multiple_of(number * block_width, block_width)
        picked[:, index * block_width:(index + 1) * block_width] = joined[:, pl.ds(column, block_width)]
    weights = lower_ref[slot].reshape(blocks * block_width, width)
    offset = jnp.dot(picked[...], weights, preferred_element_type=F32)
    reduced_ref[...] = (right_ref[slot] - offset).astype(BF16)
    if plan == "crossed":
        @pl.when(leaf % 2 == 1)
        def _():
            reduced_ref[...] = extra[1][...]


def begin_kernel(slot, rows, cores, piece_ref, *refs):
    inverse_refs, part_ref = refs[:cores], refs[cores]
    width = piece_ref.shape[1]
    quarter = inverse_refs[0].shape[-1]
    own = lax.axis_index("rows")
    for which in range(rows):
        @pl.when(own == which)
        def _():
            for turn, inverse_ref in enumerate(inverse_refs):
                weights = inverse_ref[slot, which * width:(which + 1) * width, :]
                part_ref[:, turn * quarter:(turn + 1) * quarter] = jnp.dot(
                    piece_ref[...], weights, preferred_element_type=F32)


def apply_inverse(slot, cores, piece_refs, inverse_refs, part_ref, joined, store, turns=None):
    rows = len(piece_refs)
    width = piece_refs[0].shape[1]
    quarter = inverse_refs[0].shape[-1]
    own = lax.axis_index("rows")
    if part_ref is None and turns in (None, [0]):
        place_pieces(piece_refs, joined, 0)
    for turn in range(cores) if turns is None else turns:
        inverse_ref = inverse_refs[turn]
        core = lax.rem(lax.axis_index("rhs") - turn + cores, cores)
        columns = pl.ds(pl.multiple_of(core * quarter, quarter), quarter)
        if part_ref is None:
            store(columns, jnp.dot(joined[...], inverse_ref[slot], preferred_element_type=F32))
            continue
        for which in range(rows):
            @pl.when(own == which)
            def _():
                total = part_ref[:, turn * quarter:(turn + 1) * quarter]
                for shift in range(1, rows):
                    source = (which - shift) % rows
                    weights = inverse_ref[slot, source * width:(source + 1) * width, :]
                    total = total + jnp.dot(piece_refs[shift][...], weights, preferred_element_type=F32)
                store(columns, total)


def solve_kernel(top, depth, rows, cores, plan, split, *refs):
    piece_refs = refs[:rows]
    inverse_refs = refs[rows:rows + cores]
    before_ref, held_ref, part_ref = refs[rows + cores:rows + cores + 3]
    part_ref = part_ref if split else None
    rounded_ref, solved_ref, joined = refs[-3:]
    leaf = lax.axis_index("leaf")
    active = upper_depth(leaf, top) == depth

    def store(columns, total):
        rounded_ref[:, columns] = total.astype(BF16)
        before = before_ref[:, columns] if depth > 0 else jnp.zeros_like(total)
        solved_ref[:, columns] = jnp.where(active, total, before)

    apply_inverse(1, cores, piece_refs, inverse_refs, part_ref, joined, store)
    if plan == "crossed":
        for wanted, ref in ((leaf % 4 == 1, held_ref), (leaf % 4 == 3, piece_refs[1])):
            @pl.when(wanted)
            def _():
                rounded_ref[...] = ref[...]


def last_kernel(rows, cores, split, *refs):
    piece_refs = refs[:rows]
    inverse_refs = refs[rows:rows + cores]
    before_ref, *part, out_ref, joined, staged, semaphores = refs[rows + cores:]
    part_ref = part[0] if split else None
    copies = [pltpu.make_async_copy(before_ref, out_ref.at[1], semaphores.at[0])]
    copies[0].start()

    quarter = inverse_refs[0].shape[-1]

    def store(columns, total):
        staged[:, columns] = total

    for turn in range(cores):
        core = lax.rem(lax.axis_index("rhs") - turn + cores, cores)
        columns = pl.ds(pl.multiple_of(core * quarter, quarter), quarter)
        apply_inverse(0, cores, piece_refs, inverse_refs, part_ref, joined, store, [turn])
        copies.append(pltpu.make_async_copy(
            staged.at[:, columns], out_ref.at[0, :, columns], semaphores.at[turn + 1]))
        copies[-1].start()
    for copy in copies:
        copy.wait()


WHOLE = pl.BlockSpec(memory_space=pltpu.VMEM)
FAR = pl.BlockSpec(memory_space=pltpu.HBM)


def call(kernel, near, far, outs, scratch=(), flops=0):
    several = len(outs) > 1
    size = sum(a.size * a.dtype.itemsize for a in [*near, *far])
    near = [pltpu.with_memory_space_constraint(a, pltpu.VMEM) for a in near]
    far = [pltpu.with_memory_space_constraint(a, pltpu.HBM) for a in far]
    specs = [FAR if getattr(o, "memory_space", None) == pltpu.HBM else WHOLE for o in outs]
    return pl.pallas_call(
        kernel,
        in_specs=[WHOLE] * len(near) + [FAR] * len(far),
        out_specs=specs if several else specs[0],
        out_shape=list(outs) if several else outs[0],
        scratch_shapes=list(scratch),
        cost_estimate=pl.CostEstimate(flops=flops, bytes_accessed=size, transcendentals=0),
        compiler_params=pltpu.CompilerParams(vmem_limit_bytes=8 * 2**20),
    )(*near, *far)


def local(right_side, inverse_diag, lower_blocks, block_rows):
    leafs, rows, cores = (lax.axis_size(name) for name in ("leaf", "rows", "rhs"))
    top = leafs.bit_length() - 1
    count, width = right_side.shape[1:]
    full_width = rows * width
    places = ("leaf", "rows")

    def send(value, hops, shift):
        pairs = [(a * rows + r, b * rows + (r + shift) % rows) for a, b in hops for r in range(rows)]
        return lax.ppermute(value, places, pairs)

    def spread(value, hops):
        return [send(value, hops, shift) for shift in range(rows)]

    def permute(value, target):
        pairs = []
        for place in range(leafs * rows):
            goal = target(*divmod(place, rows))
            for core in range(cores):
                if goal is None:
                    pairs.append((place * cores + core, place * cores + (core + 1) % cores))
                else:
                    pairs.append((place * cores + core, (goal[0] * rows + goal[1]) * cores + core))
        return lax.ppermute(value, ("leaf", "rows", "rhs"), pairs)

    def rows_of(value, traders=None):
        traders = range(leafs) if traders is None else traders
        return [value] + [permute(value, lambda h, r: (h, (r + shift) % rows) if h in traders else None)
                          for shift in range(1, rows)]

    def ring(value, rings, shift=0, traders=()):
        after = {a: b for stops in rings for a, b in zip(stops, [*stops[1:], stops[0]])}

        def target(h, r):
            if h in after:
                return after[h], (r + shift) % rows
            return (h, (r + 1) % rows) if h in traders else None

        return permute(value, target)

    def core_columns(own):
        turns = range(1, cores)
        return [own] + [lax.ppermute(own, "rhs", [(c, (c + t) % cores) for c in range(cores)]) for t in turns]

    def holders(depth):
        return [(2 * p + 1) * 2 ** (top - depth - 1) - 1 for p in range(2**depth)]

    near = pltpu.VMEM
    half = near((count, width), BF16)
    half_f32 = near((count, width), F32)
    joined = near((count, full_width), BF16)
    work = 2 * count * full_width * width
    semaphores = lambda n: pltpu.SemaphoreType.DMA((n,))

    crossing = top == 3 and rows == 2
    swapped = core_columns(inverse_diag)[1:]

    def load(after, arrays):
        outs = [near(a.shape, a.dtype) for a in arrays]
        return call(functools.partial(load_kernel, len(arrays)), [after], arrays, outs, [semaphores(len(arrays))])

    def paired(lefts, rights):
        return [piece for pair in zip(lefts[::-1], rights[::-1]) for piece in pair]

    reduced = call(cast_kernel, [], [right_side], [half], [near((count, width), F32), pltpu.SemaphoreType.DMA(())])
    gathered = rows_of(reduced, holders(0))
    inverses = [load(reduced, [inverse_diag]), *swapped]
    plans = ["rooted", "crossed", "traded"] if crossing else ["plain"] * top
    plans = ["plain", *plans]
    older = []
    solved = None
    for depth, plan in enumerate(plans):
        here = holders(min(depth, top - 1))
        if depth > 0:
            all_joined = near((count, depth * full_width), BF16)
            kernel = functools.partial(offset_kernel, top, depth, rows, plan)
            pieces = paired(rights[::-1], lefts[::-1]) if depth == top else paired(lefts, rights)
            if plan == "rooted":
                pieces = [*pieces, rounded]
            elif plan == "crossed":
                pieces = [late, *pieces, relayed, rounded]
            elif plan == "traded":
                rights = rights[::-1]
                pieces = [rights[0], lefts[0], rights[1], lefts[1], mine, relayed, late]
            else:
                pieces = [*pieces, *older]
            arrays = [block_rows, right, lower, *pieces]
            if plan == "rooted":
                reduced, own_root = call(kernel, arrays, [], [half, half], [all_joined, joined], work)
            elif depth < top:
                reduced, mine = call(kernel, arrays, [], [half, all_joined], [joined], work)
            else:
                reduced = call(kernel, arrays, [], [half], [all_joined, joined], work)
            if plan == "crossed":
                gathered = [reduced, ring(reduced, [(h, h + 2) for h in holders(1)], 0, here)]
            else:
                gathered = rows_of(reduced, here if depth < top else None)
        split = crossing and depth > 1
        part = []
        if split:
            kernel = functools.partial(begin_kernel, 0 if depth == top else 1, rows, cores)
            part = [call(kernel, [reduced, *inverses], [], [half_f32], (), work // rows)]
        if depth == top:
            staged = [near((count, width), F32), semaphores(cores + 1)]
            return call(functools.partial(last_kernel, rows, cores, split), [*gathered, *inverses, solved, *part], [],
                        [pltpu.HBM(right_side.shape, F32)], [joined, *staged], work)
        older = []
        if depth + 1 < top:
            reach = 2 ** (top - depth - 2)
            ways = [[(h, h - reach) for h in here], [(h, h + reach) for h in here]]
            if plan == "rooted":
                others = [(h, leafs - 1) for h in holders(0)]
                first_side, second_side = ring(own_root, ways[0] + others), ring(own_root, ways[1])
                relayed = call(choose_kernel, [first_side, second_side, own_root], [], [half])
            elif depth > 0:
                older = [send(mine, way, 0) for way in ways]
        else:
            over = [(h, h + 1) for h in here]
            older = [] if crossing else [mine, send(mine, over, 0)]
        kernel = functools.partial(solve_kernel, top, depth, rows, cores, plan, split)
        arrays = [*gathered, *inverses] + ([solved, rounded, *part] if depth else [])
        rounded, solved = call(kernel, arrays, [], [half, half_f32], [joined], work)
        if crossing and depth == 0:
            (root,) = here
            lefts = [ring(rounded, [(root, root - reach, root - 1)]), ring(rounded, ways[0], 1)]
            rights = [ring(rounded, [(root, root + reach, root + 1)]), ring(rounded, ways[1], 1)]
        elif depth + 1 < top:
            lefts, rights = [spread(rounded, way) for way in ways]
            if plan == "rooted":
                late = rows_of(relayed)[1]
        elif crossing:
            lefts, rights = rows_of(rounded), [ring(rounded, over, shift) for shift in range(rows)]
        else:
            lefts, rights = rows_of(rounded), spread(rounded, over)
        if depth == 0:
            right, lower = load(rounded, [right_side, lower_blocks])


def solution(mesh):
    return jax.shard_map(
        local,
        mesh=mesh,
        in_specs=(
            P("leaf", "rhs", "rows"),
            P("leaf", None, ("rows", "rhs")),
            P("leaf", None, None, "rows"),
            P("leaf", None),
        ),
        out_specs=P("leaf", "rhs", "rows"),
        check_vma=False,
    )
```

```python
import functools
import jax
import jax.numpy as jnp
from jax import lax
from jax.experimental import pallas as pl
from jax.experimental.pallas import tpu as pltpu
from jax.sharding import PartitionSpec as P

F32 = jnp.float32
BF16 = jnp.bfloat16


def upper_depth(leaf, top):
    return top - 1 - sum(((leaf + 1) % 2**power == 0).astype(jnp.int32) for power in range(1, top + 1))


def cast_kernel(right_ref, cast_ref, staged, semaphore):
    values = pltpu.make_async_copy(right_ref.at[1], staged, semaphore)
    values.start()
    values.wait()
    cast_ref[...] = staged[...].astype(BF16)


def load_kernel(count, after_ref, *refs):
    semaphores = refs[-1]
    copies = [pltpu.make_async_copy(refs[i], refs[count + i], semaphores.at[i]) for i in range(count)]
    for copy in copies:
        copy.start()
    for copy in copies:
        copy.wait()


def choose_kernel(first_ref, second_ref, own_ref, out_ref):
    leaf = lax.axis_index("leaf")
    first = (leaf % 4 == 0) | (leaf == lax.axis_size("leaf") - 1)
    second = leaf % 4 == 2
    for wanted, ref in ((first, first_ref), (second, second_ref), (jnp.logical_not(first | second), own_ref)):
        @pl.when(wanted)
        def _():
            out_ref[...] = ref[...]


def place_pieces(piece_refs, target_ref, start):
    rows = len(piece_refs)
    width = piece_refs[0].shape[1]
    own = lax.axis_index("rows")
    for shift, piece_ref in enumerate(piece_refs):
        source = lax.rem(own - shift + rows, rows)
        target_ref[:, pl.ds(pl.multiple_of(start + source * width, width), width)] = piece_ref[...]


def offset_kernel(top, level, rows, plan, block_rows_ref, right_ref, lower_ref, *refs):
    leaf = lax.axis_index("leaf")
    slot = 0 if level == top else 1
    if plan == "rooted":
        *refs, reduced_ref, piece_ref, joined, picked = refs
    else:
        *refs, reduced_ref, joined, picked = refs
    if plan == "crossed":
        late_ref, *refs = refs
    if level == top:
        pieces = [refs[1:2 * rows:2], refs[:2 * rows:2]]
        if plan == "traded":
            r0, l0, l1, r1 = refs[:4]
            pieces = [[l0, l1], [r0, r1]]
    elif plan == "rooted":
        r1, r0, l1, l0 = refs[:4]
        pieces = [[l0, l1], [r0, r1]]
    elif plan == "crossed":
        r1, r0, l1, l0 = refs[:4]
        pieces = [[l0, l1], [r0, r1]]
    else:
        pieces = [refs[:2 * rows:2][::-1], refs[1:2 * rows:2][::-1]]
    extra = refs[2 * rows:]
    width = right_ref.shape[2]
    full = rows * width
    reach = 2 ** (top - level - 1) if level < top else 1
    first = leaf % 2 == 0 if level == top else ((leaf + 1) // reach) % 4 == 1
    before = (level - 1) * full
    for which, wanted in enumerate((first, jnp.logical_not(first))):
        @pl.when(wanted)
        def _():
            if plan == "rooted":
                piece_ref[...] = pieces[which][0][...]
            elif plan == "traded" and which == 0:
                joined[:, :before] = extra[0][...]
            elif plan == "traded":
                place_pieces(extra[1:1 + rows], joined, 0)
                place_pieces(pieces[0], joined, full)
            elif plan == "plain" and before:
                joined[:, :before] = extra[which][...]
            place_pieces(pieces[which], joined, before)
    if plan == "rooted":
        @pl.when(upper_depth(leaf, top) == 0)
        def _():
            piece_ref[...] = extra[0][...]
    elif plan == "crossed":
        place_pieces([extra[0], late_ref], joined, 0)
    blocks, block_width = lower_ref.shape[1:3]
    highest = joined.shape[1] // block_width - 1
    numbers = block_rows_ref[...]
    for index in range(blocks):
        number = jnp.clip(numbers[slot, index], 0, highest)
        column = pl.multiple_of(number * block_width, block_width)
        picked[:, index * block_width:(index + 1) * block_width] = joined[:, pl.ds(column, block_width)]
    weights = lower_ref[slot].reshape(blocks * block_width, width)
    offset = jnp.dot(picked[...], weights, preferred_element_type=F32)
    reduced_ref[...] = (right_ref[slot] - offset).astype(BF16)
    if plan == "crossed":
        @pl.when(leaf % 2 == 1)
        def _():
            reduced_ref[...] = extra[1][...]


def begin_kernel(slot, rows, cores, piece_ref, *refs):
    inverse_refs, part_ref = refs[:cores], refs[cores]
    width = piece_ref.shape[1]
    quarter = inverse_refs[0].shape[-1]
    own = lax.axis_index("rows")
    for which in range(rows):
        @pl.when(own == which)
        def _():
            for turn, inverse_ref in enumerate(inverse_refs):
                weights = inverse_ref[slot, which * width:(which + 1) * width, :]
                part_ref[:, turn * quarter:(turn + 1) * quarter] = jnp.dot(
                    piece_ref[...], weights, preferred_element_type=F32)


def apply_inverse(slot, cores, piece_refs, inverse_refs, part_ref, joined, store, turns=None):
    rows = len(piece_refs)
    width = piece_refs[0].shape[1]
    quarter = inverse_refs[0].shape[-1]
    own = lax.axis_index("rows")
    if part_ref is None and turns in (None, [0]):
        place_pieces(piece_refs, joined, 0)
    for turn in range(cores) if turns is None else turns:
        inverse_ref = inverse_refs[turn]
        core = lax.rem(lax.axis_index("rhs") - turn + cores, cores)
        columns = pl.ds(pl.multiple_of(core * quarter, quarter), quarter)
        if part_ref is None:
            store(columns, jnp.dot(joined[...], inverse_ref[slot], preferred_element_type=F32))
            continue
        for which in range(rows):
            @pl.when(own == which)
            def _():
                total = part_ref[:, turn * quarter:(turn + 1) * quarter]
                for shift in range(1, rows):
                    source = (which - shift) % rows
                    weights = inverse_ref[slot, source * width:(source + 1) * width, :]
                    total = total + jnp.dot(piece_refs[shift][...], weights, preferred_element_type=F32)
                store(columns, total)


def solve_kernel(top, depth, rows, cores, plan, split, *refs):
    piece_refs = refs[:rows]
    inverse_refs = refs[rows:rows + cores]
    before_ref, held_ref, part_ref = refs[rows + cores:rows + cores + 3]
    part_ref = part_ref if split else None
    rounded_ref, solved_ref, joined = refs[-3:]
    leaf = lax.axis_index("leaf")
    active = upper_depth(leaf, top) == depth

    def store(columns, total):
        rounded_ref[:, columns] = total.astype(BF16)
        before = before_ref[:, columns] if depth > 0 else jnp.zeros_like(total)
        solved_ref[:, columns] = jnp.where(active, total, before)

    apply_inverse(1, cores, piece_refs, inverse_refs, part_ref, joined, store)
    if plan == "crossed":
        for wanted, ref in ((leaf % 4 == 1, held_ref), (leaf % 4 == 3, piece_refs[1])):
            @pl.when(wanted)
            def _():
                rounded_ref[...] = ref[...]


def last_kernel(rows, cores, split, *refs):
    piece_refs = refs[:rows]
    inverse_refs = refs[rows:rows + cores]
    before_ref, *part, out_ref, joined, staged, semaphores = refs[rows + cores:]
    part_ref = part[0] if split else None
    copies = [pltpu.make_async_copy(before_ref, out_ref.at[1], semaphores.at[0])]
    copies[0].start()

    quarter = inverse_refs[0].shape[-1]

    def store(columns, total):
        staged[:, columns] = total

    for turn in range(cores):
        core = lax.rem(lax.axis_index("rhs") - turn + cores, cores)
        columns = pl.ds(pl.multiple_of(core * quarter, quarter), quarter)
        apply_inverse(0, cores, piece_refs, inverse_refs, part_ref, joined, store, [turn])
        copies.append(pltpu.make_async_copy(
            staged.at[:, columns], out_ref.at[0, :, columns], semaphores.at[turn + 1]))
        copies[-1].start()
    for copy in copies:
        copy.wait()


WHOLE = pl.BlockSpec(memory_space=pltpu.VMEM)
FAR = pl.BlockSpec(memory_space=pltpu.HBM)


def call(kernel, near, far, outs, scratch=(), flops=0):
    several = len(outs) > 1
    size = sum(a.size * a.dtype.itemsize for a in [*near, *far])
    near = [pltpu.with_memory_space_constraint(a, pltpu.VMEM) for a in near]
    far = [pltpu.with_memory_space_constraint(a, pltpu.HBM) for a in far]
    specs = [FAR if getattr(o, "memory_space", None) == pltpu.HBM else WHOLE for o in outs]
    return pl.pallas_call(
        kernel,
        in_specs=[WHOLE] * len(near) + [FAR] * len(far),
        out_specs=specs if several else specs[0],
        out_shape=list(outs) if several else outs[0],
        scratch_shapes=list(scratch),
        cost_estimate=pl.CostEstimate(flops=flops, bytes_accessed=size, transcendentals=0),
        compiler_params=pltpu.CompilerParams(vmem_limit_bytes=8 * 2**20),
    )(*near, *far)


def local(right_side, inverse_diag, lower_blocks, block_rows):
    leafs, rows, cores = (lax.axis_size(name) for name in ("leaf", "rows", "rhs"))
    top = leafs.bit_length() - 1
    count, width = right_side.shape[1:]
    full_width = rows * width
    places = ("leaf", "rows")

    def send(value, hops, shift):
        pairs = [(a * rows + r, b * rows + (r + shift) % rows) for a, b in hops for r in range(rows)]
        return lax.ppermute(value, places, pairs)

    def spread(value, hops):
        return [send(value, hops, shift) for shift in range(rows)]

    def permute(value, target):
        pairs = []
        for place in range(leafs * rows):
            goal = target(*divmod(place, rows))
            for core in range(cores):
                if goal is None:
                    pairs.append((place * cores + core, place * cores + (core + 1) % cores))
                else:
                    pairs.append((place * cores + core, (goal[0] * rows + goal[1]) * cores + core))
        return lax.ppermute(value, ("leaf", "rows", "rhs"), pairs)

    def rows_of(value, traders=None):
        traders = range(leafs) if traders is None else traders
        return [value] + [permute(value, lambda h, r: (h, (r + shift) % rows) if h in traders else None)
                          for shift in range(1, rows)]

    def ring(value, rings, shift=0, traders=()):
        after = {a: b for stops in rings for a, b in zip(stops, [*stops[1:], stops[0]])}

        def target(h, r):
            if h in after:
                return after[h], (r + shift) % rows
            return (h, (r + 1) % rows) if h in traders else None

        return permute(value, target)

    def core_columns(own):
        turns = range(1, cores)
        return [own] + [lax.ppermute(own, "rhs", [(c, (c + t) % cores) for c in range(cores)]) for t in turns]

    def holders(depth):
        return [(2 * p + 1) * 2 ** (top - depth - 1) - 1 for p in range(2**depth)]

    near = pltpu.VMEM
    half = near((count, width), BF16)
    half_f32 = near((count, width), F32)
    joined = near((count, full_width), BF16)
    work = 2 * count * full_width * width
    semaphores = lambda n: pltpu.SemaphoreType.DMA((n,))

    crossing = top == 3 and rows == 2
    swapped = core_columns(inverse_diag)[1:]

    def load(after, arrays):
        outs = [near(a.shape, a.dtype) for a in arrays]
        return call(functools.partial(load_kernel, len(arrays)), [after], arrays, outs, [semaphores(len(arrays))])

    def paired(lefts, rights):
        return [piece for pair in zip(lefts[::-1], rights[::-1]) for piece in pair]

    reduced = call(cast_kernel, [], [right_side], [half], [near((count, width), F32), pltpu.SemaphoreType.DMA(())])
    gathered = rows_of(reduced, holders(0))
    inverses = [load(reduced, [inverse_diag]), *swapped]
    plans = ["rooted", "crossed", "traded"] if crossing else ["plain"] * top
    plans = ["plain", *plans]
    older = []
    solved = None
    for depth, plan in enumerate(plans):
        here = holders(min(depth, top - 1))
        if depth > 0:
            all_joined = near((count, depth * full_width), BF16)
            kernel = functools.partial(offset_kernel, top, depth, rows, plan)
            pieces = paired(rights[::-1], lefts[::-1]) if depth == top else paired(lefts, rights)
            if plan == "rooted":
                pieces = [rights[1], rights[0], lefts[1], lefts[0], rounded]
            elif plan == "crossed":
                pieces = [late, rights[1], rights[0], lefts[1], lefts[0], relayed, rounded]
            elif plan == "traded":
                pieces = [rights[0], lefts[0], lefts[1], rights[1], mine, relayed, late]
            else:
                pieces = [*pieces, *older]
            arrays = [block_rows, right, lower, *pieces]
            if plan == "rooted":
                reduced, own_root = call(kernel, arrays, [], [half, half], [all_joined, joined], work)
            elif depth < top:
                reduced, mine = call(kernel, arrays, [], [half, all_joined], [joined], work)
            else:
                reduced = call(kernel, arrays, [], [half], [all_joined, joined], work)
            if plan == "crossed":
                gathered = [reduced, ring(reduced, [(h, h + 2) for h in holders(1)], 0, here)]
            else:
                gathered = rows_of(reduced, here if depth < top else None)
        split = crossing and depth > 1
        part = []
        if split:
            kernel = functools.partial(begin_kernel, 0 if depth == top else 1, rows, cores)
            part = [call(kernel, [reduced, *inverses], [], [half_f32], (), work // rows)]
        if depth == top:
            staged = [near((count, width), F32), semaphores(cores + 1)]
            return call(functools.partial(last_kernel, rows, cores, split), [*gathered, *inverses, solved, *part], [],
                        [pltpu.HBM(right_side.shape, F32)], [joined, *staged], work)
        older = []
        if depth + 1 < top:
            reach = 2 ** (top - depth - 2)
            ways = [[(h, h - reach) for h in here], [(h, h + reach) for h in here]]
            if plan == "rooted":
                others = [(h, leafs - 1) for h in holders(0)]
                first_side, second_side = ring(own_root, ways[0] + others), ring(own_root, ways[1])
                relayed = call(choose_kernel, [first_side, second_side, own_root], [], [half])
            elif depth > 0:
                older = [send(mine, way, 0) for way in ways]
        else:
            over = [(h, h + 1) for h in here]
            older = [] if crossing else [mine, send(mine, over, 0)]
        kernel = functools.partial(solve_kernel, top, depth, rows, cores, plan, split)
        arrays = [*gathered, *inverses] + ([solved, rounded, *part] if depth else [])
        rounded, solved = call(kernel, arrays, [], [half, half_f32], [joined], work)
        if crossing and depth == 0:
            (root,) = here
            lefts = [ring(rounded, [(root, root - reach, root - 1)]), ring(rounded, ways[0], 1)]
            rights = [ring(rounded, [(root, root + reach, root + 1)]), ring(rounded, ways[1], 1)]
        elif depth + 1 < top:
            lefts, rights = [spread(rounded, way) for way in ways]
            if plan == "rooted":
                late = rows_of(relayed)[1]
        elif crossing:
            lefts, rights = rows_of(rounded), [ring(rounded, over, shift) for shift in range(rows)]
        else:
            lefts, rights = rows_of(rounded), spread(rounded, over)
        if depth == 0:
            right, lower = load(rounded, [right_side, lower_blocks])


def solution(mesh):
    return jax.shard_map(
        local,
        mesh=mesh,
        in_specs=(
            P("leaf", "rhs", "rows"),
            P("leaf", None, ("rows", "rhs")),
            P("leaf", None, None, "rows"),
            P("leaf", None),
        ),
        out_specs=P("leaf", "rhs", "rows"),
        check_vma=False,
    )
```

```python
import functools
import jax
import jax.numpy as jnp
from jax import lax
from jax.experimental import pallas as pl
from jax.experimental.pallas import tpu as pltpu
from jax.sharding import PartitionSpec as P

F32 = jnp.float32
BF16 = jnp.bfloat16


def upper_depth(leaf, top):
    return top - 1 - sum(((leaf + 1) % 2**power == 0).astype(jnp.int32) for power in range(1, top + 1))


def load_kernel(count, after_ref, *refs):
    semaphores = refs[-1]
    copies = [pltpu.make_async_copy(refs[i], refs[count + i], semaphores.at[i]) for i in range(count)]
    for copy in copies:
        copy.start()
    for copy in copies:
        copy.wait()


def choose_kernel(first_ref, second_ref, own_ref, out_ref):
    leaf = lax.axis_index("leaf")
    first = (leaf % 4 == 0) | (leaf == lax.axis_size("leaf") - 1)
    second = leaf % 4 == 2
    for wanted, ref in ((first, first_ref), (second, second_ref), (jnp.logical_not(first | second), own_ref)):
        @pl.when(wanted)
        def _():
            out_ref[...] = ref[...]


def place_pieces(piece_refs, target_ref, start):
    rows = len(piece_refs)
    width = piece_refs[0].shape[1]
    own = lax.axis_index("rows")
    for shift, piece_ref in enumerate(piece_refs):
        source = lax.rem(own - shift + rows, rows)
        target_ref[:, pl.ds(pl.multiple_of(start + source * width, width), width)] = piece_ref[...]


def offset_kernel(top, level, rows, plan, block_rows_ref, right_ref, lower_ref, *refs):
    leaf = lax.axis_index("leaf")
    slot = 0 if level == top else 1
    if plan == "rooted":
        *refs, reduced_ref, piece_ref, joined, picked = refs
    else:
        *refs, reduced_ref, joined, picked = refs
    if plan == "crossed":
        late_ref, *refs = refs
    if level == top:
        pieces = [refs[1:2 * rows:2], refs[:2 * rows:2]]
        if plan == "traded":
            r0, r1, l0, l1 = refs[:4]
            pieces = [[l0, l1], [r0, r1]]
    elif plan == "rooted":
        r1, r0, l1, l0 = refs[:4]
        pieces = [[l0, l1], [r0, r1]]
    elif plan == "crossed":
        r1, r0, l1, l0 = refs[:4]
        pieces = [[l0, l1], [r0, r1]]
    else:
        pieces = [refs[:2 * rows:2][::-1], refs[1:2 * rows:2][::-1]]
    extra = refs[2 * rows:]
    width = right_ref.shape[2]
    full = rows * width
    reach = 2 ** (top - level - 1) if level < top else 1
    first = leaf % 2 == 0 if level == top else ((leaf + 1) // reach) % 4 == 1
    before = (level - 1) * full
    for which, wanted in enumerate((first, jnp.logical_not(first))):
        @pl.when(wanted)
        def _():
            if plan == "rooted":
                piece_ref[...] = pieces[which][0][...]
            elif plan == "traded" and which == 0:
                joined[:, :before] = extra[0][...]
            elif plan == "traded":
                place_pieces(extra[1:1 + rows], joined, 0)
                place_pieces(pieces[0], joined, full)
            elif plan == "plain" and before:
                joined[:, :before] = extra[which][...]
            place_pieces(pieces[which], joined, before)
    if plan == "rooted":
        @pl.when(upper_depth(leaf, top) == 0)
        def _():
            piece_ref[...] = extra[0][...]
    elif plan == "crossed":
        place_pieces([extra[0], late_ref], joined, 0)
    blocks, block_width = lower_ref.shape[1:3]
    highest = joined.shape[1] // block_width - 1
    numbers = block_rows_ref[...]
    for index in range(blocks):
        number = jnp.clip(numbers[slot, index], 0, highest)
        column = pl.multiple_of(number * block_width, block_width)
        picked[:, index * block_width:(index + 1) * block_width] = joined[:, pl.ds(column, block_width)]
    weights = lower_ref[slot].reshape(blocks * block_width, width)
    offset = jnp.dot(picked[...], weights, preferred_element_type=F32)
    reduced_ref[...] = (right_ref[slot] - offset).astype(BF16)
    if plan == "crossed":
        @pl.when(leaf % 2 == 1)
        def _():
            reduced_ref[...] = extra[1][...]


def begin_kernel(slot, rows, cores, piece_ref, *refs):
    inverse_refs, part_ref = refs[:cores], refs[cores]
    width = piece_ref.shape[1]
    quarter = inverse_refs[0].shape[-1]
    own = lax.axis_index("rows")
    for which in range(rows):
        @pl.when(own == which)
        def _():
            for turn, inverse_ref in enumerate(inverse_refs):
                weights = inverse_ref[slot, which * width:(which + 1) * width, :]
                part_ref[:, turn * quarter:(turn + 1) * quarter] = jnp.dot(
                    piece_ref[...], weights, preferred_element_type=F32)


def apply_inverse(slot, cores, piece_refs, inverse_refs, part_ref, joined, store, turns=None):
    rows = len(piece_refs)
    width = piece_refs[0].shape[1]
    quarter = inverse_refs[0].shape[-1]
    own = lax.axis_index("rows")
    if part_ref is None and turns in (None, [0]):
        place_pieces(piece_refs, joined, 0)
    for turn in range(cores) if turns is None else turns:
        inverse_ref = inverse_refs[turn]
        core = lax.rem(lax.axis_index("rhs") - turn + cores, cores)
        columns = pl.ds(pl.multiple_of(core * quarter, quarter), quarter)
        if part_ref is None:
            store(columns, jnp.dot(joined[...], inverse_ref[slot], preferred_element_type=F32))
            continue
        for which in range(rows):
            @pl.when(own == which)
            def _():
                total = part_ref[:, turn * quarter:(turn + 1) * quarter]
                for shift in range(1, rows):
                    source = (which - shift) % rows
                    weights = inverse_ref[slot, source * width:(source + 1) * width, :]
                    total = total + jnp.dot(piece_refs[shift][...], weights, preferred_element_type=F32)
                store(columns, total)


def solve_kernel(top, depth, rows, cores, plan, split, *refs):
    piece_refs = refs[:rows]
    inverse_refs = refs[rows:rows + cores]
    before_ref, held_ref, part_ref = refs[rows + cores:rows + cores + 3]
    part_ref = part_ref if split else None
    rounded_ref, solved_ref, joined = refs[-3:]
    leaf = lax.axis_index("leaf")
    active = upper_depth(leaf, top) == depth

    def store(columns, total):
        rounded_ref[:, columns] = total.astype(BF16)
        before = before_ref[:, columns] if depth > 0 else jnp.zeros_like(total)
        solved_ref[:, columns] = jnp.where(active, total, before)

    apply_inverse(1, cores, piece_refs, inverse_refs, part_ref, joined, store)
    if plan == "crossed":
        for wanted, ref in ((leaf % 4 == 1, held_ref), (leaf % 4 == 3, piece_refs[1])):
            @pl.when(wanted)
            def _():
                rounded_ref[...] = ref[...]


def last_kernel(rows, cores, split, *refs):
    piece_refs = refs[:rows]
    inverse_refs = refs[rows:rows + cores]
    before_ref, *part, out_ref, joined, staged, semaphores = refs[rows + cores:]
    part_ref = part[0] if split else None
    copies = [pltpu.make_async_copy(before_ref, out_ref.at[1], semaphores.at[0])]
    copies[0].start()

    quarter = inverse_refs[0].shape[-1]

    def store(columns, total):
        staged[:, columns] = total

    for turn in range(cores):
        core = lax.rem(lax.axis_index("rhs") - turn + cores, cores)
        columns = pl.ds(pl.multiple_of(core * quarter, quarter), quarter)
        apply_inverse(0, cores, piece_refs, inverse_refs, part_ref, joined, store, [turn])
        copies.append(pltpu.make_async_copy(
            staged.at[:, columns], out_ref.at[0, :, columns], semaphores.at[turn + 1]))
        copies[-1].start()
    for copy in copies:
        copy.wait()


WHOLE = pl.BlockSpec(memory_space=pltpu.VMEM)
FAR = pl.BlockSpec(memory_space=pltpu.HBM)


def call(kernel, near, far, outs, scratch=(), flops=0):
    several = len(outs) > 1
    size = sum(a.size * a.dtype.itemsize for a in [*near, *far])
    near = [pltpu.with_memory_space_constraint(a, pltpu.VMEM) for a in near]
    far = [pltpu.with_memory_space_constraint(a, pltpu.HBM) for a in far]
    specs = [FAR if getattr(o, "memory_space", None) == pltpu.HBM else WHOLE for o in outs]
    return pl.pallas_call(
        kernel,
        in_specs=[WHOLE] * len(near) + [FAR] * len(far),
        out_specs=specs if several else specs[0],
        out_shape=list(outs) if several else outs[0],
        scratch_shapes=list(scratch),
        cost_estimate=pl.CostEstimate(flops=flops, bytes_accessed=size, transcendentals=0),
        compiler_params=pltpu.CompilerParams(vmem_limit_bytes=8 * 2**20),
    )(*near, *far)


def local(right_side, inverse_diag, lower_blocks, block_rows):
    leafs, rows, cores = (lax.axis_size(name) for name in ("leaf", "rows", "rhs"))
    top = leafs.bit_length() - 1
    count, width = right_side.shape[1:]
    full_width = rows * width
    places = ("leaf", "rows")

    def send(value, hops, shift):
        pairs = [(a * rows + r, b * rows + (r + shift) % rows) for a, b in hops for r in range(rows)]
        return lax.ppermute(value, places, pairs)

    def spread(value, hops):
        return [send(value, hops, shift) for shift in range(rows)]

    def permute(value, target):
        pairs = []
        for place in range(leafs * rows):
            goal = target(*divmod(place, rows))
            for core in range(cores):
                if goal is None:
                    pairs.append((place * cores + core, place * cores + (core + 1) % cores))
                else:
                    pairs.append((place * cores + core, (goal[0] * rows + goal[1]) * cores + core))
        return lax.ppermute(value, ("leaf", "rows", "rhs"), pairs)

    def rows_of(value, traders=None):
        traders = range(leafs) if traders is None else traders
        return [value] + [permute(value, lambda h, r: (h, (r + shift) % rows) if h in traders else None)
                          for shift in range(1, rows)]

    def ring(value, rings, shift=0, traders=()):
        after = {a: b for stops in rings for a, b in zip(stops, [*stops[1:], stops[0]])}

        def target(h, r):
            if h in after:
                return after[h], (r + shift) % rows
            return (h, (r + 1) % rows) if h in traders else None

        return permute(value, target)

    def core_columns(own):
        turns = range(1, cores)
        return [own] + [lax.ppermute(own, "rhs", [(c, (c + t) % cores) for c in range(cores)]) for t in turns]

    def holders(depth):
        return [(2 * p + 1) * 2 ** (top - depth - 1) - 1 for p in range(2**depth)]

    near = pltpu.VMEM
    half = near((count, width), BF16)
    half_f32 = near((count, width), F32)
    joined = near((count, full_width), BF16)
    work = 2 * count * full_width * width
    semaphores = lambda n: pltpu.SemaphoreType.DMA((n,))

    crossing = top == 3 and rows == 2
    swapped = core_columns(inverse_diag)[1:]

    def load(after, arrays):
        outs = [near(a.shape, a.dtype) for a in arrays]
        return call(functools.partial(load_kernel, len(arrays)), [after], arrays, outs, [semaphores(len(arrays))])

    def paired(lefts, rights):
        return [piece for pair in zip(lefts[::-1], rights[::-1]) for piece in pair]

    reduced = right_side[1].astype(BF16)
    gathered = rows_of(reduced, holders(0))
    inverses = [load(reduced, [inverse_diag]), *swapped]
    plans = ["rooted", "crossed", "traded"] if crossing else ["plain"] * top
    plans = ["plain", *plans]
    older = []
    solved = None
    for depth, plan in enumerate(plans):
        here = holders(min(depth, top - 1))
        if depth > 0:
            all_joined = near((count, depth * full_width), BF16)
            kernel = functools.partial(offset_kernel, top, depth, rows, plan)
            pieces = paired(rights[::-1], lefts[::-1]) if depth == top else paired(lefts, rights)
            if plan == "rooted":
                pieces = [rights[1], rights[0], lefts[1], lefts[0], rounded]
            elif plan == "crossed":
                pieces = [late, rights[1], rights[0], lefts[1], lefts[0], relayed, rounded]
            elif plan == "traded":
                pieces = [rights[0], rights[1], lefts[0], lefts[1], mine, relayed, late]
            else:
                pieces = [*pieces, *older]
            arrays = [block_rows, right, lower, *pieces]
            if plan == "rooted":
                reduced, own_root = call(kernel, arrays, [], [half, half], [all_joined, joined], work)
            elif depth < top:
                reduced, mine = call(kernel, arrays, [], [half, all_joined], [joined], work)
            else:
                reduced = call(kernel, arrays, [], [half], [all_joined, joined], work)
            if plan == "crossed":
                gathered = [reduced, ring(reduced, [(h, h + 2) for h in holders(1)], 0, here)]
            else:
                gathered = rows_of(reduced, here if depth < top else None)
        split = crossing and depth > 1
        part = []
        if split:
            kernel = functools.partial(begin_kernel, 0 if depth == top else 1, rows, cores)
            part = [call(kernel, [reduced, *inverses], [], [half_f32], (), work // rows)]
        if depth == top:
            staged = [near((count, width), F32), semaphores(cores + 1)]
            return call(functools.partial(last_kernel, rows, cores, split), [*gathered, *inverses, solved, *part], [],
                        [pltpu.HBM(right_side.shape, F32)], [joined, *staged], work)
        older = []
        if depth + 1 < top:
            reach = 2 ** (top - depth - 2)
            ways = [[(h, h - reach) for h in here], [(h, h + reach) for h in here]]
            if plan == "rooted":
                others = [(h, leafs - 1) for h in holders(0)]
                first_side, second_side = ring(own_root, ways[0] + others), ring(own_root, ways[1])
                relayed = call(choose_kernel, [first_side, second_side, own_root], [], [half])
            elif depth > 0:
                older = [send(mine, way, 0) for way in ways]
        else:
            over = [(h, h + 1) for h in here]
            older = [] if crossing else [mine, send(mine, over, 0)]
        kernel = functools.partial(solve_kernel, top, depth, rows, cores, plan, split)
        arrays = [*gathered, *inverses] + ([solved, rounded, *part] if depth else [])
        rounded, solved = call(kernel, arrays, [], [half, half_f32], [joined], work)
        if crossing and depth == 0:
            (root,) = here
            lefts = [ring(rounded, [(root, root - reach, root - 1)]), ring(rounded, ways[0], 1)]
            rights = [ring(rounded, [(root, root + reach, root + 1)]), ring(rounded, ways[1], 1)]
        elif depth + 1 < top:
            lefts, rights = [spread(rounded, way) for way in ways]
            if plan == "rooted":
                late = rows_of(relayed)[1]
        elif crossing:
            lefts, rights = rows_of(rounded), [ring(rounded, over, shift) for shift in range(rows)]
        else:
            lefts, rights = rows_of(rounded), spread(rounded, over)
        if depth == 0:
            right, lower = load(rounded, [right_side, lower_blocks])


def solution(mesh):
    return jax.shard_map(
        local,
        mesh=mesh,
        in_specs=(
            P("leaf", "rhs", "rows"),
            P("leaf", None, ("rows", "rhs")),
            P("leaf", None, None, "rows"),
            P("leaf", None),
        ),
        out_specs=P("leaf", "rhs", "rows"),
        check_vma=False,
    )
```

```python
import functools
import jax
import jax.numpy as jnp
from jax import lax
from jax.experimental import pallas as pl
from jax.experimental.pallas import tpu as pltpu
from jax.sharding import PartitionSpec as P

F32 = jnp.float32
BF16 = jnp.bfloat16


def upper_depth(leaf, top):
    return top - 1 - sum(((leaf + 1) % 2**power == 0).astype(jnp.int32) for power in range(1, top + 1))


def load_kernel(count, after_ref, *refs):
    semaphores = refs[-1]
    copies = [pltpu.make_async_copy(refs[i], refs[count + i], semaphores.at[i]) for i in range(count)]
    for copy in copies:
        copy.start()
    for copy in copies:
        copy.wait()


def choose_kernel(first_ref, second_ref, own_ref, out_ref):
    leaf = lax.axis_index("leaf")
    first = (leaf % 4 == 0) | (leaf == lax.axis_size("leaf") - 1)
    second = leaf % 4 == 2
    for wanted, ref in ((first, first_ref), (second, second_ref), (jnp.logical_not(first | second), own_ref)):
        @pl.when(wanted)
        def _():
            out_ref[...] = ref[...]


def place_pieces(piece_refs, target_ref, start):
    rows = len(piece_refs)
    width = piece_refs[0].shape[1]
    own = lax.axis_index("rows")
    for shift, piece_ref in enumerate(piece_refs):
        source = lax.rem(own - shift + rows, rows)
        target_ref[:, pl.ds(pl.multiple_of(start + source * width, width), width)] = piece_ref[...]


def offset_kernel(top, level, rows, plan, block_rows_ref, right_ref, lower_ref, *refs):
    leaf = lax.axis_index("leaf")
    slot = 0 if level == top else 1
    if plan == "rooted":
        *refs, reduced_ref, piece_ref, joined, picked = refs
    else:
        *refs, reduced_ref, joined, picked = refs
    if plan == "crossed":
        late_ref, *refs = refs
    if level == top:
        pieces = [refs[1:2 * rows:2], refs[:2 * rows:2]]
        if plan == "traded":
            r0, r1, l0, l1 = refs[:4]
            pieces = [[l0, l1], [r0, r1]]
    elif plan == "rooted":
        r1, r0, l1, l0 = refs[:4]
        pieces = [[l0, l1], [r0, r1]]
    elif plan == "crossed":
        r1, r0, l1, l0 = refs[:4]
        pieces = [[l0, l1], [r0, r1]]
    else:
        pieces = [refs[:2 * rows:2][::-1], refs[1:2 * rows:2][::-1]]
    extra = refs[2 * rows:]
    width = right_ref.shape[2]
    full = rows * width
    reach = 2 ** (top - level - 1) if level < top else 1
    first = leaf % 2 == 0 if level == top else ((leaf + 1) // reach) % 4 == 1
    before = (level - 1) * full
    for which, wanted in enumerate((first, jnp.logical_not(first))):
        @pl.when(wanted)
        def _():
            if plan == "rooted":
                piece_ref[...] = pieces[which][0][...]
            elif plan == "traded" and which == 0:
                joined[:, :before] = extra[0][...]
            elif plan == "traded":
                place_pieces(extra[1:1 + rows], joined, 0)
                place_pieces(pieces[0], joined, full)
            elif plan == "plain" and before:
                joined[:, :before] = extra[which][...]
            place_pieces(pieces[which], joined, before)
    if plan == "rooted":
        @pl.when(upper_depth(leaf, top) == 0)
        def _():
            piece_ref[...] = extra[0][...]
    elif plan == "crossed":
        place_pieces([extra[0], late_ref], joined, 0)
    blocks, block_width = lower_ref.shape[1:3]
    highest = joined.shape[1] // block_width - 1
    numbers = block_rows_ref[...]
    for index in range(blocks):
        number = jnp.clip(numbers[slot, index], 0, highest)
        column = pl.multiple_of(number * block_width, block_width)
        picked[:, index * block_width:(index + 1) * block_width] = joined[:, pl.ds(column, block_width)]
    weights = lower_ref[slot].reshape(blocks * block_width, width)
    offset = jnp.dot(picked[...], weights, preferred_element_type=F32)
    reduced_ref[...] = (right_ref[slot] - offset).astype(BF16)
    if plan == "crossed":
        @pl.when(leaf % 2 == 1)
        def _():
            reduced_ref[...] = extra[1][...]


def begin_kernel(slot, rows, cores, piece_ref, *refs):
    inverse_refs, part_ref = refs[:cores], refs[cores]
    width = piece_ref.shape[1]
    quarter = inverse_refs[0].shape[-1]
    own = lax.axis_index("rows")
    for which in range(rows):
        @pl.when(own == which)
        def _():
            for turn, inverse_ref in enumerate(inverse_refs):
                weights = inverse_ref[slot, which * width:(which + 1) * width, :]
                part_ref[:, turn * quarter:(turn + 1) * quarter] = jnp.dot(
                    piece_ref[...], weights, preferred_element_type=F32)


def apply_inverse(slot, cores, piece_refs, inverse_refs, part_ref, joined, store):
    rows = len(piece_refs)
    width = piece_refs[0].shape[1]
    quarter = inverse_refs[0].shape[-1]

    def share(turn):
        core = lax.rem(lax.axis_index("rhs") - turn + cores, cores)
        return pl.ds(pl.multiple_of(core * quarter, quarter), quarter)

    if part_ref is None:
        place_pieces(piece_refs, joined, 0)
        for turn, inverse_ref in enumerate(inverse_refs):
            store(turn, share(turn), jnp.dot(joined[...], inverse_ref[slot], preferred_element_type=F32))
        return
    for which in range(rows):
        @pl.when(lax.axis_index("rows") == which)
        def _():
            for turn, inverse_ref in enumerate(inverse_refs):
                total = part_ref[:, turn * quarter:(turn + 1) * quarter]
                for shift in range(1, rows):
                    source = (which - shift) % rows
                    weights = inverse_ref[slot, source * width:(source + 1) * width, :]
                    total = total + jnp.dot(piece_refs[shift][...], weights, preferred_element_type=F32)
                store(turn, share(turn), total)


def solve_kernel(top, depth, rows, cores, plan, split, *refs):
    piece_refs = refs[:rows]
    inverse_refs = refs[rows:rows + cores]
    before_ref, held_ref, part_ref = refs[rows + cores:rows + cores + 3]
    part_ref = part_ref if split else None
    rounded_ref, solved_ref, joined = refs[-3:]
    leaf = lax.axis_index("leaf")
    active = upper_depth(leaf, top) == depth

    def store(turn, columns, total):
        rounded_ref[:, columns] = total.astype(BF16)
        before = before_ref[:, columns] if depth > 0 else jnp.zeros_like(total)
        solved_ref[:, columns] = jnp.where(active, total, before)

    apply_inverse(1, cores, piece_refs, inverse_refs, part_ref, joined, store)
    if plan == "crossed":
        for wanted, ref in ((leaf % 4 == 1, held_ref), (leaf % 4 == 3, piece_refs[1])):
            @pl.when(wanted)
            def _():
                rounded_ref[...] = ref[...]


def last_kernel(rows, cores, split, *refs):
    piece_refs = refs[:rows]
    inverse_refs = refs[rows:rows + cores]
    before_ref, *part, out_ref, joined, staged, semaphores = refs[rows + cores:]
    part_ref = part[0] if split else None
    quarter = inverse_refs[0].shape[-1]
    earlier = pltpu.make_async_copy(before_ref, out_ref.at[1], semaphores.at[0])
    earlier.start()

    def written(turn, columns):
        return pltpu.make_async_copy(staged.at[:, columns], out_ref.at[0, :, columns], semaphores.at[turn + 1])

    def store(turn, columns, total):
        staged[:, columns] = total
        written(turn, columns).start()

    apply_inverse(0, cores, piece_refs, inverse_refs, part_ref, joined, store)
    for turn in range(cores):
        written(turn, pl.ds(0, quarter)).wait()
    earlier.wait()


WHOLE = pl.BlockSpec(memory_space=pltpu.VMEM)
FAR = pl.BlockSpec(memory_space=pltpu.HBM)


def call(kernel, near, far, outs, scratch=(), flops=0):
    several = len(outs) > 1
    size = sum(a.size * a.dtype.itemsize for a in [*near, *far])
    near = [pltpu.with_memory_space_constraint(a, pltpu.VMEM) for a in near]
    far = [pltpu.with_memory_space_constraint(a, pltpu.HBM) for a in far]
    specs = [FAR if getattr(o, "memory_space", None) == pltpu.HBM else WHOLE for o in outs]
    return pl.pallas_call(
        kernel,
        in_specs=[WHOLE] * len(near) + [FAR] * len(far),
        out_specs=specs if several else specs[0],
        out_shape=list(outs) if several else outs[0],
        scratch_shapes=list(scratch),
        cost_estimate=pl.CostEstimate(flops=flops, bytes_accessed=size, transcendentals=0),
        compiler_params=pltpu.CompilerParams(vmem_limit_bytes=8 * 2**20),
    )(*near, *far)


def local(right_side, inverse_diag, lower_blocks, block_rows):
    leafs, rows, cores = (lax.axis_size(name) for name in ("leaf", "rows", "rhs"))
    top = leafs.bit_length() - 1
    count, width = right_side.shape[1:]
    full_width = rows * width
    places = ("leaf", "rows")

    def send(value, hops, shift):
        pairs = [(a * rows + r, b * rows + (r + shift) % rows) for a, b in hops for r in range(rows)]
        return lax.ppermute(value, places, pairs)

    def spread(value, hops):
        return [send(value, hops, shift) for shift in range(rows)]

    def permute(value, target):
        pairs = []
        for place in range(leafs * rows):
            goal = target(*divmod(place, rows))
            for core in range(cores):
                if goal is None:
                    pairs.append((place * cores + core, place * cores + (core + 1) % cores))
                else:
                    pairs.append((place * cores + core, (goal[0] * rows + goal[1]) * cores + core))
        return lax.ppermute(value, ("leaf", "rows", "rhs"), pairs)

    def rows_of(value, traders=None):
        traders = range(leafs) if traders is None else traders
        return [value] + [permute(value, lambda h, r: (h, (r + shift) % rows) if h in traders else None)
                          for shift in range(1, rows)]

    def ring(value, rings, shift=0, traders=()):
        after = {a: b for stops in rings for a, b in zip(stops, [*stops[1:], stops[0]])}

        def target(h, r):
            if h in after:
                return after[h], (r + shift) % rows
            return (h, (r + 1) % rows) if h in traders else None

        return permute(value, target)

    def core_columns(own):
        turns = range(1, cores)
        return [own] + [lax.ppermute(own, "rhs", [(c, (c + t) % cores) for c in range(cores)]) for t in turns]

    def holders(depth):
        return [(2 * p + 1) * 2 ** (top - depth - 1) - 1 for p in range(2**depth)]

    near = pltpu.VMEM
    half = near((count, width), BF16)
    half_f32 = near((count, width), F32)
    joined = near((count, full_width), BF16)
    work = 2 * count * full_width * width
    semaphores = lambda n: pltpu.SemaphoreType.DMA((n,))

    crossing = top == 3 and rows == 2
    swapped = core_columns(inverse_diag)[1:]

    def load(after, arrays):
        outs = [near(a.shape, a.dtype) for a in arrays]
        return call(functools.partial(load_kernel, len(arrays)), [after], arrays, outs, [semaphores(len(arrays))])

    def paired(lefts, rights):
        return [piece for pair in zip(lefts[::-1], rights[::-1]) for piece in pair]

    reduced = right_side[1].astype(BF16)
    gathered = rows_of(reduced, holders(0))
    inverse_own, right, lower = load(reduced, [inverse_diag, right_side, lower_blocks])
    inverses = [inverse_own, *swapped]
    plans = ["rooted", "crossed", "traded"] if crossing else ["plain"] * top
    plans = ["plain", *plans]
    older = []
    solved = None
    for depth, plan in enumerate(plans):
        here = holders(min(depth, top - 1))
        if depth > 0:
            all_joined = near((count, depth * full_width), BF16)
            kernel = functools.partial(offset_kernel, top, depth, rows, plan)
            pieces = paired(rights[::-1], lefts[::-1]) if depth == top else paired(lefts, rights)
            if plan == "rooted":
                pieces = [rights[1], rights[0], lefts[1], lefts[0], rounded]
            elif plan == "crossed":
                pieces = [late, rights[1], rights[0], lefts[1], lefts[0], relayed, rounded]
            elif plan == "traded":
                pieces = [rights[0], rights[1], lefts[0], lefts[1], mine, relayed, late]
            else:
                pieces = [*pieces, *older]
            arrays = [block_rows, right, lower, *pieces]
            if plan == "rooted":
                reduced, own_root = call(kernel, arrays, [], [half, half], [all_joined, joined], work)
            elif depth < top:
                reduced, mine = call(kernel, arrays, [], [half, all_joined], [joined], work)
            else:
                reduced = call(kernel, arrays, [], [half], [all_joined, joined], work)
            if plan == "crossed":
                gathered = [reduced, ring(reduced, [(h, h + 2) for h in holders(1)], 0, here)]
            else:
                gathered = rows_of(reduced, here if depth < top else None)
        split = crossing and depth > 1
        part = []
        if split:
            kernel = functools.partial(begin_kernel, 0 if depth == top else 1, rows, cores)
            part = [call(kernel, [reduced, *inverses], [], [half_f32], (), work // rows)]
        if depth == top:
            staged = [near((count, width), F32), semaphores(cores + 1)]
            return call(functools.partial(last_kernel, rows, cores, split), [*gathered, *inverses, solved, *part], [],
                        [pltpu.HBM(right_side.shape, F32)], [joined, *staged], work)
        older = []
        if depth + 1 < top:
            reach = 2 ** (top - depth - 2)
            ways = [[(h, h - reach) for h in here], [(h, h + reach) for h in here]]
            if plan == "rooted":
                others = [(h, leafs - 1) for h in holders(0)]
                first_side, second_side = ring(own_root, ways[0] + others), ring(own_root, ways[1])
                relayed = call(choose_kernel, [first_side, second_side, own_root], [], [half])
            elif depth > 0:
                older = [send(mine, way, 0) for way in ways]
        else:
            over = [(h, h + 1) for h in here]
            older = [] if crossing else [mine, send(mine, over, 0)]
        kernel = functools.partial(solve_kernel, top, depth, rows, cores, plan, split)
        arrays = [*gathered, *inverses] + ([solved, rounded, *part] if depth else [])
        rounded, solved = call(kernel, arrays, [], [half, half_f32], [joined], work)
        if crossing and depth == 0:
            (root,) = here
            lefts = [ring(rounded, [(root, root - reach, root - 1)]), ring(rounded, ways[0], 1)]
            rights = [ring(rounded, [(root, root + reach, root + 1)]), ring(rounded, ways[1], 1)]
        elif depth + 1 < top:
            lefts, rights = [spread(rounded, way) for way in ways]
            if plan == "rooted":
                late = rows_of(relayed)[1]
        elif crossing:
            lefts, rights = rows_of(rounded), [ring(rounded, over, shift) for shift in range(rows)]
        else:
            lefts, rights = rows_of(rounded), spread(rounded, over)


def solution(mesh):
    return jax.shard_map(
        local,
        mesh=mesh,
        in_specs=(
            P("leaf", "rhs", "rows"),
            P("leaf", None, ("rows", "rhs")),
            P("leaf", None, None, "rows"),
            P("leaf", None),
        ),
        out_specs=P("leaf", "rhs", "rows"),
        check_vma=False,
    )
```

```python
import functools
import jax
import jax.numpy as jnp
from jax import lax
from jax.experimental import pallas as pl
from jax.experimental.pallas import tpu as pltpu
from jax.sharding import PartitionSpec as P

F32 = jnp.float32
BF16 = jnp.bfloat16


def upper_depth(leaf, top):
    return top - 1 - sum(((leaf + 1) % 2**power == 0).astype(jnp.int32) for power in range(1, top + 1))


def load_kernel(count, after_ref, *refs):
    semaphores = refs[-1]
    copies = [pltpu.make_async_copy(refs[i], refs[count + i], semaphores.at[i]) for i in range(count)]
    for copy in copies:
        copy.start()
    for copy in copies:
        copy.wait()


def choose_kernel(first_ref, second_ref, own_ref, out_ref):
    leaf = lax.axis_index("leaf")
    first = (leaf % 4 == 0) | (leaf == lax.axis_size("leaf") - 1)
    second = leaf % 4 == 2
    for wanted, ref in ((first, first_ref), (second, second_ref), (jnp.logical_not(first | second), own_ref)):
        @pl.when(wanted)
        def _():
            out_ref[...] = ref[...]


def place_pieces(piece_refs, target_ref, start):
    rows = len(piece_refs)
    width = piece_refs[0].shape[1]
    own = lax.axis_index("rows")
    for shift, piece_ref in enumerate(piece_refs):
        source = lax.rem(own - shift + rows, rows)
        target_ref[:, pl.ds(pl.multiple_of(start + source * width, width), width)] = piece_ref[...]


def offset_kernel(top, level, rows, plan, block_rows_ref, right_ref, lower_ref, *refs):
    leaf = lax.axis_index("leaf")
    slot = 0 if level == top else 1
    if plan == "rooted":
        *refs, reduced_ref, piece_ref, joined, picked = refs
    else:
        *refs, reduced_ref, joined, picked = refs
    if plan == "crossed":
        late_ref, *refs = refs
    if level == top:
        pieces = [refs[1:2 * rows:2], refs[:2 * rows:2]]
        if plan == "traded":
            r0, r1, l0, l1 = refs[:4]
            pieces = [[l0, l1], [r0, r1]]
    elif plan == "rooted":
        r1, r0, l1, l0 = refs[:4]
        pieces = [[l0, l1], [r0, r1]]
    elif plan == "crossed":
        r1, r0, l1, l0 = refs[:4]
        pieces = [[l0, l1], [r0, r1]]
    else:
        pieces = [refs[:2 * rows:2][::-1], refs[1:2 * rows:2][::-1]]
    extra = refs[2 * rows:]
    width = right_ref.shape[2]
    full = rows * width
    reach = 2 ** (top - level - 1) if level < top else 1
    first = leaf % 2 == 0 if level == top else ((leaf + 1) // reach) % 4 == 1
    before = (level - 1) * full
    for which, wanted in enumerate((first, jnp.logical_not(first))):
        @pl.when(wanted)
        def _():
            if plan == "rooted":
                piece_ref[...] = pieces[which][0][...]
            elif plan == "traded" and which == 0:
                joined[:, :before] = extra[0][...]
            elif plan == "traded":
                place_pieces(extra[1:1 + rows], joined, 0)
                place_pieces(pieces[0], joined, full)
            elif plan == "plain" and before:
                joined[:, :before] = extra[which][...]
            place_pieces(pieces[which], joined, before)
    if plan == "rooted":
        @pl.when(upper_depth(leaf, top) == 0)
        def _():
            piece_ref[...] = extra[0][...]
    elif plan == "crossed":
        place_pieces([extra[0], late_ref], joined, 0)
    blocks, block_width = lower_ref.shape[1:3]
    highest = joined.shape[1] // block_width - 1

    def product():
        numbers = block_rows_ref[...]
        for index in range(blocks):
            number = jnp.clip(numbers[slot, index], 0, highest)
            column = pl.multiple_of(number * block_width, block_width)
            picked[:, index * block_width:(index + 1) * block_width] = joined[:, pl.ds(column, block_width)]
        weights = lower_ref[slot].reshape(blocks * block_width, width)
        offset = jnp.dot(picked[...], weights, preferred_element_type=F32)
        reduced_ref[...] = (right_ref[slot] - offset).astype(BF16)

    if level == top:
        product()
        return
    active = upper_depth(leaf, top) == level
    pl.when(active)(product)

    @pl.when(jnp.logical_not(active))
    def _():
        reduced_ref[...] = extra[1][...] if plan == "crossed" else jnp.zeros_like(reduced_ref)


def begin_kernel(top, depth, rows, cores, piece_ref, *refs):
    inverse_refs, part_ref = refs[:cores], refs[cores]
    width = piece_ref.shape[1]
    quarter = inverse_refs[0].shape[-1]
    slot = 0 if depth == top else 1
    own = lax.axis_index("rows")
    active = (upper_depth(lax.axis_index("leaf"), top) == depth) | (depth == top)
    for which in range(rows):
        @pl.when((own == which) & active)
        def _():
            for turn, inverse_ref in enumerate(inverse_refs):
                weights = inverse_ref[slot, which * width:(which + 1) * width, :]
                part_ref[:, turn * quarter:(turn + 1) * quarter] = jnp.dot(
                    piece_ref[...], weights, preferred_element_type=F32)


def apply_inverse(slot, cores, piece_refs, inverse_refs, part_ref, joined, store):
    rows = len(piece_refs)
    width = piece_refs[0].shape[1]
    quarter = inverse_refs[0].shape[-1]

    def share(turn):
        core = lax.rem(lax.axis_index("rhs") - turn + cores, cores)
        return pl.ds(pl.multiple_of(core * quarter, quarter), quarter)

    if part_ref is None:
        place_pieces(piece_refs, joined, 0)
        for turn, inverse_ref in enumerate(inverse_refs):
            store(turn, share(turn), jnp.dot(joined[...], inverse_ref[slot], preferred_element_type=F32))
        return
    for which in range(rows):
        @pl.when(lax.axis_index("rows") == which)
        def _():
            for turn, inverse_ref in enumerate(inverse_refs):
                total = part_ref[:, turn * quarter:(turn + 1) * quarter]
                for shift in range(1, rows):
                    source = (which - shift) % rows
                    weights = inverse_ref[slot, source * width:(source + 1) * width, :]
                    total = total + jnp.dot(piece_refs[shift][...], weights, preferred_element_type=F32)
                store(turn, share(turn), total)


def solve_kernel(top, depth, rows, cores, plan, split, *refs):
    piece_refs = refs[:rows]
    inverse_refs = refs[rows:rows + cores]
    before_ref, held_ref, part_ref = refs[rows + cores:rows + cores + 3]
    part_ref = part_ref if split else None
    rounded_ref, solved_ref, joined = refs[-3:]
    leaf = lax.axis_index("leaf")
    active = upper_depth(leaf, top) == depth

    def store(turn, columns, total):
        rounded_ref[:, columns] = total.astype(BF16)
        solved_ref[:, columns] = total

    @pl.when(active)
    def _():
        apply_inverse(1, cores, piece_refs, inverse_refs, part_ref, joined, store)

    @pl.when(jnp.logical_not(active))
    def _():
        rounded_ref[...] = jnp.zeros_like(rounded_ref)
        solved_ref[...] = before_ref[...] if depth > 0 else jnp.zeros_like(solved_ref)

    if plan == "crossed":
        for wanted, ref in ((leaf % 4 == 1, held_ref), (leaf % 4 == 3, piece_refs[1])):
            @pl.when(wanted)
            def _():
                rounded_ref[...] = ref[...]


def last_kernel(rows, cores, split, *refs):
    piece_refs = refs[:rows]
    inverse_refs = refs[rows:rows + cores]
    before_ref, *part, out_ref, joined, staged, semaphores = refs[rows + cores:]
    part_ref = part[0] if split else None
    quarter = inverse_refs[0].shape[-1]
    earlier = pltpu.make_async_copy(before_ref, out_ref.at[1], semaphores.at[0])
    earlier.start()

    def written(turn, columns):
        return pltpu.make_async_copy(staged.at[:, columns], out_ref.at[0, :, columns], semaphores.at[turn + 1])

    def store(turn, columns, total):
        staged[:, columns] = total
        written(turn, columns).start()

    apply_inverse(0, cores, piece_refs, inverse_refs, part_ref, joined, store)
    for turn in range(cores):
        written(turn, pl.ds(0, quarter)).wait()
    earlier.wait()


WHOLE = pl.BlockSpec(memory_space=pltpu.VMEM)
FAR = pl.BlockSpec(memory_space=pltpu.HBM)


def call(kernel, near, far, outs, scratch=(), flops=0):
    several = len(outs) > 1
    size = sum(a.size * a.dtype.itemsize for a in [*near, *far])
    near = [pltpu.with_memory_space_constraint(a, pltpu.VMEM) for a in near]
    far = [pltpu.with_memory_space_constraint(a, pltpu.HBM) for a in far]
    specs = [FAR if getattr(o, "memory_space", None) == pltpu.HBM else WHOLE for o in outs]
    return pl.pallas_call(
        kernel,
        in_specs=[WHOLE] * len(near) + [FAR] * len(far),
        out_specs=specs if several else specs[0],
        out_shape=list(outs) if several else outs[0],
        scratch_shapes=list(scratch),
        cost_estimate=pl.CostEstimate(flops=flops, bytes_accessed=size, transcendentals=0),
        compiler_params=pltpu.CompilerParams(vmem_limit_bytes=8 * 2**20),
    )(*near, *far)


def local(right_side, inverse_diag, lower_blocks, block_rows):
    leafs, rows, cores = (lax.axis_size(name) for name in ("leaf", "rows", "rhs"))
    top = leafs.bit_length() - 1
    count, width = right_side.shape[1:]
    full_width = rows * width
    places = ("leaf", "rows")

    def send(value, hops, shift):
        pairs = [(a * rows + r, b * rows + (r + shift) % rows) for a, b in hops for r in range(rows)]
        return lax.ppermute(value, places, pairs)

    def spread(value, hops):
        return [send(value, hops, shift) for shift in range(rows)]

    def permute(value, target):
        pairs = []
        for place in range(leafs * rows):
            goal = target(*divmod(place, rows))
            for core in range(cores):
                if goal is None:
                    pairs.append((place * cores + core, place * cores + (core + 1) % cores))
                else:
                    pairs.append((place * cores + core, (goal[0] * rows + goal[1]) * cores + core))
        return lax.ppermute(value, ("leaf", "rows", "rhs"), pairs)

    def rows_of(value, traders=None):
        traders = range(leafs) if traders is None else traders
        return [value] + [permute(value, lambda h, r: (h, (r + shift) % rows) if h in traders else None)
                          for shift in range(1, rows)]

    def ring(value, rings, shift=0, traders=()):
        after = {a: b for stops in rings for a, b in zip(stops, [*stops[1:], stops[0]])}

        def target(h, r):
            if h in after:
                return after[h], (r + shift) % rows
            return (h, (r + 1) % rows) if h in traders else None

        return permute(value, target)

    def core_columns(own):
        turns = range(1, cores)
        return [own] + [lax.ppermute(own, "rhs", [(c, (c + t) % cores) for c in range(cores)]) for t in turns]

    def holders(depth):
        return [(2 * p + 1) * 2 ** (top - depth - 1) - 1 for p in range(2**depth)]

    near = pltpu.VMEM
    half = near((count, width), BF16)
    half_f32 = near((count, width), F32)
    joined = near((count, full_width), BF16)
    work = 2 * count * full_width * width
    semaphores = lambda n: pltpu.SemaphoreType.DMA((n,))

    crossing = top == 3 and rows == 2
    swapped = core_columns(inverse_diag)[1:]

    def load(after, arrays):
        outs = [near(a.shape, a.dtype) for a in arrays]
        return call(functools.partial(load_kernel, len(arrays)), [after], arrays, outs, [semaphores(len(arrays))])

    def paired(lefts, rights):
        return [piece for pair in zip(lefts[::-1], rights[::-1]) for piece in pair]

    reduced = right_side[1].astype(BF16)
    gathered = rows_of(reduced, holders(0))
    inverse_own, right, lower = load(reduced, [inverse_diag, right_side, lower_blocks])
    inverses = [inverse_own, *swapped]
    plans = ["rooted", "crossed", "traded"] if crossing else ["plain"] * top
    plans = ["plain", *plans]
    older = []
    solved = None
    for depth, plan in enumerate(plans):
        here = holders(min(depth, top - 1))
        if depth > 0:
            all_joined = near((count, depth * full_width), BF16)
            kernel = functools.partial(offset_kernel, top, depth, rows, plan)
            pieces = paired(rights[::-1], lefts[::-1]) if depth == top else paired(lefts, rights)
            if plan == "rooted":
                pieces = [rights[1], rights[0], lefts[1], lefts[0], rounded]
            elif plan == "crossed":
                pieces = [late, rights[1], rights[0], lefts[1], lefts[0], relayed, rounded]
            elif plan == "traded":
                pieces = [rights[0], rights[1], lefts[0], lefts[1], mine, relayed, late]
            else:
                pieces = [*pieces, *older]
            arrays = [block_rows, right, lower, *pieces]
            if plan == "rooted":
                reduced, own_root = call(kernel, arrays, [], [half, half], [all_joined, joined], work)
            elif depth < top:
                reduced, mine = call(kernel, arrays, [], [half, all_joined], [joined], work)
            else:
                reduced = call(kernel, arrays, [], [half], [all_joined, joined], work)
            if plan == "crossed":
                gathered = [reduced, ring(reduced, [(h, h + 2) for h in holders(1)], 0, here)]
            else:
                gathered = rows_of(reduced, here if depth < top else None)
        split = crossing and depth > 1
        part = []
        if split:
            kernel = functools.partial(begin_kernel, top, depth, rows, cores)
            part = [call(kernel, [reduced, *inverses], [], [half_f32], (), work // rows)]
        if depth == top:
            staged = [near((count, width), F32), semaphores(cores + 1)]
            return call(functools.partial(last_kernel, rows, cores, split), [*gathered, *inverses, solved, *part], [],
                        [pltpu.HBM(right_side.shape, F32)], [joined, *staged], work)
        older = []
        if depth + 1 < top:
            reach = 2 ** (top - depth - 2)
            ways = [[(h, h - reach) for h in here], [(h, h + reach) for h in here]]
            if plan == "rooted":
                others = [(h, leafs - 1) for h in holders(0)]
                first_side, second_side = ring(own_root, ways[0] + others), ring(own_root, ways[1])
                relayed = call(choose_kernel, [first_side, second_side, own_root], [], [half])
            elif depth > 0:
                older = [send(mine, way, 0) for way in ways]
        else:
            over = [(h, h + 1) for h in here]
            older = [] if crossing else [mine, send(mine, over, 0)]
        kernel = functools.partial(solve_kernel, top, depth, rows, cores, plan, split)
        arrays = [*gathered, *inverses] + ([solved, rounded, *part] if depth else [])
        rounded, solved = call(kernel, arrays, [], [half, half_f32], [joined], work)
        if crossing and depth == 0:
            (root,) = here
            lefts = [ring(rounded, [(root, root - reach, root - 1)]), ring(rounded, ways[0], 1)]
            rights = [ring(rounded, [(root, root + reach, root + 1)]), ring(rounded, ways[1], 1)]
        elif depth + 1 < top:
            lefts, rights = [spread(rounded, way) for way in ways]
            if plan == "rooted":
                late = rows_of(relayed)[1]
        elif crossing:
            lefts, rights = rows_of(rounded), [ring(rounded, over, shift) for shift in range(rows)]
        else:
            lefts, rights = rows_of(rounded), spread(rounded, over)


def solution(mesh):
    return jax.shard_map(
        local,
        mesh=mesh,
        in_specs=(
            P("leaf", "rhs", "rows"),
            P("leaf", None, ("rows", "rhs")),
            P("leaf", None, None, "rows"),
            P("leaf", None),
        ),
        out_specs=P("leaf", "rhs", "rows"),
        check_vma=False,
    )
```

```python
import functools
import jax
import jax.numpy as jnp
from jax import lax
from jax.experimental import pallas as pl
from jax.experimental.pallas import tpu as pltpu
from jax.sharding import PartitionSpec as P

F32 = jnp.float32
BF16 = jnp.bfloat16


def upper_depth(leaf, top):
    return top - 1 - sum(((leaf + 1) % 2**power == 0).astype(jnp.int32) for power in range(1, top + 1))


def load_kernel(count, after_ref, *refs):
    semaphores = refs[-1]
    copies = [pltpu.make_async_copy(refs[i], refs[count + i], semaphores.at[i]) for i in range(count)]
    for copy in copies:
        copy.start()
    for copy in copies:
        copy.wait()


def choose_kernel(first_ref, second_ref, own_ref, out_ref):
    leaf = lax.axis_index("leaf")
    first = (leaf % 4 == 0) | (leaf == lax.axis_size("leaf") - 1)
    second = leaf % 4 == 2
    for wanted, ref in ((first, first_ref), (second, second_ref), (jnp.logical_not(first | second), own_ref)):
        @pl.when(wanted)
        def _():
            out_ref[...] = ref[...]


def place_pieces(piece_refs, target_ref, start):
    rows = len(piece_refs)
    width = piece_refs[0].shape[1]
    own = lax.axis_index("rows")
    for shift, piece_ref in enumerate(piece_refs):
        source = lax.rem(own - shift + rows, rows)
        target_ref[:, pl.ds(pl.multiple_of(start + source * width, width), width)] = piece_ref[...]


def offset_kernel(top, level, rows, plan, block_rows_ref, right_ref, lower_ref, *refs):
    leaf = lax.axis_index("leaf")
    slot = 0 if level == top else 1
    if plan == "rooted":
        *refs, reduced_ref, piece_ref, joined, picked = refs
    else:
        *refs, reduced_ref, joined, picked = refs
    if plan == "crossed":
        late_ref, *refs = refs
    if level == top:
        pieces = [refs[1:2 * rows:2], refs[:2 * rows:2]]
        if plan == "traded":
            r1, l0, l1, r0 = refs[:4]
            pieces = [[l0, l1], [r0, r1]]
    elif plan == "rooted":
        r1, r0, l1, l0 = refs[:4]
        pieces = [[l0, l1], [r0, r1]]
    elif plan == "crossed":
        r1, r0, l1, l0 = refs[:4]
        pieces = [[l0, l1], [r0, r1]]
    else:
        pieces = [refs[:2 * rows:2][::-1], refs[1:2 * rows:2][::-1]]
    extra = refs[2 * rows:]
    width = right_ref.shape[2]
    full = rows * width
    reach = 2 ** (top - level - 1) if level < top else 1
    first = leaf % 2 == 0 if level == top else ((leaf + 1) // reach) % 4 == 1
    before = (level - 1) * full
    for which, wanted in enumerate((first, jnp.logical_not(first))):
        @pl.when(wanted)
        def _():
            if plan == "rooted":
                piece_ref[...] = pieces[which][0][...]
            elif plan == "traded" and which == 0:
                joined[:, :before] = extra[0][...]
            elif plan == "traded":
                place_pieces(extra[1:1 + rows], joined, 0)
                place_pieces(pieces[0], joined, full)
            elif plan == "plain" and before:
                joined[:, :before] = extra[which][...]
            place_pieces(pieces[which], joined, before)
    if plan == "rooted":
        @pl.when(upper_depth(leaf, top) == 0)
        def _():
            piece_ref[...] = extra[0][...]
    elif plan == "crossed":
        place_pieces([extra[0], late_ref], joined, 0)
    blocks, block_width = lower_ref.shape[1:3]
    highest = joined.shape[1] // block_width - 1

    def product():
        numbers = block_rows_ref[...]
        for index in range(blocks):
            number = jnp.clip(numbers[slot, index], 0, highest)
            column = pl.multiple_of(number * block_width, block_width)
            picked[:, index * block_width:(index + 1) * block_width] = joined[:, pl.ds(column, block_width)]
        weights = lower_ref[slot].reshape(blocks * block_width, width)
        offset = jnp.dot(picked[...], weights, preferred_element_type=F32)
        reduced_ref[...] = (right_ref[slot] - offset).astype(BF16)

    if level == top:
        product()
        return
    active = upper_depth(leaf, top) == level
    pl.when(active)(product)

    @pl.when(jnp.logical_not(active))
    def _():
        reduced_ref[...] = extra[1][...] if plan == "crossed" else jnp.zeros_like(reduced_ref)


def begin_kernel(top, depth, rows, cores, piece_ref, *refs):
    inverse_refs, part_ref = refs[:cores], refs[cores]
    width = piece_ref.shape[1]
    quarter = inverse_refs[0].shape[-1]
    slot = 0 if depth == top else 1
    own = lax.axis_index("rows")
    active = (upper_depth(lax.axis_index("leaf"), top) == depth) | (depth == top)
    for which in range(rows):
        @pl.when((own == which) & active)
        def _():
            for turn, inverse_ref in enumerate(inverse_refs):
                weights = inverse_ref[slot, which * width:(which + 1) * width, :]
                part_ref[:, turn * quarter:(turn + 1) * quarter] = jnp.dot(
                    piece_ref[...], weights, preferred_element_type=F32)


def apply_inverse(slot, cores, piece_refs, inverse_refs, part_ref, joined, store):
    rows = len(piece_refs)
    width = piece_refs[0].shape[1]
    quarter = inverse_refs[0].shape[-1]

    def share(turn):
        core = lax.rem(lax.axis_index("rhs") - turn + cores, cores)
        return pl.ds(pl.multiple_of(core * quarter, quarter), quarter)

    if part_ref is None:
        place_pieces(piece_refs, joined, 0)
        for turn, inverse_ref in enumerate(inverse_refs):
            store(turn, share(turn), jnp.dot(joined[...], inverse_ref[slot], preferred_element_type=F32))
        return
    for which in range(rows):
        @pl.when(lax.axis_index("rows") == which)
        def _():
            for turn, inverse_ref in enumerate(inverse_refs):
                total = part_ref[:, turn * quarter:(turn + 1) * quarter]
                for shift in range(1, rows):
                    source = (which - shift) % rows
                    weights = inverse_ref[slot, source * width:(source + 1) * width, :]
                    total = total + jnp.dot(piece_refs[shift][...], weights, preferred_element_type=F32)
                store(turn, share(turn), total)


def solve_kernel(top, depth, rows, cores, plan, split, *refs):
    piece_refs = refs[:rows]
    inverse_refs = refs[rows:rows + cores]
    before_ref, held_ref, part_ref = refs[rows + cores:rows + cores + 3]
    part_ref = part_ref if split else None
    rounded_ref, solved_ref, joined = refs[-3:]
    leaf = lax.axis_index("leaf")
    active = upper_depth(leaf, top) == depth

    def store(turn, columns, total):
        rounded_ref[:, columns] = total.astype(BF16)
        solved_ref[:, columns] = total

    @pl.when(active)
    def _():
        apply_inverse(1, cores, piece_refs, inverse_refs, part_ref, joined, store)

    @pl.when(jnp.logical_not(active))
    def _():
        rounded_ref[...] = jnp.zeros_like(rounded_ref)
        solved_ref[...] = before_ref[...] if depth > 0 else jnp.zeros_like(solved_ref)

    if plan == "crossed":
        for wanted, ref in ((leaf % 4 == 1, held_ref), (leaf % 4 == 3, piece_refs[1])):
            @pl.when(wanted)
            def _():
                rounded_ref[...] = ref[...]


def last_kernel(rows, cores, split, *refs):
    piece_refs = refs[:rows]
    inverse_refs = refs[rows:rows + cores]
    before_ref, *part, out_ref, joined, staged, semaphores = refs[rows + cores:]
    part_ref = part[0] if split else None
    quarter = inverse_refs[0].shape[-1]
    earlier = pltpu.make_async_copy(before_ref, out_ref.at[1], semaphores.at[0])
    earlier.start()

    def written(turn, columns):
        return pltpu.make_async_copy(staged.at[:, columns], out_ref.at[0, :, columns], semaphores.at[turn + 1])

    def store(turn, columns, total):
        staged[:, columns] = total
        written(turn, columns).start()

    apply_inverse(0, cores, piece_refs, inverse_refs, part_ref, joined, store)
    for turn in range(cores):
        written(turn, pl.ds(0, quarter)).wait()
    earlier.wait()


WHOLE = pl.BlockSpec(memory_space=pltpu.VMEM)
FAR = pl.BlockSpec(memory_space=pltpu.HBM)


def call(kernel, near, far, outs, scratch=(), flops=0):
    several = len(outs) > 1
    size = sum(a.size * a.dtype.itemsize for a in [*near, *far])
    near = [pltpu.with_memory_space_constraint(a, pltpu.VMEM) for a in near]
    far = [pltpu.with_memory_space_constraint(a, pltpu.HBM) for a in far]
    specs = [FAR if getattr(o, "memory_space", None) == pltpu.HBM else WHOLE for o in outs]
    return pl.pallas_call(
        kernel,
        in_specs=[WHOLE] * len(near) + [FAR] * len(far),
        out_specs=specs if several else specs[0],
        out_shape=list(outs) if several else outs[0],
        scratch_shapes=list(scratch),
        cost_estimate=pl.CostEstimate(flops=flops, bytes_accessed=size, transcendentals=0),
        compiler_params=pltpu.CompilerParams(vmem_limit_bytes=8 * 2**20),
    )(*near, *far)


def local(right_side, inverse_diag, lower_blocks, block_rows):
    leafs, rows, cores = (lax.axis_size(name) for name in ("leaf", "rows", "rhs"))
    top = leafs.bit_length() - 1
    count, width = right_side.shape[1:]
    full_width = rows * width
    places = ("leaf", "rows")

    def send(value, hops, shift):
        pairs = [(a * rows + r, b * rows + (r + shift) % rows) for a, b in hops for r in range(rows)]
        return lax.ppermute(value, places, pairs)

    def spread(value, hops):
        return [send(value, hops, shift) for shift in range(rows)]

    def permute(value, target):
        pairs = []
        for place in range(leafs * rows):
            goal = target(*divmod(place, rows))
            for core in range(cores):
                if goal is None:
                    pairs.append((place * cores + core, place * cores + (core + 1) % cores))
                else:
                    pairs.append((place * cores + core, (goal[0] * rows + goal[1]) * cores + core))
        return lax.ppermute(value, ("leaf", "rows", "rhs"), pairs)

    def rows_of(value, traders=None):
        traders = range(leafs) if traders is None else traders
        return [value] + [permute(value, lambda h, r: (h, (r + shift) % rows) if h in traders else None)
                          for shift in range(1, rows)]

    def ring(value, rings, shift=0, traders=()):
        after = {a: b for stops in rings for a, b in zip(stops, [*stops[1:], stops[0]])}

        def target(h, r):
            if h in after:
                return after[h], (r + shift) % rows
            return (h, (r + 1) % rows) if h in traders else None

        return permute(value, target)

    def core_columns(own):
        turns = range(1, cores)
        return [own] + [lax.ppermute(own, "rhs", [(c, (c + t) % cores) for c in range(cores)]) for t in turns]

    def holders(depth):
        return [(2 * p + 1) * 2 ** (top - depth - 1) - 1 for p in range(2**depth)]

    near = pltpu.VMEM
    half = near((count, width), BF16)
    half_f32 = near((count, width), F32)
    joined = near((count, full_width), BF16)
    work = 2 * count * full_width * width
    semaphores = lambda n: pltpu.SemaphoreType.DMA((n,))

    crossing = top == 3 and rows == 2
    swapped = core_columns(inverse_diag)[1:]

    def load(after, arrays):
        outs = [near(a.shape, a.dtype) for a in arrays]
        return call(functools.partial(load_kernel, len(arrays)), [after], arrays, outs, [semaphores(len(arrays))])

    def paired(lefts, rights):
        return [piece for pair in zip(lefts[::-1], rights[::-1]) for piece in pair]

    reduced = right_side[1].astype(BF16)
    gathered = rows_of(reduced, holders(0))
    inverse_own, right, lower = load(reduced, [inverse_diag, right_side, lower_blocks])
    inverses = [inverse_own, *swapped]
    plans = ["rooted", "crossed", "traded"] if crossing else ["plain"] * top
    plans = ["plain", *plans]
    older = []
    solved = None
    for depth, plan in enumerate(plans):
        here = holders(min(depth, top - 1))
        if depth > 0:
            all_joined = near((count, depth * full_width), BF16)
            kernel = functools.partial(offset_kernel, top, depth, rows, plan)
            pieces = paired(rights[::-1], lefts[::-1]) if depth == top else paired(lefts, rights)
            if plan == "rooted":
                pieces = [rights[1], rights[0], lefts[1], lefts[0], rounded]
            elif plan == "crossed":
                pieces = [late, rights[1], rights[0], lefts[1], lefts[0], relayed, rounded]
            elif plan == "traded":
                pieces = [rights[1], lefts[0], lefts[1], rights[0], mine, relayed, late]
            else:
                pieces = [*pieces, *older]
            arrays = [block_rows, right, lower, *pieces]
            if plan == "rooted":
                reduced, own_root = call(kernel, arrays, [], [half, half], [all_joined, joined], work)
            elif depth < top:
                reduced, mine = call(kernel, arrays, [], [half, all_joined], [joined], work)
            else:
                reduced = call(kernel, arrays, [], [half], [all_joined, joined], work)
            if plan == "crossed":
                gathered = [reduced, ring(reduced, [(h, h + 2) for h in holders(1)], 0, here)]
            else:
                gathered = rows_of(reduced, here if depth < top else None)
        split = crossing and depth > 1
        part = []
        if split:
            kernel = functools.partial(begin_kernel, top, depth, rows, cores)
            part = [call(kernel, [reduced, *inverses], [], [half_f32], (), work // rows)]
        if depth == top:
            staged = [near((count, width), F32), semaphores(cores + 1)]
            return call(functools.partial(last_kernel, rows, cores, split), [*gathered, *inverses, solved, *part], [],
                        [pltpu.HBM(right_side.shape, F32)], [joined, *staged], work)
        older = []
        if depth + 1 < top:
            reach = 2 ** (top - depth - 2)
            ways = [[(h, h - reach) for h in here], [(h, h + reach) for h in here]]
            if plan == "rooted":
                others = [(h, leafs - 1) for h in holders(0)]
                first_side, second_side = ring(own_root, ways[0] + others), ring(own_root, ways[1])
                relayed = call(choose_kernel, [first_side, second_side, own_root], [], [half])
            elif depth > 0:
                older = [send(mine, way, 0) for way in ways]
        else:
            over = [(h, h + 1) for h in here]
            older = [] if crossing else [mine, send(mine, over, 0)]
        kernel = functools.partial(solve_kernel, top, depth, rows, cores, plan, split)
        arrays = [*gathered, *inverses] + ([solved, rounded, *part] if depth else [])
        rounded, solved = call(kernel, arrays, [], [half, half_f32], [joined], work)
        if crossing and depth == 0:
            (root,) = here
            lefts = [ring(rounded, [(root, root - reach, root - 1)]), ring(rounded, ways[0], 1)]
            rights = [ring(rounded, [(root, root + reach, root + 1)]), ring(rounded, ways[1], 1)]
        elif depth + 1 < top:
            lefts, rights = [spread(rounded, way) for way in ways]
            if plan == "rooted":
                late = rows_of(relayed)[1]
        elif crossing:
            lefts, rights = rows_of(rounded), [ring(rounded, over, shift) for shift in range(rows)]
        else:
            lefts, rights = rows_of(rounded), spread(rounded, over)


def solution(mesh):
    return jax.shard_map(
        local,
        mesh=mesh,
        in_specs=(
            P("leaf", "rhs", "rows"),
            P("leaf", None, ("rows", "rhs")),
            P("leaf", None, None, "rows"),
            P("leaf", None),
        ),
        out_specs=P("leaf", "rhs", "rows"),
        check_vma=False,
    )
```
